32 devices in a mesh: dp: 8 (over y, x, core), tensor: 4 (over z).
Axes of the slice: x: 2, y: 2, z: 4, core: 2. Of those that a mesh axis runs over, the one named last changes fastest.
Arguments:
- block_input: bfloat16 [64, 2048, 1024], P('dp', None, 'tensor'), may hold values from -6 to 6
- routes: int32 [64, 256], P('dp'), may hold values from 0 to 2047, as said below
- out_grad: bfloat16 [64, 2048, 1024], P('dp', None, 'tensor'), may hold values from -6 to 6
- w_qkv: bfloat16 [1024, 3, 1024], P(None, None, 'tensor'), may hold values from -0.1875 to 0.1875
- w_out: bfloat16 [1024, 1024], P('tensor'), may hold values from -1 to 1
- w_up: bfloat16 [1024, 4096], P(None, 'tensor'), may hold values from -0.1875 to 0.1875
- w_down: bfloat16 [4096, 1024], P('tensor'), may hold values from -0.125 to 0.125
- gain_attn: float32 [1024], P('tensor'), may hold values from 0.1 to 1.9
- gain_mlp: float32 [1024], P('tensor'), may hold values from 0.1 to 1.9
- w_router: float32 [1024], P('tensor'), may hold values from -0.1875 to 0.1875
Outputs:
- layer_out: bfloat16 [64, 2048, 1024], P('dp', None, 'tensor')
- input_grad: bfloat16 [64, 2048, 1024], P('dp', None, 'tensor')
- grad_w_qkv: float32 [1024, 3, 1024], P(None, None, 'tensor')
- grad_w_out: float32 [1024, 1024], P('tensor')
- grad_w_up: float32 [1024, 4096], P(None, 'tensor')
- grad_w_down: float32 [4096, 1024], P('tensor')
- grad_gain_attn: float32 [1024], P('tensor')
- grad_gain_mlp: float32 [1024], P('tensor')
- grad_w_router: float32 [1024], P('tensor')
The draws below stay inside these ranges and needn't reach their ends.
Inputs may be any that keep to these rules, and one draw needn't show every extreme that they name: `routes`: each row holds 256 distinct positions of its sequence in increasing order; in some sequences they are the first 256 positions, in others they are spread over the sequence.
All inputs are finite; a program needn't handle non-finite values.
Results may differ from the reference program's by a relative error of at most 0.012.
Values may be sent and summed in bfloat16 or wider, within the bound.
A program may use at most 192 MiB of HBM per device.

```python
import jax
import jax.numpy as jnp
from jax import lax

D = 1024
HEAD_DIM = 64
FF = 4096
SEQ_LEN = 2048
CAP = 256
SEQS = 64


def draw_routes(key, part):
    key = jax.random.fold_in(key, 7)
    key_mode, key_pick, key_first, key_second = jax.random.split(key, 4)
    pick_keys = jax.random.split(key_pick, SEQS)

    def spread_one(one_key):
        shuffled = jax.random.permutation(one_key, SEQ_LEN - 1)
        chosen = jnp.sort(shuffled[:CAP - 1])
        return jnp.concatenate([chosen, jnp.full((1,), SEQ_LEN - 1, shuffled.dtype)])
    spread = jax.vmap(spread_one)(pick_keys).astype(jnp.int32)
    leading = jnp.broadcast_to(jnp.arange(CAP, dtype=jnp.int32), (SEQS, CAP))
    route_modes = jax.random.randint(key_mode, (SEQS,), 0, 2)
    first_seq = jax.random.randint(key_first, (), 0, SEQS)
    second = (first_seq + 1 + jax.random.randint(key_second, (), 0, SEQS - 1)) % SEQS
    route_modes = route_modes.at[first_seq].set(1).at[second].set(0)
    return jnp.where(route_modes[:, None] == 1, spread, leading).astype(jnp.int32)


def block_levels(stream_key, extent, pieces, smallest, largest):
    factor_of = 1.0
    for dim, blocks in pieces:
        steps = jax.random.uniform(jax.random.fold_in(jax.random.fold_in(stream_key, 6), dim), (blocks,), jnp.float32, smallest / len(pieces), largest / len(pieces))
        factor_of = factor_of * jnp.repeat(jnp.exp(steps), extent[dim] // blocks).reshape((-1,) + (1,) * (len(extent) - 1 - dim))
    return factor_of


def scatter_about(own_key, dims, deviation, bound, shards=(), kind=jnp.bfloat16):
    loudness = block_levels(own_key, dims, shards, -0.22, 0.18) if shards else 1.0
    array = jax.random.normal(own_key, dims, jnp.float32) * deviation * loudness
    return jnp.minimum(jnp.maximum(array, -bound), bound).astype(kind)


def setup_inputs(seed: int = 0) -> dict:
    key_list = jax.random.split(jax.random.key(seed), 11)
    return {
        "block_input": scatter_about(key_list[0], (SEQS, SEQ_LEN, D), 1.0, 6.0, ((0, 8), (2, 4))),
        "routes": draw_routes(jax.random.fold_in(key_list[10], 71), 0),
        "out_grad": scatter_about(key_list[2], (SEQS, SEQ_LEN, D), 1.0, 6.0, ((0, 8), (2, 4))),
        "w_qkv": scatter_about(key_list[3], (D, 3, D), D ** -0.5, 0.1875, ((2, 4),)),
        "w_out": scatter_about(key_list[4], (D, D), (D // 32) ** -0.5, 1.0, ((0, 4),)),
        "w_up": scatter_about(key_list[5], (D, FF), D ** -0.5, 0.1875, ((1, 4),)),
        "w_down": scatter_about(key_list[6], (FF, D), (FF // 2) ** -0.5, 0.125, ((0, 4),)),
        "gain_attn": jnp.clip(1.0 + 0.18 * jax.random.normal(key_list[7], (D,), jnp.float32), 0.1, 1.9),
        "gain_mlp": jnp.clip(1.0 + 0.18 * jax.random.normal(key_list[8], (D,), jnp.float32), 0.1, 1.9),
        "w_router": scatter_about(key_list[9], (D,), D ** -0.5, 0.1875, ((0, 4),), jnp.float32),
    }


EPS = 1e-06
HIGH = lax.Precision.HIGHEST

@jax.custom_vjp
def low(v):
    return lax.optimization_barrier(v.astype(jnp.bfloat16)).astype(jnp.float32)

@jax.custom_vjp
def low_back(v):
    return v

def low_keep(v):
    return (low(v), None)

def low_pass(kept, grad):
    return (grad,)

def back_keep(v):
    return (v, None)

def back_low(kept, grad):
    return (low(grad),)
low.defvjp(low_keep, low_pass)
low_back.defvjp(back_keep, back_low)

def forward(inputs, route_rows, w_qkv, w_out, w_up, w_down, gain_attn, gain_mlp, w_router):
    seq_count, routed_count = route_rows.shape
    model_width = inputs.shape[2]
    head_count = model_width // HEAD_DIM
    row_ids = jnp.arange(seq_count)[:, None]
    picked = inputs[row_ids, route_rows]
    inv_one = lax.rsqrt(lax.optimization_barrier(jnp.sum(picked * picked, axis=-1, keepdims=True)) / model_width + EPS)
    router = jax.nn.sigmoid(lax.optimization_barrier(jnp.sum(picked * w_router, axis=-1, keepdims=True)))
    normed_one = low(picked * inv_one * gain_attn)
    projected = low_back(low(jnp.einsum('scd,dkh->sckh', normed_one, w_qkv, precision=HIGH)))
    split_heads = projected.reshape(seq_count, routed_count, 3, head_count, HEAD_DIM)
    queries = split_heads[:, :, 0]
    key_rows = split_heads[:, :, 1]
    value_rows = split_heads[:, :, 2]
    score_scale = HEAD_DIM ** (-0.5)
    causal = jnp.arange(routed_count)[:, None] >= jnp.arange(routed_count)[None, :]
    scores = low_back(jnp.einsum('sqhe,skhe->shqk', queries, key_rows, precision=HIGH) * score_scale)
    scores = jnp.where(causal, scores, -1e+30)
    attn_probs = low(jax.nn.softmax(scores, axis=-1))
    head_out = low_back(low(jnp.einsum('shqk,skhe->sqhe', attn_probs, value_rows, precision=HIGH)))
    head_out = head_out.reshape(seq_count, routed_count, model_width)
    attn_out = low_back(jnp.einsum('sce,ed->scd', head_out, w_out, precision=HIGH))
    middle = picked + attn_out
    inv_two = lax.rsqrt(lax.optimization_barrier(jnp.sum(middle * middle, axis=-1, keepdims=True)) / model_width + EPS)
    normed_two = low(middle * inv_two * gain_mlp)
    pre_act = low_back(jnp.einsum('scd,df->scf', normed_two, w_up, precision=HIGH))
    hidden = low(jax.nn.gelu(pre_act, approximate=False))
    mlp_out = low_back(jnp.einsum('scf,fd->scd', hidden, w_down, precision=HIGH))
    update = attn_out + mlp_out
    return inputs.at[row_ids, route_rows].add(router * update)

def reference(block_input, routes, out_grad, w_qkv, w_out, w_up, w_down, gain_attn, gain_mlp, w_router):
    params = tuple((weight.astype(jnp.float32) for weight in (w_qkv, w_out, w_up, w_down, gain_attn, gain_mlp, w_router)))
    groups = routes.shape[0] // 2
    input_groups = block_input.reshape(groups, 2, block_input.shape[1], block_input.shape[2])
    grad_groups = out_grad.reshape(groups, 2, out_grad.shape[1], out_grad.shape[2])
    route_groups = routes.reshape(groups, 2, routes.shape[1])

    def scan_step(totals, scan_item):
        input_group, route_group, grad_group = scan_item

        def local_forward(inputs, *weights):
            return forward(inputs, route_group, *weights)
        result, backward = jax.vjp(local_forward, input_group.astype(jnp.float32), *params)
        gradients = backward(grad_group.astype(jnp.float32))
        totals = tuple((total_one + grad_one for total_one, grad_one in zip(totals, gradients[1:])))
        return (totals, (result.astype(jnp.bfloat16), gradients[0].astype(jnp.bfloat16)))
    zero_totals = tuple((jnp.zeros_like(weight) for weight in params))
    totals, (outputs, input_grads) = lax.scan(scan_step, zero_totals, (input_groups, route_groups, grad_groups))
    return (outputs.reshape(block_input.shape), input_grads.reshape(block_input.shape), totals[0], totals[1], totals[2], totals[3], totals[4], totals[5], totals[6])
```

```python
import functools

import jax
import jax.numpy as jnp
from jax import lax
from jax.experimental import pallas as pl
from jax.experimental.pallas import tpu as pltpu
from jax.sharding import PartitionSpec as P

HEAD_DIM = 64
EPS = 1e-06
F32 = jnp.float32
BF16 = jnp.bfloat16


def exact_gelu(values):
    return jax.nn.gelu(values, approximate=False)


def gather_kernel(routes_ref, block_ref, out_ref):
    length = block_ref.shape[1]
    places = lax.broadcasted_iota(jnp.int32, (routes_ref.shape[1], length), 1)
    chosen = (routes_ref[0] == places).astype(BF16)
    out_ref[0] = jnp.dot(chosen, block_ref[0], preferred_element_type=F32).astype(BF16)


def gather_rows(routes, block):
    seqs, length, cols = block.shape
    cap = routes.shape[1]
    return pl.pallas_call(
        gather_kernel,
        grid=(seqs,),
        in_specs=[
            pl.BlockSpec((1, cap, 1), lambda s: (s, 0, 0)),
            pl.BlockSpec((1, length, cols), lambda s: (s, 0, 0)),
        ],
        out_specs=pl.BlockSpec((1, cap, cols), lambda s: (s, 0, 0)),
        out_shape=jax.ShapeDtypeStruct((seqs, cap, cols), BF16),
        cost_estimate=pl.CostEstimate(
            flops=2 * seqs * cap * length * cols, bytes_accessed=block.size * 2, transcendentals=0
        ),
        name="gather_rows",
    )(routes[:, :, None], block)


def scatter_kernel(routes_ref, block_ref, rows_ref, out_ref):
    length = block_ref.shape[1]
    cap = routes_ref.shape[2]
    places = lax.broadcasted_iota(jnp.int32, (length, cap), 0)
    chosen = routes_ref[0] == places
    hit = jnp.max(chosen.astype(F32), axis=1, keepdims=True) > 0.0
    spread = jnp.dot(chosen.astype(BF16), rows_ref[0], preferred_element_type=F32)
    out_ref[0] = jnp.where(hit, spread, block_ref[0].astype(F32)).astype(BF16)


def scatter_rows(routes, block, rows):
    seqs, length, cols = block.shape
    cap = rows.shape[1]
    return pl.pallas_call(
        scatter_kernel,
        grid=(seqs,),
        in_specs=[
            pl.BlockSpec((1, 1, cap), lambda s: (s, 0, 0)),
            pl.BlockSpec((1, length, cols), lambda s: (s, 0, 0)),
            pl.BlockSpec((1, cap, cols), lambda s: (s, 0, 0)),
        ],
        out_specs=pl.BlockSpec((1, length, cols), lambda s: (s, 0, 0)),
        out_shape=jax.ShapeDtypeStruct(block.shape, BF16),
        cost_estimate=pl.CostEstimate(
            flops=2 * seqs * cap * length * cols, bytes_accessed=block.size * 4, transcendentals=0
        ),
        name="scatter_rows",
    )(routes[:, None, :], block, rows)


MESH = pl.DeviceIdType.MESH
GROUP = 8


def flip(value, bit):
    return value + bit - 2 * bit * lax.rem(lax.div(value, jnp.int32(bit)), jnp.int32(2))


class Place:
    def __init__(self):
        self.dp = lax.axis_index("dp").astype(jnp.int32)
        self.t = lax.axis_index("tensor").astype(jnp.int32)
        self.j = lax.rem(self.dp, jnp.int32(GROUP))
        self.c = lax.rem(self.j, jnp.int32(2))
        self.x = lax.rem(lax.div(self.j, jnp.int32(2)), jnp.int32(2))
        self.y = lax.div(self.j, jnp.int32(4))

    def slot(self, mask):
        value = self.j
        for bit in (1, 2, 4):
            if mask & bit:
                value = flip(value, bit)
        return value

    def shard(self, r):
        value = self.t
        for bit in (1, 2):
            if r & bit:
                value = flip(value, bit)
        return value

    def device(self, mask=0, r=0):
        value = self.dp
        for bit in (1, 2, 4):
            if mask & bit:
                value = flip(value, bit)
        return (value, self.shard(r))

    def greet(self):
        barrier = pltpu.get_barrier_semaphore()
        partners = [(mask, 0) for mask in (1, 2, 4)] + [(0, r) for r in (1, 2, 3)]
        for mask, r in partners:
            pl.semaphore_signal(barrier, inc=1, device_id=self.device(mask, r), device_id_type=MESH)
        pl.semaphore_wait(barrier, len(partners))


def remote(src, dst, send_sem, recv_sem, device):
    return pltpu.make_async_remote_copy(
        src_ref=src, dst_ref=dst, send_sem=send_sem, recv_sem=recv_sem, device_id=device, device_id_type=MESH
    )


CORE, X, Y = 1, 2, 4


def spread_slices(place, full, r, sends, recvs, own=None):
    def block(mask, part=None):
        ref = full.at[place.shard(r)] if r is not None else full
        ref = ref.at[:, place.slot(mask)]
        if part is None:
            return ref
        half = ref.shape[1] // 2
        return ref.at[:, pl.ds(part * half, half)]

    def copy(k, mask, to, part=None, src=None):
        return remote(src if src is not None else block(mask, part), block(mask, part), sends.at[k], recvs.at[k], place.device(to))

    def landed(k, mask, part=None):
        remote(block(mask, part), block(mask, part), sends.at[k], recvs.at[k], place.device(CORE)).wait_recv()

    plan = [
        (0, 0, X, None),
        (1, 0, Y, None),
        (2, 0, CORE, None),
        (3, X, Y, 0),
        (4, Y, X, 1),
        (5, X, CORE, None),
        (6, Y, CORE, None),
        (7, X | Y, CORE, None),
    ]

    def begin():
        for k in (0, 1, 2):
            _, mask, to, part = plan[k]
            copy(k, mask, to, part, own).start()

    def forward():
        landed(0, X)
        copy(*plan[3]).start()
        copy(*plan[5]).start()
        landed(1, Y)
        copy(*plan[4]).start()
        copy(*plan[6]).start()

    def corner():
        landed(3, X | Y, 0)
        landed(4, X | Y, 1)
        copy(*plan[7]).start()

    def finish():
        for k, mask in ((2, CORE), (5, CORE | X), (6, CORE | Y), (7, CORE | X | Y)):
            landed(k, mask)
        for k, mask, to, part in plan:
            copy(k, mask, to, part, own if k < 3 else None).wait_send()

    return [begin, forward, corner, finish]


def pipelined(chains):
    depth = max(len(chain) for chain in chains)
    for tick in range(len(chains) + depth - 1):
        for i in range(max(0, tick - depth + 1), min(tick, len(chains) - 1) + 1):
            stage = tick - i
            if stage < len(chains[i]):
                chains[i][stage]()


def exchange_rows(place, src, dst, sends, recvs):
    def copy(r):
        return remote(src.at[place.shard(r)], dst.at[place.t], sends.at[r - 1], recvs.at[r - 1], place.device(0, r))

    def landed(r):
        return remote(src.at[place.t], dst.at[place.shard(r)], sends.at[r - 1], recvs.at[r - 1], place.device(0, r))

    def begin():
        for r in (2, 3, 1):
            copy(r).start()

    def finish():
        for r in (1, 2, 3):
            landed(r).wait_recv()
        for r in (1, 2, 3):
            copy(r).wait_send()

    return begin, finish


def gather_all_kernel(*refs):
    picked, grads = refs[0:2]
    locals_ = refs[2:6]
    got_picked, got_grads = refs[6:8]
    fulls = refs[8:12]
    z_send, z_recv, p_send, p_recv, row_send, row_recv, own_sem = refs[12:]
    place = Place()
    own = [
        pltpu.make_async_copy(picked.at[place.t], got_picked.at[place.t], own_sem.at[0]),
        pltpu.make_async_copy(grads.at[place.t], got_grads.at[place.t], own_sem.at[1]),
    ]
    for w in range(4):
        own.append(pltpu.make_async_copy(locals_[w], fulls[w].at[place.t], own_sem.at[2 + w]))
    for copy in own:
        copy.start()
    place.greet()

    def z_copy(w, r):
        if r == 3:
            block = fulls[w].at[place.shard(2), :, place.j]
            return remote(block, block, z_send.at[w, 2], z_recv.at[w, 2], place.device(0, 1))
        return remote(
            locals_[w].at[:, place.j],
            fulls[w].at[place.t, :, place.j],
            z_send.at[w, r - 1],
            z_recv.at[w, r - 1],
            place.device(0, r),
        )

    def z_landed(w, r):
        block = fulls[w].at[place.shard(r), :, place.j]
        remote(block, block, z_send.at[w, r - 1], z_recv.at[w, r - 1], place.device(0, 1)).wait_recv()

    def z_begin(w):
        z_copy(w, 2).start()
        z_copy(w, 1).start()

    rows_one = exchange_rows(place, picked, got_picked, row_send.at[0], row_recv.at[0])
    rows_two = exchange_rows(place, grads, got_grads, row_send.at[1], row_recv.at[1])
    chains = []
    for w in range(4):
        for r in (2, 1, 3):
            stages = spread_slices(place, fulls[w], r, p_send.at[w, r - 1], p_recv.at[w, r - 1])

            def first(w=w, r=r, begin=stages[0]):
                z_landed(w, r)
                if r == 2:
                    z_copy(w, 3).start()
                    if w == 0:
                        rows_one[0]()
                    if w + 1 < 4:
                        z_begin(w + 1)
                    if w == 2:
                        rows_two[0]()
                begin()

            chains.append([first] + stages[1:])
    z_begin(0)
    pipelined(chains)
    for w in range(4):
        for r in (1, 2, 3):
            z_copy(w, r).wait_send()
    rows_one[1]()
    rows_two[1]()
    for copy in own:
        copy.wait()


ANY = pl.BlockSpec(memory_space=pl.ANY)


def gather_all(picked, grads, local):
    shapes = [jax.ShapeDtypeStruct(picked.shape, BF16)] * 2 + [
        jax.ShapeDtypeStruct((4,) + w.shape, BF16) for w in local
    ]
    dma = pltpu.SemaphoreType.DMA
    return pl.pallas_call(
        gather_all_kernel,
        in_specs=[ANY] * 6,
        out_specs=[ANY] * 6,
        out_shape=shapes,
        scratch_shapes=[
            dma((4, 3)),
            dma((4, 3)),
            dma((4, 3, 8)),
            dma((4, 3, 8)),
            dma((2, 3)),
            dma((2, 3)),
            dma((6,)),
        ],
        compiler_params=pltpu.CompilerParams(collective_id=1, has_side_effects=True),
        name="gather_all",
    )(picked, grads, *local)


def add_blocks(target, extra, leads):
    for index_t, index_e in leads:
        target[index_t] = (target[index_t].astype(F32) + extra[index_e].astype(F32)).astype(BF16)


def sum_chain(place, grad, sum1, got1, got2, got3, got4, got5, stage, sends, recvs, sem):
    count, rows = grad.shape[1], grad.shape[5]
    half = rows // 2
    low, high = pl.ds(0, half), pl.ds(half, half)
    c, x, y, t = place.c, place.x, place.y, place.t
    own = pltpu.make_async_copy(grad.at[:, :, :, :, c], sum1, sem)
    every = [(tt, k) for tt in range(4) for k in range(count)]

    def copy(n):
        src, dst, device = (
            lambda: (grad.at[:, :, :, :, 1 - c], got1, place.device(CORE)),
            lambda: (sum1.at[:, :, :, 1 - x, low], got2.at[0], place.device(X)),
            lambda: (sum1.at[:, :, 1 - y, :, high], got2.at[1], place.device(Y)),
            lambda: (sum1.at[:, :, 1 - y, x, low], got3.at[0], place.device(Y)),
            lambda: (sum1.at[:, :, y, 1 - x, high], got3.at[1], place.device(X)),
            lambda: (sum1.at[place.shard(1), :, y, x], got4.at[0], place.device(0, 1)),
            lambda: (sum1.at[place.shard(3), :, y, x], got4.at[1], place.device(0, 1)),
            lambda: (sum1.at[place.shard(2), :, y, x], got5, place.device(0, 2)),
        )[n]()
        return remote(src, dst, sends.at[n], recvs.at[n], device)

    def s0():
        own.start()
        copy(0).start()

    def s1():
        own.wait()
        copy(0).wait_recv()
        for tt, k in every:
            for b in range(2):
                for a in range(2):
                    i = (tt, k, b, a)
                    sum1[i] = (sum1[i].astype(F32) + got1[i].astype(F32)).astype(BF16)
        copy(1).start()
        copy(2).start()

    def s2():
        copy(1).wait_recv()
        copy(1).wait_send()
        for tt, k in every:
            for b in range(2):
                i = (tt, k, b, x, low)
                sum1[i] = (sum1[i].astype(F32) + got2[0, tt, k, b].astype(F32)).astype(BF16)
        copy(3).start()
        copy(2).wait_recv()
        copy(2).wait_send()
        for tt, k in every:
            for a in range(2):
                i = (tt, k, y, a, high)
                sum1[i] = (sum1[i].astype(F32) + got2[1, tt, k, a].astype(F32)).astype(BF16)
        copy(4).start()

    def s3():
        for side, n in ((0, 3), (1, 4)):
            copy(n).wait_recv()
            copy(n).wait_send()
            part = (low, high)[side]
            for tt, k in every:
                i = (tt, k, y, x, part)
                sum1[i] = (sum1[i].astype(F32) + got3[side, tt, k].astype(F32)).astype(BF16)
        copy(5).start()
        copy(6).start()

    def s4():
        for side, shard in ((0, t), (1, place.shard(2))):
            copy(5 + side).wait_recv()
            copy(5 + side).wait_send()
            for k in range(count):
                i = (shard, k, y, x)
                sum1[i] = (sum1[i].astype(F32) + got4[side, k].astype(F32)).astype(BF16)
        copy(7).start()

    def s5():
        copy(7).wait_recv()
        copy(7).wait_send()
        copy(0).wait_send()
        for k in range(count):
            i = (t, k, y, x)
            stage[k, place.j] = (sum1[i].astype(F32) + got5[k].astype(F32)).astype(BF16)

    stages = spread_slices(place, stage, None, sends.at[pl.ds(8, 8)], recvs.at[pl.ds(8, 8)])

    def last():
        s5()
        stages[0]()

    return [s0, s1, s2, s3, s4, last] + stages[1:]


def sum_all_kernel(count, *refs):
    out_rows, in_rows = refs[0:2]
    grads = refs[2 : 2 + count]
    got_out, got_in = refs[2 + count : 4 + count]
    results = refs[4 + count : 4 + 2 * count]
    rest = refs[4 + 2 * count :]
    buffers = [rest[7 * i : 7 * i + 7] for i in range(count)]
    sends, recvs, own_sem, row_send, row_recv, res_sem = rest[7 * count :]
    place = Place()
    own = [
        pltpu.make_async_copy(out_rows.at[place.t], got_out.at[place.t], res_sem.at[0]),
        pltpu.make_async_copy(in_rows.at[place.t], got_in.at[place.t], res_sem.at[1]),
    ]
    for copy in own:
        copy.start()
    place.greet()
    rows_one = exchange_rows(place, out_rows, got_out, row_send.at[0], row_recv.at[0])
    rows_two = exchange_rows(place, in_rows, got_in, row_send.at[1], row_recv.at[1])
    chains = [
        sum_chain(place, grads[i], *buffers[i], sends.at[i], recvs.at[i], own_sem.at[i]) for i in range(count)
    ]
    write = []
    for i in range(count):
        copy = pltpu.make_async_copy(buffers[i][6], results[i], res_sem.at[2 + i])
        chains[i].append(copy.start)
        write.append(copy)
    rows_one[0]()
    rows_two[0]()
    pipelined(chains)
    rows_one[1]()
    rows_two[1]()
    for copy in own + write:
        copy.wait()


def sum_all(out_rows, in_rows, grads):
    count = len(grads)
    dma = pltpu.SemaphoreType.DMA
    scratch = []
    for g in grads:
        _, k, _, _, _, rows, cols = g.shape
        scratch += [
            pltpu.VMEM((4, k, 2, 2, rows, cols), BF16),
            pltpu.VMEM((4, k, 2, 2, rows, cols), BF16),
            pltpu.VMEM((2, 4, k, 2, rows // 2, cols), BF16),
            pltpu.VMEM((2, 4, k, rows // 2, cols), BF16),
            pltpu.VMEM((2, k, rows, cols), BF16),
            pltpu.VMEM((k, rows, cols), BF16),
            pltpu.VMEM((k, 8, rows, cols), BF16),
        ]
    return pl.pallas_call(
        functools.partial(sum_all_kernel, count),
        in_specs=[ANY] * (2 + count),
        out_specs=[ANY] * (2 + count),
        out_shape=[jax.ShapeDtypeStruct(out_rows.shape, BF16)] * 2
        + [jax.ShapeDtypeStruct((g.shape[1], 8) + g.shape[5:], BF16) for g in grads],
        scratch_shapes=scratch
        + [dma((count, 16)), dma((count, 16)), dma((count,)), dma((2, 3)), dma((2, 3)), dma((2 + count,))],
        compiler_params=pltpu.CompilerParams(
            collective_id=2, has_side_effects=True, vmem_limit_bytes=60 * 1024 * 1024
        ),
        name="sum_all",
    )(out_rows, in_rows, *grads)


def body(all_dp, n_t, block_input, routes, out_grad, w_qkv, w_out, w_up, w_down, gain_attn, gain_mlp, w_router):
    seqs, length, cols = block_input.shape
    cap = routes.shape[1]
    width = cols * n_t
    own = seqs // n_t
    rows = own * cap
    heads = cols // HEAD_DIM
    outer_bits = [1 << i for i in range(3, all_dp.bit_length() - 1)]

    def send(value, mask_dp, mask_t):
        pairs = [
            (d * n_t + s, (d ^ mask_dp) * n_t + (s ^ mask_t)) for d in range(all_dp) for s in range(n_t)
        ]
        return lax.ppermute(value, ("dp", "tensor"), pairs)

    vectors = lax.all_gather(jnp.stack([gain_attn, gain_mlp, w_router]), "tensor", axis=1, tiled=True)
    gain_one, gain_two, route_w = vectors[0], vectors[1], vectors[2]

    local = [
        w_qkv.transpose(1, 0, 2).reshape(3, GROUP, width // GROUP, cols),
        w_out.reshape(1, GROUP, cols // GROUP, width),
        w_up.reshape(1, GROUP, width // GROUP, w_up.shape[1]),
        w_down.reshape(1, GROUP, w_down.shape[0] // GROUP, width),
    ]
    picked_all = gather_rows(routes, block_input).reshape(n_t, rows, cols)
    grad_all = gather_rows(routes, out_grad).reshape(n_t, rows, cols)
    picked, grad_rows, wq, wo, wu, wd = gather_all(picked_all, grad_all, local)
    wq = wq.reshape(n_t, 3, width, cols)
    wo = wo.reshape(n_t, cols, width)
    wu = wu.reshape(n_t, width, -1)
    wd = wd.reshape(n_t, -1, width)
    picked = picked.transpose(1, 0, 2).reshape(rows, width).astype(F32)
    grad_rows = grad_rows.transpose(1, 0, 2).reshape(rows, width).astype(F32)

    inv_one = lax.rsqrt(jnp.sum(picked * picked, axis=-1, keepdims=True) / width + EPS)
    router = jax.nn.sigmoid(jnp.sum(picked * route_w, axis=-1, keepdims=True))
    normed_one = (picked * inv_one * gain_one).astype(BF16)
    projected = jnp.einsum("sd,rkde->rkse", normed_one, wq, preferred_element_type=F32).astype(BF16)
    split = projected.reshape(n_t, 3, own, cap, heads, HEAD_DIM)
    queries, keys, values = split[:, 0], split[:, 1], split[:, 2]
    scale = HEAD_DIM ** (-0.5)
    causal = jnp.arange(cap)[:, None] >= jnp.arange(cap)[None, :]
    scores = jnp.einsum("rsqhe,rskhe->rshqk", queries, keys, preferred_element_type=F32) * scale
    scores = jnp.where(causal, scores, -1e30)
    top = jnp.max(scores, axis=-1, keepdims=True)
    exps = jnp.exp(scores - top)
    total = jnp.sum(exps, axis=-1, keepdims=True)
    probs_full = exps / total
    probs = probs_full.astype(BF16)
    head_out = jnp.einsum("rshqk,rskhe->rsqhe", probs, values, preferred_element_type=F32).astype(BF16)
    head_out = head_out.reshape(n_t, rows, cols)
    attn_out = jnp.einsum("rse,red->sd", head_out, wo, preferred_element_type=F32)
    middle = picked + attn_out
    inv_two = lax.rsqrt(jnp.sum(middle * middle, axis=-1, keepdims=True) / width + EPS)
    normed_two = (middle * inv_two * gain_two).astype(BF16)
    pre_act = jnp.einsum("sd,rdf->rsf", normed_two, wu, preferred_element_type=F32)
    hidden, gelu_back = jax.vjp(exact_gelu, pre_act)
    hidden = hidden.astype(BF16)
    mlp_out = jnp.einsum("rsf,rfd->sd", hidden, wd, preferred_element_type=F32)
    update = attn_out + mlp_out
    out_rows = (picked + router * update).astype(BF16).reshape(rows, n_t, cols).transpose(1, 0, 2)

    d_update = router * grad_rows
    d_router = jnp.sum(grad_rows * update, axis=-1, keepdims=True)
    d_mlp = d_update.astype(BF16)
    grad_down = jnp.einsum("rsf,sd->rfd", hidden, d_mlp, preferred_element_type=F32).astype(BF16)
    d_hidden = jnp.einsum("sd,rfd->rsf", d_mlp, wd, preferred_element_type=F32)
    d_pre = gelu_back(d_hidden)[0].astype(BF16)
    grad_up = jnp.einsum("sd,rsf->rdf", normed_two, d_pre, preferred_element_type=F32).astype(BF16)
    d_normed_two = jnp.einsum("rsf,rdf->sd", d_pre, wu, preferred_element_type=F32)
    grad_gain_mlp = jnp.sum(d_normed_two * middle * inv_two, axis=0)
    e_two = d_normed_two * gain_two
    proj_two = jnp.sum(e_two * middle, axis=-1, keepdims=True)
    d_middle = inv_two * e_two - middle * inv_two**3 * proj_two / width
    d_attn = (d_update + d_middle).astype(BF16)
    grad_out = jnp.einsum("rse,sd->red", head_out, d_attn, preferred_element_type=F32).astype(BF16)
    d_head = jnp.einsum("sd,red->rse", d_attn, wo, preferred_element_type=F32).astype(BF16)
    d_head = d_head.reshape(n_t, own, cap, heads, HEAD_DIM)
    d_values = jnp.einsum("rshqk,rsqhe->rskhe", probs, d_head, preferred_element_type=F32)
    d_probs = jnp.einsum("rsqhe,rskhe->rshqk", d_head, values, preferred_element_type=F32)
    row_dot = jnp.sum(probs_full * d_probs, axis=-1, keepdims=True)
    d_scores = (probs_full * (d_probs - row_dot)).astype(BF16)
    d_queries = jnp.einsum("rshqk,rskhe->rsqhe", d_scores, keys, preferred_element_type=F32) * scale
    d_keys = jnp.einsum("rshqk,rsqhe->rskhe", d_scores, queries, preferred_element_type=F32) * scale
    d_proj = jnp.stack([d_queries, d_keys, d_values], axis=1).astype(BF16)
    d_proj = d_proj.reshape(n_t, 3, rows, cols)
    grad_qkv = jnp.einsum("sd,rkse->rkde", normed_one, d_proj, preferred_element_type=F32).astype(BF16)
    d_normed_one = jnp.einsum("rkse,rkde->sd", d_proj, wq, preferred_element_type=F32)
    grad_gain_attn = jnp.sum(d_normed_one * picked * inv_one, axis=0)
    e_one = d_normed_one * gain_one
    d_logit = d_router * router * (1.0 - router)
    grad_router = jnp.sum(d_logit * picked, axis=0)
    proj_one = jnp.sum(e_one * picked, axis=-1, keepdims=True)
    d_picked = (
        grad_rows
        + d_middle
        + inv_one * e_one
        - picked * inv_one**3 * proj_one / width
        + d_logit * route_w
    )
    in_rows = d_picked.astype(BF16).reshape(rows, n_t, cols).transpose(1, 0, 2)

    def cut(value):
        a, b, c, d = value.shape
        return value.reshape(a, b, 2, 2, 2, c // GROUP, d)

    got_out, got_in, s_down, s_up, s_out, s_qkv = sum_all(
        out_rows,
        in_rows,
        [cut(grad_down[:, None]), cut(grad_up[:, None]), cut(grad_out[:, None]), cut(grad_qkv)],
    )
    layer_out = scatter_rows(routes, block_input, got_out.reshape(seqs, cap, cols))
    input_grad = scatter_rows(routes, out_grad, got_in.reshape(seqs, cap, cols))
    sums = jnp.stack([grad_gain_attn, grad_gain_mlp, grad_router])
    sums = lax.psum_scatter(sums, "tensor", scatter_dimension=1, tiled=True)
    sums = lax.psum(sums, "dp")

    def settle(value, shape):
        value = value.reshape(shape).astype(F32)
        for bit in outer_bits:
            value = value + send(value, bit, 0)
        return value

    g_qkv = settle(s_qkv, (3, width, cols)).transpose(1, 0, 2)
    g_out = settle(s_out, w_out.shape)
    g_up = settle(s_up, w_up.shape)
    g_down = settle(s_down, w_down.shape)
    return (layer_out, input_grad, g_qkv, g_out, g_up, g_down, sums[0], sums[1], sums[2])


def solution(mesh):
    placed = (
        P("dp", None, "tensor"),
        P("dp", None),
        P("dp", None, "tensor"),
        P(None, None, "tensor"),
        P("tensor", None),
        P(None, "tensor"),
        P("tensor", None),
        P("tensor"),
        P("tensor"),
        P("tensor"),
    )
    return jax.shard_map(
        functools.partial(body, mesh.shape["dp"], mesh.shape["tensor"]),
        mesh=mesh,
        in_specs=placed,
        out_specs=(
            P("dp", None, "tensor"),
            P("dp", None, "tensor"),
            P(None, None, "tensor"),
            P("tensor", None),
            P(None, "tensor"),
            P("tensor", None),
            P("tensor"),
            P("tensor"),
            P("tensor"),
        ),
        check_vma=False,
    )
```

```python
import functools

import jax
import jax.numpy as jnp
from jax import lax
from jax.experimental import pallas as pl
from jax.experimental.pallas import tpu as pltpu
from jax.sharding import PartitionSpec as P

HEAD_DIM = 64
EPS = 1e-06
F32 = jnp.float32
BF16 = jnp.bfloat16


def exact_gelu(values):
    return jax.nn.gelu(values, approximate=False)


def gather_kernel(routes_ref, block_ref, out_ref):
    length = block_ref.shape[1]
    places = lax.broadcasted_iota(jnp.int32, (routes_ref.shape[1], length), 1)
    chosen = (routes_ref[0] == places).astype(BF16)
    out_ref[0] = jnp.dot(chosen, block_ref[0], preferred_element_type=F32).astype(BF16)


def gather_rows(routes, block):
    seqs, length, cols = block.shape
    cap = routes.shape[1]
    return pl.pallas_call(
        gather_kernel,
        grid=(seqs,),
        in_specs=[
            pl.BlockSpec((1, cap, 1), lambda s: (s, 0, 0)),
            pl.BlockSpec((1, length, cols), lambda s: (s, 0, 0)),
        ],
        out_specs=pl.BlockSpec((1, cap, cols), lambda s: (s, 0, 0)),
        out_shape=jax.ShapeDtypeStruct((seqs, cap, cols), BF16),
        cost_estimate=pl.CostEstimate(
            flops=2 * seqs * cap * length * cols, bytes_accessed=block.size * 2, transcendentals=0
        ),
        name="gather_rows",
    )(routes[:, :, None], block)


def scatter_kernel(routes_ref, block_ref, rows_ref, out_ref):
    length = block_ref.shape[1]
    cap = routes_ref.shape[2]
    places = lax.broadcasted_iota(jnp.int32, (length, cap), 0)
    chosen = routes_ref[0] == places
    hit = jnp.max(chosen.astype(F32), axis=1, keepdims=True) > 0.0
    spread = jnp.dot(chosen.astype(BF16), rows_ref[0], preferred_element_type=F32)
    out_ref[0] = jnp.where(hit, spread, block_ref[0].astype(F32)).astype(BF16)


def scatter_rows(routes, block, rows):
    seqs, length, cols = block.shape
    cap = rows.shape[1]
    return pl.pallas_call(
        scatter_kernel,
        grid=(seqs,),
        in_specs=[
            pl.BlockSpec((1, 1, cap), lambda s: (s, 0, 0)),
            pl.BlockSpec((1, length, cols), lambda s: (s, 0, 0)),
            pl.BlockSpec((1, cap, cols), lambda s: (s, 0, 0)),
        ],
        out_specs=pl.BlockSpec((1, length, cols), lambda s: (s, 0, 0)),
        out_shape=jax.ShapeDtypeStruct(block.shape, BF16),
        cost_estimate=pl.CostEstimate(
            flops=2 * seqs * cap * length * cols, bytes_accessed=block.size * 4, transcendentals=0
        ),
        name="scatter_rows",
    )(routes[:, None, :], block, rows)


MESH = pl.DeviceIdType.MESH
GROUP = 8


def flip(value, bit):
    return value + bit - 2 * bit * lax.rem(lax.div(value, jnp.int32(bit)), jnp.int32(2))


class Place:
    def __init__(self):
        self.dp = lax.axis_index("dp").astype(jnp.int32)
        self.t = lax.axis_index("tensor").astype(jnp.int32)
        self.j = lax.rem(self.dp, jnp.int32(GROUP))
        self.c = lax.rem(self.j, jnp.int32(2))
        self.x = lax.rem(lax.div(self.j, jnp.int32(2)), jnp.int32(2))
        self.y = lax.div(self.j, jnp.int32(4))

    def slot(self, mask):
        value = self.j
        for bit in (1, 2, 4):
            if mask & bit:
                value = flip(value, bit)
        return value

    def shard(self, r):
        value = self.t
        for bit in (1, 2):
            if r & bit:
                value = flip(value, bit)
        return value

    def device(self, mask=0, r=0):
        value = self.dp
        for bit in (1, 2, 4):
            if mask & bit:
                value = flip(value, bit)
        return (value, self.shard(r))

    def greet(self):
        barrier = pltpu.get_barrier_semaphore()
        partners = [(mask, 0) for mask in (1, 2, 4)] + [(0, r) for r in (1, 2, 3)]
        for mask, r in partners:
            pl.semaphore_signal(barrier, inc=1, device_id=self.device(mask, r), device_id_type=MESH)
        pl.semaphore_wait(barrier, len(partners))


def remote(src, dst, send_sem, recv_sem, device):
    return pltpu.make_async_remote_copy(
        src_ref=src, dst_ref=dst, send_sem=send_sem, recv_sem=recv_sem, device_id=device, device_id_type=MESH
    )


CORE, X, Y = 1, 2, 4


def spread_slices(place, full, r, sends, recvs, own=None):
    def block(mask, part=None):
        ref = full.at[place.shard(r)] if r is not None else full
        ref = ref.at[:, place.slot(mask)]
        if part is None:
            return ref
        half = ref.shape[1] // 2
        return ref.at[:, pl.ds(part * half, half)]

    def copy(k, mask, to, part=None, src=None):
        return remote(src if src is not None else block(mask, part), block(mask, part), sends.at[k], recvs.at[k], place.device(to))

    def landed(k, mask, part=None):
        remote(block(mask, part), block(mask, part), sends.at[k], recvs.at[k], place.device(CORE)).wait_recv()

    plan = [
        (0, 0, X, None),
        (1, 0, Y, None),
        (2, 0, CORE, None),
        (3, X, Y, 0),
        (4, Y, X, 1),
        (5, X, CORE, None),
        (6, Y, CORE, None),
        (7, X | Y, CORE, None),
    ]

    def begin():
        for k in (0, 1, 2):
            _, mask, to, part = plan[k]
            copy(k, mask, to, part, own).start()

    def forward():
        landed(0, X)
        copy(*plan[3]).start()
        copy(*plan[5]).start()
        landed(1, Y)
        copy(*plan[4]).start()
        copy(*plan[6]).start()

    def corner():
        landed(3, X | Y, 0)
        landed(4, X | Y, 1)
        copy(*plan[7]).start()

    def finish():
        for k, mask in ((2, CORE), (5, CORE | X), (6, CORE | Y), (7, CORE | X | Y)):
            landed(k, mask)
        for k, mask, to, part in plan:
            copy(k, mask, to, part, own if k < 3 else None).wait_send()

    return [begin, forward, corner, finish]


def pipelined(chains, after=None):
    depth = max(len(chain) for chain in chains)
    for tick in range(len(chains) + depth - 1):
        for i in range(max(0, tick - depth + 1), min(tick, len(chains) - 1) + 1):
            stage = tick - i
            if stage < len(chains[i]):
                chains[i][stage]()
        if after is not None:
            after(tick)


def exchange_rows(place, src, dst, sends, recvs):
    def copy(r):
        return remote(src.at[place.shard(r)], dst.at[place.t], sends.at[r - 1], recvs.at[r - 1], place.device(0, r))

    def landed(r):
        return remote(src.at[place.t], dst.at[place.shard(r)], sends.at[r - 1], recvs.at[r - 1], place.device(0, r))

    def begin():
        for r in (2, 3, 1):
            copy(r).start()

    def finish():
        for r in (1, 2, 3):
            landed(r).wait_recv()
        for r in (1, 2, 3):
            copy(r).wait_send()

    return begin, finish


ANY = pl.BlockSpec(memory_space=pl.ANY)
WIDE = 128


def dot(a, b):
    return jnp.dot(a, b, preferred_element_type=F32)


def dot_nt(a, b):
    return lax.dot_general(a, b, (((1,), (1,)), ((), ())), preferred_element_type=F32)


def dot_tn(a, b):
    return lax.dot_general(a, b, (((0,), (0,)), ((), ())), preferred_element_type=F32)


def chunks(total, size, step):
    def one(i, carry):
        step(pl.ds(pl.multiple_of(i * size, size), size))
        return carry

    lax.fori_loop(0, total // size, one, 0)


def joined(ref, rows):
    return jnp.concatenate([ref[a, rows, :].astype(F32) for a in range(4)], axis=1)


def gain(vec, i):
    return jnp.concatenate([vec[a, i : i + 1, :] for a in range(4)], axis=1)


def norm_one(pk, vec, n1, stats):
    gain_one, route_w = gain(vec, 0), gain(vec, 2)
    width = gain_one.shape[1]

    def step(rows):
        x = joined(pk, rows)
        inv = lax.rsqrt(jnp.sum(x * x, axis=1, keepdims=True) / width + EPS)
        n1[rows, :] = (x * inv * gain_one).astype(BF16)
        stats[rows, 0:1] = inv
        stats[rows, 1:2] = jax.nn.sigmoid(jnp.sum(x * route_w, axis=1, keepdims=True))

    chunks(n1.shape[0], 64, step)


def project(a, n1, fq, qkv):
    width = n1.shape[1]

    def step(k, carry):
        weight = fq[a, k].reshape(width, -1)
        qkv[a, k] = dot(n1[...], weight).astype(BF16)
        return carry

    lax.fori_loop(0, 3, step, 0)


def attend(a, cap, qkv, ho):
    rows, cols = qkv.shape[2], qkv.shape[3]
    pairs = cols // WIDE
    scale = HEAD_DIM ** (-0.5)

    def step(i, carry):
        seq, pair = lax.div(i, jnp.int32(pairs)), lax.rem(i, jnp.int32(pairs))
        rs = pl.ds(pl.multiple_of(seq * cap, cap), cap)
        cs = pl.ds(pl.multiple_of(pair * WIDE, WIDE), WIDE)
        q, k, v = qkv[a, 0, rs, cs], qkv[a, 1, rs, cs], qkv[a, 2, rs, cs]
        first = lax.broadcasted_iota(jnp.int32, (cap, WIDE), 1) < HEAD_DIM
        causal = lax.broadcasted_iota(jnp.int32, (cap, cap), 0) >= lax.broadcasted_iota(jnp.int32, (cap, cap), 1)
        outs = []
        for mine in (first, jnp.logical_not(first)):
            scores = dot_nt(jnp.where(mine, q, jnp.zeros_like(q)), k) * scale
            scores = jnp.where(causal, scores, -1e30)
            exps = jnp.exp(scores - jnp.max(scores, axis=1, keepdims=True))
            probs = (exps / jnp.sum(exps, axis=1, keepdims=True)).astype(BF16)
            outs.append(dot(probs, v))
        ho[a, rs, cs] = jnp.where(first, outs[0], outs[1]).astype(BF16)
        return carry

    lax.fori_loop(0, rows // cap * pairs, step, 0)


def attend_out(pk, vec, ho, fo, at, n2, stats):
    gain_two = gain(vec, 1)
    rows, width = n2.shape
    cols = ho.shape[2]

    def product(rs):
        total = dot(ho[0, rs, :], fo[0].reshape(cols, width))
        for a in range(1, 4):
            total += dot(ho[a, rs, :], fo[a].reshape(cols, width))
        at[rs, :] = total

    chunks(rows, 256, product)

    def step(rs):
        mid = joined(pk, rs) + at[rs, :]
        inv = lax.rsqrt(jnp.sum(mid * mid, axis=1, keepdims=True) / width + EPS)
        n2[rs, :] = (mid * inv * gain_two).astype(BF16)
        stats[rs, 2:3] = inv

    chunks(rows, 64, step)


def raise_up(a, n2, fu, hid, gp, pre):
    rows, width = n2.shape
    inner = hid.shape[2]
    block = pre.shape[1]

    def step(i, carry):
        cs = pl.ds(pl.multiple_of(i * block, block), block)
        weight = fu[a, 0, :, :, cs].reshape(width, block)
        pre[...] = dot(n2[...], weight)

        def bend(rs):
            x = pre[rs, :]
            cdf = 0.5 * (1.0 + lax.erf(x * (2.0**-0.5)))
            hid[a, rs, cs] = (x * cdf).astype(BF16)
            gp[a, rs, cs] = (cdf + x * jnp.exp(-0.5 * x * x) * 0.3989422804014327).astype(BF16)

        chunks(rows, 64, bend)
        return carry

    lax.fori_loop(0, inner // block, step, 0)


def bring_down(a, hid, fd, acc, start):
    inner, width = hid.shape[2], acc.shape[1]
    block = 256

    def step(i, carry):
        cs = pl.ds(pl.multiple_of(i * block, block), block)
        part = dot(hid[a], fd[a, 0, :, :, cs].reshape(inner, block))
        if start:
            acc[:, cs] = part
        else:
            acc[:, cs] += part
        return carry

    lax.fori_loop(0, width // block, step, 0)


def finish_rows(pk, gr, at, acc, rows_out, stats):
    cols = pk.shape[2]

    def step(rs):
        update = at[rs, :] + acc[rs, :]
        router = stats[rs, 1:2]
        result = joined(pk, rs) + router * update
        for a in range(4):
            rows_out[a, rs, :] = result[:, a * cols : (a + 1) * cols].astype(BF16)
        lean = jnp.sum(joined(gr, rs) * update, axis=1, keepdims=True)
        stats[rs, 3:4] = lean * router * (1.0 - router)

    chunks(acc.shape[0], 64, step)


def forward_kernel(cap, *refs):
    picked, grads, vector = refs[0:3]
    local = refs[3:7]
    outs = refs[7:21]
    fulls = refs[21:25]
    pk, gr, vec, n1, qkv, ho, at, n2, hid, gp, acc, rows_out, stats, pre = refs[25:39]
    z_send, z_recv, p_send, p_recv, row_send, row_recv, own_sem, out_sem = refs[39:]
    place = Place()
    own = [
        pltpu.make_async_copy(picked.at[place.t], pk.at[place.t], own_sem.at[0]),
        pltpu.make_async_copy(grads.at[place.t], gr.at[place.t], own_sem.at[1]),
        pltpu.make_async_copy(vector, vec.at[place.t], own_sem.at[2]),
    ]
    for w in range(4):
        own.append(pltpu.make_async_copy(local[w], fulls[w].at[place.t], own_sem.at[3 + w]))
    for copy in own:
        copy.start()
    place.greet()

    def z_copy(w, r):
        if r == 3:
            block = fulls[w].at[place.shard(2), :, place.j]
            return remote(block, block, z_send.at[w, 2], z_recv.at[w, 2], place.device(0, 1))
        return remote(
            local[w].at[:, place.j],
            fulls[w].at[place.t, :, place.j],
            z_send.at[w, r - 1],
            z_recv.at[w, r - 1],
            place.device(0, r),
        )

    def z_landed(w, r):
        block = fulls[w].at[place.shard(r), :, place.j]
        remote(block, block, z_send.at[w, r - 1], z_recv.at[w, r - 1], place.device(0, 1)).wait_recv()

    def z_begin(w):
        z_copy(w, 2).start()
        z_copy(w, 1).start()

    def vec_copy(r):
        return remote(vector, vec.at[place.t], row_send.at[2, r - 1], row_recv.at[2, r - 1], place.device(0, r))

    def vec_landed(r):
        dst = vec.at[place.shard(r)]
        return remote(dst, dst, row_send.at[2, r - 1], row_recv.at[2, r - 1], place.device(0, r))

    rows_one = exchange_rows(place, picked, pk, row_send.at[0], row_recv.at[0])
    rows_two = exchange_rows(place, grads, gr, row_send.at[1], row_recv.at[1])
    q, o, u, d = 0, 1, 2, 3
    chains = []
    for w in range(4):
        for r in (2, 1, 3):
            stages = spread_slices(place, fulls[w], r, p_send.at[w, r - 1], p_recv.at[w, r - 1])

            def first(w=w, r=r, begin=stages[0]):
                z_landed(w, r)
                if r == 2:
                    z_copy(w, 3).start()
                    if w == 0:
                        rows_one[0]()
                    if w + 1 < 4:
                        z_begin(w + 1)
                    if w == 2:
                        rows_two[0]()
                begin()

            chains.append([first] + stages[1:])

    saved = [
        pltpu.make_async_copy(src, dst, out_sem.at[i])
        for i, (src, dst) in enumerate(zip(list(fulls) + [pk, gr, n1, qkv, ho, at, hid, gp, rows_out, stats], outs))
    ]

    def read_rows():
        rows_one[1]()
        for copy in own[:3]:
            copy.wait()
        for r in (1, 2, 3):
            vec_landed(r).wait_recv()
        norm_one(pk, vec, n1, stats)
        saved[4].start()
        saved[6].start()

    def heads_of(r):
        a = place.shard(r)
        project(a, n1, fulls[q], qkv)
        attend(a, cap, qkv, ho)

    def up_of(r):
        raise_up(place.shard(r), n2, fulls[u], hid, gp, pre)

    def down_of(r, start=False):
        bring_down(place.shard(r), hid, fulls[d], acc, start)

    def after(tick):
        if tick == 2:
            read_rows()
            own[3].wait()
            heads_of(0)
        if tick in (3, 4, 5):
            heads_of((2, 1, 3)[tick - 3])
        if tick == 5:
            saved[0].start()
            saved[7].start()
            saved[8].start()
        if tick == 8:
            own[4].wait()
            attend_out(pk, vec, ho, fulls[o], at, n2, stats)
            saved[1].start()
            saved[9].start()
            own[5].wait()
            up_of(0)
        if tick in (9, 10, 11):
            up_of((2, 1, 3)[tick - 9])
        if tick == 11:
            for i in (2, 10, 11):
                saved[i].start()
            own[6].wait()
            down_of(0, True)
        if tick in (12, 13, 14):
            down_of((2, 1, 3)[tick - 12])

    z_begin(0)
    for r in (1, 2, 3):
        vec_copy(r).start()
    pipelined(chains, after)
    saved[3].start()
    rows_two[1]()
    saved[5].start()
    finish_rows(pk, gr, at, acc, rows_out, stats)
    saved[12].start()
    saved[13].start()
    for w in range(4):
        for r in (1, 2, 3):
            z_copy(w, r).wait_send()
    for r in (1, 2, 3):
        vec_copy(r).wait_send()
    for copy in saved:
        copy.wait()


def forward(cap, picked, grads, vector, local):
    _, rows, cols = picked.shape
    width = 4 * cols
    inner = local[2].shape[3]
    fulls = [(4,) + w.shape for w in local]
    dma = pltpu.SemaphoreType.DMA
    kept = [
        ((4, rows, cols), BF16),
        ((4, rows, cols), BF16),
        ((rows, width), BF16),
        ((4, 3, rows, cols), BF16),
        ((4, rows, cols), BF16),
        ((rows, width), F32),
        ((4, rows, inner), BF16),
        ((4, rows, inner), BF16),
        ((4, rows, cols), BF16),
        ((rows, WIDE), F32),
    ]
    vmem = pltpu.VMEM
    scratch = [vmem(f, BF16) for f in fulls] + [
        vmem((4, rows, cols), BF16),
        vmem((4, rows, cols), BF16),
        vmem((4, 8, cols), F32),
        vmem((rows, width), BF16),
        vmem((4, 3, rows, cols), BF16),
        vmem((4, rows, cols), BF16),
        vmem((rows, width), F32),
        vmem((rows, width), BF16),
        vmem((4, rows, inner), BF16),
        vmem((4, rows, inner), BF16),
        vmem((rows, width), F32),
        vmem((4, rows, cols), BF16),
        vmem((rows, WIDE), F32),
        vmem((rows, 256), F32),
        dma((4, 3)),
        dma((4, 3)),
        dma((4, 3, 8)),
        dma((4, 3, 8)),
        dma((3, 3)),
        dma((3, 3)),
        dma((7,)),
        dma((14,)),
    ]
    return pl.pallas_call(
        functools.partial(forward_kernel, cap),
        in_specs=[ANY] * 7,
        out_specs=[ANY] * 14,
        out_shape=[jax.ShapeDtypeStruct(f, BF16) for f in fulls] + [jax.ShapeDtypeStruct(*k) for k in kept],
        scratch_shapes=scratch,
        compiler_params=pltpu.CompilerParams(
            collective_id=1, has_side_effects=True, vmem_limit_bytes=60 * 1024 * 1024
        ),
        name="forward",
    )(picked, grads, vector, *local)


def add_blocks(target, extra, leads):
    for index_t, index_e in leads:
        target[index_t] = (target[index_t].astype(F32) + extra[index_e].astype(F32)).astype(BF16)


def sum_chain(place, grad, sum1, got1, got2, got3, got4, got5, stage, sends, recvs, sem):
    count, rows = grad.shape[1], grad.shape[5]
    half = rows // 2
    low, high = pl.ds(0, half), pl.ds(half, half)
    c, x, y, t = place.c, place.x, place.y, place.t
    own = pltpu.make_async_copy(grad.at[:, :, :, :, c], sum1, sem)
    every = [(tt, k) for tt in range(4) for k in range(count)]

    def copy(n):
        src, dst, device = (
            lambda: (grad.at[:, :, :, :, 1 - c], got1, place.device(CORE)),
            lambda: (sum1.at[:, :, :, 1 - x, low], got2.at[0], place.device(X)),
            lambda: (sum1.at[:, :, 1 - y, :, high], got2.at[1], place.device(Y)),
            lambda: (sum1.at[:, :, 1 - y, x, low], got3.at[0], place.device(Y)),
            lambda: (sum1.at[:, :, y, 1 - x, high], got3.at[1], place.device(X)),
            lambda: (sum1.at[place.shard(1), :, y, x], got4.at[0], place.device(0, 1)),
            lambda: (sum1.at[place.shard(3), :, y, x], got4.at[1], place.device(0, 1)),
            lambda: (sum1.at[place.shard(2), :, y, x], got5, place.device(0, 2)),
        )[n]()
        return remote(src, dst, sends.at[n], recvs.at[n], device)

    def s0():
        own.start()
        copy(0).start()

    def s1():
        own.wait()
        copy(0).wait_recv()
        for tt, k in every:
            for b in range(2):
                for a in range(2):
                    i = (tt, k, b, a)
                    sum1[i] = (sum1[i].astype(F32) + got1[i].astype(F32)).astype(BF16)
        copy(1).start()
        copy(2).start()

    def s2():
        copy(1).wait_recv()
        copy(1).wait_send()
        for tt, k in every:
            for b in range(2):
                i = (tt, k, b, x, low)
                sum1[i] = (sum1[i].astype(F32) + got2[0, tt, k, b].astype(F32)).astype(BF16)
        copy(3).start()
        copy(2).wait_recv()
        copy(2).wait_send()
        for tt, k in every:
            for a in range(2):
                i = (tt, k, y, a, high)
                sum1[i] = (sum1[i].astype(F32) + got2[1, tt, k, a].astype(F32)).astype(BF16)
        copy(4).start()

    def s3():
        for side, n in ((0, 3), (1, 4)):
            copy(n).wait_recv()
            copy(n).wait_send()
            part = (low, high)[side]
            for tt, k in every:
                i = (tt, k, y, x, part)
                sum1[i] = (sum1[i].astype(F32) + got3[side, tt, k].astype(F32)).astype(BF16)
        copy(5).start()
        copy(6).start()

    def s4():
        for side, shard in ((0, t), (1, place.shard(2))):
            copy(5 + side).wait_recv()
            copy(5 + side).wait_send()
            for k in range(count):
                i = (shard, k, y, x)
                sum1[i] = (sum1[i].astype(F32) + got4[side, k].astype(F32)).astype(BF16)
        copy(7).start()

    def s5():
        copy(7).wait_recv()
        copy(7).wait_send()
        copy(0).wait_send()
        for k in range(count):
            i = (t, k, y, x)
            stage[k, place.j] = (sum1[i].astype(F32) + got5[k].astype(F32)).astype(BF16)

    stages = spread_slices(place, stage, None, sends.at[pl.ds(8, 8)], recvs.at[pl.ds(8, 8)])

    def last():
        s5()
        stages[0]()

    return [s0, s1, s2, s3, s4, last] + stages[1:]


def sum_all_kernel(count, *refs):
    out_rows, in_rows = refs[0:2]
    grads = refs[2 : 2 + count]
    got_out, got_in = refs[2 + count : 4 + count]
    results = refs[4 + count : 4 + 2 * count]
    rest = refs[4 + 2 * count :]
    buffers = [rest[7 * i : 7 * i + 7] for i in range(count)]
    sends, recvs, own_sem, row_send, row_recv, res_sem = rest[7 * count :]
    place = Place()
    own = [
        pltpu.make_async_copy(out_rows.at[place.t], got_out.at[place.t], res_sem.at[0]),
        pltpu.make_async_copy(in_rows.at[place.t], got_in.at[place.t], res_sem.at[1]),
    ]
    for copy in own:
        copy.start()
    place.greet()
    rows_one = exchange_rows(place, out_rows, got_out, row_send.at[0], row_recv.at[0])
    rows_two = exchange_rows(place, in_rows, got_in, row_send.at[1], row_recv.at[1])
    chains = [
        sum_chain(place, grads[i], *buffers[i], sends.at[i], recvs.at[i], own_sem.at[i]) for i in range(count)
    ]
    write = []
    for i in range(count):
        copy = pltpu.make_async_copy(buffers[i][6], results[i], res_sem.at[2 + i])
        chains[i].append(copy.start)
        write.append(copy)
    rows_one[0]()
    rows_two[0]()
    pipelined(chains)
    rows_one[1]()
    rows_two[1]()
    for copy in own + write:
        copy.wait()


def sum_all(out_rows, in_rows, grads):
    count = len(grads)
    dma = pltpu.SemaphoreType.DMA
    scratch = []
    for g in grads:
        _, k, _, _, _, rows, cols = g.shape
        scratch += [
            pltpu.VMEM((4, k, 2, 2, rows, cols), BF16),
            pltpu.VMEM((4, k, 2, 2, rows, cols), BF16),
            pltpu.VMEM((2, 4, k, 2, rows // 2, cols), BF16),
            pltpu.VMEM((2, 4, k, rows // 2, cols), BF16),
            pltpu.VMEM((2, k, rows, cols), BF16),
            pltpu.VMEM((k, rows, cols), BF16),
            pltpu.VMEM((k, 8, rows, cols), BF16),
        ]
    return pl.pallas_call(
        functools.partial(sum_all_kernel, count),
        in_specs=[ANY] * (2 + count),
        out_specs=[ANY] * (2 + count),
        out_shape=[jax.ShapeDtypeStruct(out_rows.shape, BF16)] * 2
        + [jax.ShapeDtypeStruct((g.shape[1], 8) + g.shape[5:], BF16) for g in grads],
        scratch_shapes=scratch
        + [dma((count, 16)), dma((count, 16)), dma((count,)), dma((2, 3)), dma((2, 3)), dma((2 + count,))],
        compiler_params=pltpu.CompilerParams(
            collective_id=2, has_side_effects=True, vmem_limit_bytes=60 * 1024 * 1024
        ),
        name="sum_all",
    )(out_rows, in_rows, *grads)


def body(all_dp, n_t, block_input, routes, out_grad, w_qkv, w_out, w_up, w_down, gain_attn, gain_mlp, w_router):
    seqs, length, cols = block_input.shape
    cap = routes.shape[1]
    width = cols * n_t
    own = seqs // n_t
    rows = own * cap
    heads = cols // HEAD_DIM
    outer_bits = [1 << i for i in range(3, all_dp.bit_length() - 1)]

    def send(value, mask_dp, mask_t):
        pairs = [
            (d * n_t + s, (d ^ mask_dp) * n_t + (s ^ mask_t)) for d in range(all_dp) for s in range(n_t)
        ]
        return lax.ppermute(value, ("dp", "tensor"), pairs)

    vector = jnp.concatenate([gain_attn[None], gain_mlp[None], w_router[None], jnp.zeros((5, cols), F32)])
    local = [
        w_qkv.transpose(1, 0, 2).reshape(3, GROUP, width // GROUP, cols),
        w_out.reshape(1, GROUP, cols // GROUP, width),
        w_up.reshape(1, GROUP, width // GROUP, w_up.shape[1]),
        w_down.reshape(1, GROUP, w_down.shape[0] // GROUP, width),
    ]
    picked_all = gather_rows(routes, block_input).reshape(n_t, rows, cols)
    grad_all = gather_rows(routes, out_grad).reshape(n_t, rows, cols)
    wq, wo, wu, wd, picked, grad_rows, normed_one, qkv, head_out, attn_out, hidden, bend, out_rows, stats = forward(
        cap, picked_all, grad_all, vector, local
    )
    wq = wq.reshape(n_t, 3, width, cols)
    wo = wo.reshape(n_t, cols, width)
    wu = wu.reshape(n_t, width, -1)
    wd = wd.reshape(n_t, -1, width)
    picked = picked.transpose(1, 0, 2).reshape(rows, width).astype(F32)
    grad_rows = grad_rows.transpose(1, 0, 2).reshape(rows, width).astype(F32)
    inv_one, router, inv_two, d_logit = stats[:, 0:1], stats[:, 1:2], stats[:, 2:3], stats[:, 3:4]
    middle = picked + attn_out
    vectors = lax.all_gather(vector[:3], "tensor", axis=1, tiled=True)
    gain_one, gain_two, route_w = vectors[0], vectors[1], vectors[2]
    normed_two = (middle * inv_two * gain_two).astype(BF16)
    split = qkv.reshape(n_t, 3, own, cap, heads, HEAD_DIM)
    queries, keys, values = split[:, 0], split[:, 1], split[:, 2]
    scale = HEAD_DIM ** (-0.5)
    causal = jnp.arange(cap)[:, None] >= jnp.arange(cap)[None, :]
    scores = jnp.einsum("rsqhe,rskhe->rshqk", queries, keys, preferred_element_type=F32) * scale
    scores = jnp.where(causal, scores, -1e30)
    top = jnp.max(scores, axis=-1, keepdims=True)
    exps = jnp.exp(scores - top)
    total = jnp.sum(exps, axis=-1, keepdims=True)
    probs_full = exps / total
    probs = probs_full.astype(BF16)

    d_update = router * grad_rows
    d_mlp = d_update.astype(BF16)
    grad_down = jnp.einsum("rsf,sd->rfd", hidden, d_mlp, preferred_element_type=F32).astype(BF16)
    d_hidden = jnp.einsum("sd,rfd->rsf", d_mlp, wd, preferred_element_type=F32)
    d_pre = (d_hidden * bend.astype(F32)).astype(BF16)
    grad_up = jnp.einsum("sd,rsf->rdf", normed_two, d_pre, preferred_element_type=F32).astype(BF16)
    d_normed_two = jnp.einsum("rsf,rdf->sd", d_pre, wu, preferred_element_type=F32)
    grad_gain_mlp = jnp.sum(d_normed_two * middle * inv_two, axis=0)
    e_two = d_normed_two * gain_two
    proj_two = jnp.sum(e_two * middle, axis=-1, keepdims=True)
    d_middle = inv_two * e_two - middle * inv_two**3 * proj_two / width
    d_attn = (d_update + d_middle).astype(BF16)
    grad_out = jnp.einsum("rse,sd->red", head_out, d_attn, preferred_element_type=F32).astype(BF16)
    d_head = jnp.einsum("sd,red->rse", d_attn, wo, preferred_element_type=F32).astype(BF16)
    d_head = d_head.reshape(n_t, own, cap, heads, HEAD_DIM)
    d_values = jnp.einsum("rshqk,rsqhe->rskhe", probs, d_head, preferred_element_type=F32)
    d_probs = jnp.einsum("rsqhe,rskhe->rshqk", d_head, values, preferred_element_type=F32)
    row_dot = jnp.sum(probs_full * d_probs, axis=-1, keepdims=True)
    d_scores = (probs_full * (d_probs - row_dot)).astype(BF16)
    d_queries = jnp.einsum("rshqk,rskhe->rsqhe", d_scores, keys, preferred_element_type=F32) * scale
    d_keys = jnp.einsum("rshqk,rsqhe->rskhe", d_scores, queries, preferred_element_type=F32) * scale
    d_proj = jnp.stack([d_queries, d_keys, d_values], axis=1).astype(BF16)
    d_proj = d_proj.reshape(n_t, 3, rows, cols)
    grad_qkv = jnp.einsum("sd,rkse->rkde", normed_one, d_proj, preferred_element_type=F32).astype(BF16)
    d_normed_one = jnp.einsum("rkse,rkde->sd", d_proj, wq, preferred_element_type=F32)
    grad_gain_attn = jnp.sum(d_normed_one * picked * inv_one, axis=0)
    e_one = d_normed_one * gain_one
    grad_router = jnp.sum(d_logit * picked, axis=0)
    proj_one = jnp.sum(e_one * picked, axis=-1, keepdims=True)
    d_picked = (
        grad_rows
        + d_middle
        + inv_one * e_one
        - picked * inv_one**3 * proj_one / width
        + d_logit * route_w
    )
    in_rows = d_picked.astype(BF16).reshape(rows, n_t, cols).transpose(1, 0, 2)

    def cut(value):
        a, b, c, d = value.shape
        return value.reshape(a, b, 2, 2, 2, c // GROUP, d)

    got_out, got_in, s_down, s_up, s_out, s_qkv = sum_all(
        out_rows,
        in_rows,
        [cut(grad_down[:, None]), cut(grad_up[:, None]), cut(grad_out[:, None]), cut(grad_qkv)],
    )
    layer_out = scatter_rows(routes, block_input, got_out.reshape(seqs, cap, cols))
    input_grad = scatter_rows(routes, out_grad, got_in.reshape(seqs, cap, cols))
    sums = jnp.stack([grad_gain_attn, grad_gain_mlp, grad_router])
    sums = lax.psum_scatter(sums, "tensor", scatter_dimension=1, tiled=True)
    sums = lax.psum(sums, "dp")

    def settle(value, shape):
        value = value.reshape(shape).astype(F32)
        for bit in outer_bits:
            value = value + send(value, bit, 0)
        return value

    g_qkv = settle(s_qkv, (3, width, cols)).transpose(1, 0, 2)
    g_out = settle(s_out, w_out.shape)
    g_up = settle(s_up, w_up.shape)
    g_down = settle(s_down, w_down.shape)
    return (layer_out, input_grad, g_qkv, g_out, g_up, g_down, sums[0], sums[1], sums[2])


def solution(mesh):
    placed = (
        P("dp", None, "tensor"),
        P("dp", None),
        P("dp", None, "tensor"),
        P(None, None, "tensor"),
        P("tensor", None),
        P(None, "tensor"),
        P("tensor", None),
        P("tensor"),
        P("tensor"),
        P("tensor"),
    )
    return jax.shard_map(
        functools.partial(body, mesh.shape["dp"], mesh.shape["tensor"]),
        mesh=mesh,
        in_specs=placed,
        out_specs=(
            P("dp", None, "tensor"),
            P("dp", None, "tensor"),
            P(None, None, "tensor"),
            P("tensor", None),
            P(None, "tensor"),
            P("tensor", None),
            P("tensor"),
            P("tensor"),
            P("tensor"),
        ),
        check_vma=False,
    )
```

```python
import functools

import jax
import jax.numpy as jnp
from jax import lax
from jax.experimental import pallas as pl
from jax.experimental.pallas import tpu as pltpu
from jax.sharding import PartitionSpec as P

HEAD_DIM = 64
EPS = 1e-06
F32 = jnp.float32
BF16 = jnp.bfloat16


def exact_gelu(values):
    return jax.nn.gelu(values, approximate=False)


def gather_kernel(routes_ref, block_ref, out_ref):
    length = block_ref.shape[1]
    places = lax.broadcasted_iota(jnp.int32, (routes_ref.shape[1], length), 1)
    chosen = (routes_ref[0] == places).astype(BF16)
    out_ref[0] = jnp.dot(chosen, block_ref[0], preferred_element_type=F32).astype(BF16)


def gather_rows(routes, block):
    seqs, length, cols = block.shape
    cap = routes.shape[1]
    return pl.pallas_call(
        gather_kernel,
        grid=(seqs,),
        in_specs=[
            pl.BlockSpec((1, cap, 1), lambda s: (s, 0, 0)),
            pl.BlockSpec((1, length, cols), lambda s: (s, 0, 0)),
        ],
        out_specs=pl.BlockSpec((1, cap, cols), lambda s: (s, 0, 0)),
        out_shape=jax.ShapeDtypeStruct((seqs, cap, cols), BF16),
        cost_estimate=pl.CostEstimate(
            flops=2 * seqs * cap * length * cols, bytes_accessed=block.size * 2, transcendentals=0
        ),
        name="gather_rows",
    )(routes[:, :, None], block)


def scatter_kernel(routes_ref, block_ref, rows_ref, out_ref):
    length = block_ref.shape[1]
    cap = routes_ref.shape[2]
    places = lax.broadcasted_iota(jnp.int32, (length, cap), 0)
    chosen = routes_ref[0] == places
    hit = jnp.max(chosen.astype(F32), axis=1, keepdims=True) > 0.0
    spread = jnp.dot(chosen.astype(BF16), rows_ref[0], preferred_element_type=F32)
    out_ref[0] = jnp.where(hit, spread, block_ref[0].astype(F32)).astype(BF16)


def scatter_rows(routes, block, rows):
    seqs, length, cols = block.shape
    cap = rows.shape[1]
    return pl.pallas_call(
        scatter_kernel,
        grid=(seqs,),
        in_specs=[
            pl.BlockSpec((1, 1, cap), lambda s: (s, 0, 0)),
            pl.BlockSpec((1, length, cols), lambda s: (s, 0, 0)),
            pl.BlockSpec((1, cap, cols), lambda s: (s, 0, 0)),
        ],
        out_specs=pl.BlockSpec((1, length, cols), lambda s: (s, 0, 0)),
        out_shape=jax.ShapeDtypeStruct(block.shape, BF16),
        cost_estimate=pl.CostEstimate(
            flops=2 * seqs * cap * length * cols, bytes_accessed=block.size * 4, transcendentals=0
        ),
        name="scatter_rows",
    )(routes[:, None, :], block, rows)


MESH = pl.DeviceIdType.MESH
GROUP = 8


def flip(value, bit):
    return value + bit - 2 * bit * lax.rem(lax.div(value, jnp.int32(bit)), jnp.int32(2))


class Place:
    def __init__(self):
        self.dp = lax.axis_index("dp").astype(jnp.int32)
        self.t = lax.axis_index("tensor").astype(jnp.int32)
        self.j = lax.rem(self.dp, jnp.int32(GROUP))
        self.c = lax.rem(self.j, jnp.int32(2))
        self.x = lax.rem(lax.div(self.j, jnp.int32(2)), jnp.int32(2))
        self.y = lax.div(self.j, jnp.int32(4))

    def slot(self, mask):
        value = self.j
        for bit in (1, 2, 4):
            if mask & bit:
                value = flip(value, bit)
        return value

    def shard(self, r):
        value = self.t
        for bit in (1, 2):
            if r & bit:
                value = flip(value, bit)
        return value

    def device(self, mask=0, r=0):
        value = self.dp
        for bit in (1, 2, 4):
            if mask & bit:
                value = flip(value, bit)
        return (value, self.shard(r))

    def greet(self):
        barrier = pltpu.get_barrier_semaphore()
        partners = [(mask, 0) for mask in (1, 2, 4)] + [(0, r) for r in (1, 2, 3)]
        for mask, r in partners:
            pl.semaphore_signal(barrier, inc=1, device_id=self.device(mask, r), device_id_type=MESH)
        pl.semaphore_wait(barrier, len(partners))


def remote(src, dst, send_sem, recv_sem, device):
    return pltpu.make_async_remote_copy(
        src_ref=src, dst_ref=dst, send_sem=send_sem, recv_sem=recv_sem, device_id=device, device_id_type=MESH
    )


CORE, X, Y = 1, 2, 4


def spread_slices(place, full, r, sends, recvs, own=None):
    def block(mask, part=None):
        ref = full.at[place.shard(r)] if r is not None else full
        ref = ref.at[:, place.slot(mask)]
        if part is None:
            return ref
        half = ref.shape[1] // 2
        return ref.at[:, pl.ds(part * half, half)]

    def copy(k, mask, to, part=None, src=None):
        return remote(src if src is not None else block(mask, part), block(mask, part), sends.at[k], recvs.at[k], place.device(to))

    def landed(k, mask, part=None):
        remote(block(mask, part), block(mask, part), sends.at[k], recvs.at[k], place.device(CORE)).wait_recv()

    plan = [
        (0, 0, X, None),
        (1, 0, Y, None),
        (2, 0, CORE, None),
        (3, X, Y, 0),
        (4, Y, X, 1),
        (5, X, CORE, None),
        (6, Y, CORE, None),
        (7, X | Y, CORE, None),
    ]

    def begin():
        for k in (0, 1, 2):
            _, mask, to, part = plan[k]
            copy(k, mask, to, part, own).start()

    def forward():
        landed(0, X)
        copy(*plan[3]).start()
        copy(*plan[5]).start()
        landed(1, Y)
        copy(*plan[4]).start()
        copy(*plan[6]).start()

    def corner():
        landed(3, X | Y, 0)
        landed(4, X | Y, 1)
        copy(*plan[7]).start()

    def finish():
        for k, mask in ((2, CORE), (5, CORE | X), (6, CORE | Y), (7, CORE | X | Y)):
            landed(k, mask)
        for k, mask, to, part in plan:
            copy(k, mask, to, part, own if k < 3 else None).wait_send()

    return [begin, forward, corner, finish]


def pipelined(chains, after=None):
    depth = max(len(chain) for chain in chains)
    for tick in range(len(chains) + depth - 1):
        for i in range(max(0, tick - depth + 1), min(tick, len(chains) - 1) + 1):
            stage = tick - i
            if stage < len(chains[i]):
                chains[i][stage]()
        if after is not None:
            after(tick)


def exchange_rows(place, src, dst, sends, recvs):
    def copy(r):
        return remote(src.at[place.shard(r)], dst.at[place.t], sends.at[r - 1], recvs.at[r - 1], place.device(0, r))

    def landed(r):
        return remote(src.at[place.t], dst.at[place.shard(r)], sends.at[r - 1], recvs.at[r - 1], place.device(0, r))

    def begin():
        for r in (2, 3, 1):
            copy(r).start()

    def finish():
        for r in (1, 2, 3):
            landed(r).wait_recv()
        for r in (1, 2, 3):
            copy(r).wait_send()

    return begin, finish


ANY = pl.BlockSpec(memory_space=pl.ANY)
WIDE = 128


def dot(a, b):
    return jnp.dot(a, b, preferred_element_type=F32)


def dot_nt(a, b):
    return lax.dot_general(a, b, (((1,), (1,)), ((), ())), preferred_element_type=F32)


def dot_tn(a, b):
    return lax.dot_general(a, b, (((0,), (0,)), ((), ())), preferred_element_type=F32)


def chunks(total, size, step):
    def one(i, carry):
        step(pl.ds(pl.multiple_of(i * size, size), size))
        return carry

    lax.fori_loop(0, total // size, one, 0)


def joined(ref, rows):
    return jnp.concatenate([ref[a, rows, :].astype(F32) for a in range(4)], axis=1)


def gain(vec, i):
    return jnp.concatenate([vec[a, i : i + 1, :] for a in range(4)], axis=1)


def norm_one(pk, vec, n1, stats):
    gain_one, route_w = gain(vec, 0), gain(vec, 2)
    width = gain_one.shape[1]

    def step(rows):
        x = joined(pk, rows)
        inv = lax.rsqrt(jnp.sum(x * x, axis=1, keepdims=True) / width + EPS)
        n1[rows, :] = (x * inv * gain_one).astype(BF16)
        stats[rows, 0:1] = inv
        stats[rows, 1:2] = jax.nn.sigmoid(jnp.sum(x * route_w, axis=1, keepdims=True))

    chunks(n1.shape[0], 64, step)


def project(a, n1, fq, qkv):
    width = n1.shape[1]

    def step(k, carry):
        weight = fq[a, k].reshape(width, -1)
        qkv[a, k] = dot(n1[...], weight).astype(BF16)
        return carry

    lax.fori_loop(0, 3, step, 0)


def attend(a, cap, qkv, ho):
    rows, cols = qkv.shape[2], qkv.shape[3]
    pairs = cols // WIDE
    scale = HEAD_DIM ** (-0.5)

    def step(i, carry):
        seq, pair = lax.div(i, jnp.int32(pairs)), lax.rem(i, jnp.int32(pairs))
        rs = pl.ds(pl.multiple_of(seq * cap, cap), cap)
        cs = pl.ds(pl.multiple_of(pair * WIDE, WIDE), WIDE)
        q, k, v = qkv[a, 0, rs, cs], qkv[a, 1, rs, cs], qkv[a, 2, rs, cs]
        first = lax.broadcasted_iota(jnp.int32, (cap, WIDE), 1) < HEAD_DIM
        causal = lax.broadcasted_iota(jnp.int32, (cap, cap), 0) >= lax.broadcasted_iota(jnp.int32, (cap, cap), 1)
        outs = []
        for mine in (first, jnp.logical_not(first)):
            scores = dot_nt(jnp.where(mine, q, jnp.zeros_like(q)), k) * scale
            scores = jnp.where(causal, scores, -1e30)
            exps = jnp.exp(scores - jnp.max(scores, axis=1, keepdims=True))
            probs = (exps / jnp.sum(exps, axis=1, keepdims=True)).astype(BF16)
            outs.append(dot(probs, v))
        ho[a, rs, cs] = jnp.where(first, outs[0], outs[1]).astype(BF16)
        return carry

    lax.fori_loop(0, rows // cap * pairs, step, 0)


def attend_out(pk, vec, ho, fo, at, n2, stats):
    gain_two = gain(vec, 1)
    rows, width = n2.shape
    cols = ho.shape[2]

    def product(rs):
        total = dot(ho[0, rs, :], fo[0].reshape(cols, width))
        for a in range(1, 4):
            total += dot(ho[a, rs, :], fo[a].reshape(cols, width))
        at[rs, :] = total

    chunks(rows, 256, product)

    def step(rs):
        mid = joined(pk, rs) + at[rs, :]
        inv = lax.rsqrt(jnp.sum(mid * mid, axis=1, keepdims=True) / width + EPS)
        n2[rs, :] = (mid * inv * gain_two).astype(BF16)
        stats[rs, 2:3] = inv

    chunks(rows, 64, step)


def raise_up(a, n2, fu, hid, gp, pre):
    rows, width = n2.shape
    inner = hid.shape[2]
    block = pre.shape[1]

    def step(i, carry):
        cs = pl.ds(pl.multiple_of(i * block, block), block)
        weight = fu[a, 0, :, :, cs].reshape(width, block)
        pre[...] = dot(n2[...], weight)

        def bend(rs):
            x = pre[rs, :]
            cdf = 0.5 * (1.0 + lax.erf(x * (2.0**-0.5)))
            hid[a, rs, cs] = (x * cdf).astype(BF16)
            gp[a, rs, cs] = (cdf + x * jnp.exp(-0.5 * x * x) * 0.3989422804014327).astype(BF16)

        chunks(rows, 64, bend)
        return carry

    lax.fori_loop(0, inner // block, step, 0)


def bring_down(a, hid, fd, acc, start):
    inner, width = hid.shape[2], acc.shape[1]
    block = 256

    def step(i, carry):
        cs = pl.ds(pl.multiple_of(i * block, block), block)
        part = dot(hid[a], fd[a, 0, :, :, cs].reshape(inner, block))
        if start:
            acc[:, cs] = part
        else:
            acc[:, cs] += part
        return carry

    lax.fori_loop(0, width // block, step, 0)


def finish_rows(pk, gr, at, acc, rows_out, stats):
    cols = pk.shape[2]

    def step(rs):
        update = at[rs, :] + acc[rs, :]
        router = stats[rs, 1:2]
        result = joined(pk, rs) + router * update
        for a in range(4):
            rows_out[a, rs, :] = result[:, a * cols : (a + 1) * cols].astype(BF16)
        lean = jnp.sum(joined(gr, rs) * update, axis=1, keepdims=True)
        stats[rs, 3:4] = lean * router * (1.0 - router)

    chunks(acc.shape[0], 64, step)


def forward_kernel(cap, *refs):
    picked, grads, vector = refs[0:3]
    local = refs[3:7]
    outs = refs[7:22]
    fulls = refs[22:26]
    pk, gr, vec, n1, qkv, ho, at, n2, hid, gp, acc, rows_out, stats, pre = refs[26:40]
    z_send, z_recv, p_send, p_recv, row_send, row_recv, own_sem, out_sem = refs[40:]
    place = Place()
    own = [
        pltpu.make_async_copy(picked.at[place.t], pk.at[place.t], own_sem.at[0]),
        pltpu.make_async_copy(grads.at[place.t], gr.at[place.t], own_sem.at[1]),
        pltpu.make_async_copy(vector, vec.at[place.t], own_sem.at[2]),
    ]
    for w in range(4):
        own.append(pltpu.make_async_copy(local[w], fulls[w].at[place.t], own_sem.at[3 + w]))
    for copy in own:
        copy.start()
    place.greet()

    def z_copy(w, r):
        if r == 3:
            block = fulls[w].at[place.shard(2), :, place.j]
            return remote(block, block, z_send.at[w, 2], z_recv.at[w, 2], place.device(0, 1))
        return remote(
            local[w].at[:, place.j],
            fulls[w].at[place.t, :, place.j],
            z_send.at[w, r - 1],
            z_recv.at[w, r - 1],
            place.device(0, r),
        )

    def z_landed(w, r):
        block = fulls[w].at[place.shard(r), :, place.j]
        remote(block, block, z_send.at[w, r - 1], z_recv.at[w, r - 1], place.device(0, 1)).wait_recv()

    def z_begin(w):
        z_copy(w, 2).start()
        z_copy(w, 1).start()

    def vec_copy(r):
        return remote(vector, vec.at[place.t], row_send.at[2, r - 1], row_recv.at[2, r - 1], place.device(0, r))

    def vec_landed(r):
        dst = vec.at[place.shard(r)]
        return remote(dst, dst, row_send.at[2, r - 1], row_recv.at[2, r - 1], place.device(0, r))

    rows_one = exchange_rows(place, picked, pk, row_send.at[0], row_recv.at[0])
    rows_two = exchange_rows(place, grads, gr, row_send.at[1], row_recv.at[1])
    q, o, u, d = 0, 1, 2, 3
    chains = []
    for w in range(4):
        for r in (2, 1, 3):
            stages = spread_slices(place, fulls[w], r, p_send.at[w, r - 1], p_recv.at[w, r - 1])

            def first(w=w, r=r, begin=stages[0]):
                z_landed(w, r)
                if r == 2:
                    z_copy(w, 3).start()
                    if w == 0:
                        rows_one[0]()
                    if w + 1 < 4:
                        z_begin(w + 1)
                    if w == 2:
                        rows_two[0]()
                begin()

            chains.append([first] + stages[1:])

    saved = [
        pltpu.make_async_copy(src, dst, out_sem.at[i])
        for i, (src, dst) in enumerate(zip(list(fulls) + [pk, gr, n1, qkv, ho, at, hid, gp, rows_out, stats, vec], outs))
    ]

    def read_rows():
        rows_one[1]()
        for copy in own[:3]:
            copy.wait()
        for r in (1, 2, 3):
            vec_landed(r).wait_recv()
        norm_one(pk, vec, n1, stats)
        saved[4].start()
        saved[6].start()
        saved[14].start()

    def heads_of(r):
        a = place.shard(r)
        project(a, n1, fulls[q], qkv)
        attend(a, cap, qkv, ho)

    def up_of(r):
        raise_up(place.shard(r), n2, fulls[u], hid, gp, pre)

    def down_of(r, start=False):
        bring_down(place.shard(r), hid, fulls[d], acc, start)

    def after(tick):
        if tick == 2:
            read_rows()
            own[3].wait()
            heads_of(0)
        if tick in (3, 4, 5):
            heads_of((2, 1, 3)[tick - 3])
        if tick == 5:
            saved[0].start()
            saved[7].start()
            saved[8].start()
        if tick == 8:
            own[4].wait()
            attend_out(pk, vec, ho, fulls[o], at, n2, stats)
            saved[1].start()
            saved[9].start()
            own[5].wait()
            up_of(0)
        if tick in (9, 10, 11):
            up_of((2, 1, 3)[tick - 9])
        if tick == 11:
            for i in (2, 10, 11):
                saved[i].start()
            own[6].wait()
            down_of(0, True)
        if tick in (12, 13, 14):
            down_of((2, 1, 3)[tick - 12])

    z_begin(0)
    for r in (1, 2, 3):
        vec_copy(r).start()
    pipelined(chains, after)
    saved[3].start()
    rows_two[1]()
    saved[5].start()
    finish_rows(pk, gr, at, acc, rows_out, stats)
    saved[12].start()
    saved[13].start()
    for w in range(4):
        for r in (1, 2, 3):
            z_copy(w, r).wait_send()
    for r in (1, 2, 3):
        vec_copy(r).wait_send()
    for copy in saved:
        copy.wait()


def forward(cap, picked, grads, vector, local):
    _, rows, cols = picked.shape
    width = 4 * cols
    inner = local[2].shape[3]
    fulls = [(4,) + w.shape for w in local]
    dma = pltpu.SemaphoreType.DMA
    kept = [
        ((4, rows, cols), BF16),
        ((4, rows, cols), BF16),
        ((rows, width), BF16),
        ((4, 3, rows, cols), BF16),
        ((4, rows, cols), BF16),
        ((rows, width), F32),
        ((4, rows, inner), BF16),
        ((4, rows, inner), BF16),
        ((4, rows, cols), BF16),
        ((rows, WIDE), F32),
        ((4, 8, cols), F32),
    ]
    vmem = pltpu.VMEM
    scratch = [vmem(f, BF16) for f in fulls] + [
        vmem((4, rows, cols), BF16),
        vmem((4, rows, cols), BF16),
        vmem((4, 8, cols), F32),
        vmem((rows, width), BF16),
        vmem((4, 3, rows, cols), BF16),
        vmem((4, rows, cols), BF16),
        vmem((rows, width), F32),
        vmem((rows, width), BF16),
        vmem((4, rows, inner), BF16),
        vmem((4, rows, inner), BF16),
        vmem((rows, width), F32),
        vmem((4, rows, cols), BF16),
        vmem((rows, WIDE), F32),
        vmem((rows, 256), F32),
        dma((4, 3)),
        dma((4, 3)),
        dma((4, 3, 8)),
        dma((4, 3, 8)),
        dma((3, 3)),
        dma((3, 3)),
        dma((7,)),
        dma((15,)),
    ]
    return pl.pallas_call(
        functools.partial(forward_kernel, cap),
        in_specs=[ANY] * 7,
        out_specs=[ANY] * 15,
        out_shape=[jax.ShapeDtypeStruct(f, BF16) for f in fulls] + [jax.ShapeDtypeStruct(*k) for k in kept],
        scratch_shapes=scratch,
        compiler_params=pltpu.CompilerParams(
            collective_id=1, has_side_effects=True, vmem_limit_bytes=60 * 1024 * 1024
        ),
        name="forward",
    )(picked, grads, vector, *local)


def half_blocks(ref_cols, count, parity):
    parts = []
    for b in range(count // 2):
        start = pl.multiple_of((2 * b + parity) * WIDE, WIDE)
        parts.append(ref_cols(pl.ds(start, WIDE)))
    return jnp.concatenate(parts, axis=1)


def outer(left, right, width, put, block=512):
    turned = jnp.transpose(left)

    def step(i, carry):
        cs = pl.ds(pl.multiple_of(i * block, block), block)
        put(cs, dot(turned, right(cs)))
        return carry

    lax.fori_loop(0, width // block, step, 0)


class Sum:
    def __init__(self, place, away, buf, got2, got3, got4, got5, result, sends, recvs, own_sem):
        self.place, self.away, self.buf, self.result = place, away, buf, result
        self.got2, self.got3, self.got4, self.got5 = got2, got3, got4, got5
        self.sends, self.recvs = sends, recvs
        rows = buf.shape[4]
        self.low, self.high = pl.ds(0, rows // 2), pl.ds(rows // 2, rows // 2)
        self.keep = pltpu.make_async_copy(
            buf.at[place.t, :, place.y, place.x], result.at[:, place.j], own_sem
        )
        self.spread = spread_slices(
            place,
            result,
            None,
            sends.at[pl.ds(11, 8)],
            recvs.at[pl.ds(11, 8)],
            own=buf.at[place.t, :, place.y, place.x],
        )

    def core(self, a):
        return remote(self.away.at[a], self.buf.at[a], self.sends.at[a], self.recvs.at[a], self.place.device(CORE))

    def copy(self, n):
        p, buf = self.place, self.buf
        x, y, low, high = p.x, p.y, self.low, self.high
        src, dst, device = (
            lambda: (buf.at[:, :, :, 1 - x, low], self.got2.at[0], p.device(X)),
            lambda: (buf.at[:, :, 1 - y, :, high], self.got2.at[1], p.device(Y)),
            lambda: (buf.at[:, :, 1 - y, x, low], self.got3.at[0], p.device(Y)),
            lambda: (buf.at[:, :, y, 1 - x, high], self.got3.at[1], p.device(X)),
            lambda: (buf.at[p.shard(1), :, y, x], self.got4.at[0], p.device(0, 1)),
            lambda: (buf.at[p.shard(3), :, y, x], self.got4.at[1], p.device(0, 1)),
            lambda: (buf.at[p.shard(2), :, y, x], self.got5, p.device(0, 2)),
        )[n]()
        return remote(src, dst, self.sends.at[4 + n], self.recvs.at[4 + n], device)

    def took(self, n):
        self.copy(n).wait_recv()
        self.copy(n).wait_send()

    def add(self, index, extra):
        self.buf[index] = (self.buf[index].astype(F32) + extra.astype(F32)).astype(BF16)

    def one(self):
        for a in range(4):
            self.core(a).wait_send()
        self.copy(0).start()
        self.copy(1).start()

    def two(self):
        p = self.place
        self.took(0)
        for a in range(4):
            for b in range(2):
                self.add((a, 0, b, p.x, self.low), self.got2[0, a, 0, b])
        self.copy(2).start()
        self.took(1)
        for a in range(4):
            for b in range(2):
                self.add((a, 0, p.y, b, self.high), self.got2[1, a, 0, b])
        self.copy(3).start()

    def three(self):
        p = self.place
        for n, part in ((0, self.low), (1, self.high)):
            self.took(2 + n)
            for a in range(4):
                self.add((a, 0, p.y, p.x, part), self.got3[n, a, 0])
        self.copy(4).start()
        self.copy(5).start()

    def four(self):
        p = self.place
        for n, shard in ((0, p.t), (1, p.shard(2))):
            self.took(4 + n)
            self.add((shard, 0, p.y, p.x), self.got4[n, 0])
        self.copy(6).start()

    def five(self):
        p = self.place
        self.took(6)
        self.add((p.t, 0, p.y, p.x), self.got5[0])
        self.keep.start()
        self.spread[0]()

    def stages(self):
        return [self.two, self.three, self.four, self.five] + self.spread[1:] + [self.keep.wait]


def attend_back(a, cap, qkv, dh):
    rows, cols = qkv.shape[2], qkv.shape[3]
    pairs = cols // WIDE
    scale = HEAD_DIM ** (-0.5)

    def step(i, carry):
        seq, pair = lax.div(i, jnp.int32(pairs)), lax.rem(i, jnp.int32(pairs))
        rs = pl.ds(pl.multiple_of(seq * cap, cap), cap)
        cs = pl.ds(pl.multiple_of(pair * WIDE, WIDE), WIDE)
        q, k, v, g = qkv[a, 0, rs, cs], qkv[a, 1, rs, cs], qkv[a, 2, rs, cs], dh[a, rs, cs]
        first = lax.broadcasted_iota(jnp.int32, (cap, WIDE), 1) < HEAD_DIM
        causal = lax.broadcasted_iota(jnp.int32, (cap, cap), 0) >= lax.broadcasted_iota(jnp.int32, (cap, cap), 1)
        dq = dk = dv = None
        for mine in (first, jnp.logical_not(first)):
            zero = jnp.zeros_like(q)
            qh, kh, gh = jnp.where(mine, q, zero), jnp.where(mine, k, zero), jnp.where(mine, g, zero)
            scores = jnp.where(causal, dot_nt(qh, k) * scale, -1e30)
            exps = jnp.exp(scores - jnp.max(scores, axis=1, keepdims=True))
            probs = exps / jnp.sum(exps, axis=1, keepdims=True)
            d_probs = dot_nt(gh, v)
            lean = jnp.sum(probs * d_probs, axis=1, keepdims=True)
            d_scores = (probs * (d_probs - lean)).astype(BF16)
            parts = (dot(d_scores, kh), dot_tn(d_scores, qh), dot_tn(probs.astype(BF16), gh))
            dq, dk, dv = parts if dq is None else (dq + parts[0], dk + parts[1], dv + parts[2])
        qkv[a, 0, rs, cs] = (dq * scale).astype(BF16)
        qkv[a, 1, rs, cs] = (dk * scale).astype(BF16)
        qkv[a, 2, rs, cs] = dv.astype(BF16)
        return carry

    lax.fori_loop(0, rows // cap * pairs, step, 0)


def backward_kernel(cap, *refs):
    out_rows, vector = refs[0:2]
    saved = refs[2:11]
    weights = refs[11:15]
    got_out, got_in, small = refs[15:18]
    results = refs[18:22]
    pk, gr, n1, qkv, ho, at, hid, gp, stats = refs[22:31]
    vec, slots, dm, dn, n2, pre, spare, own_out = refs[31:39]
    bufs, got2, got3, got4, got5 = refs[39:43], refs[43:47], refs[47:51], refs[51:55], refs[55:59]
    sums, heard, pieces = refs[59:62]
    sends, recvs, row_send, row_recv, in_sem, slot_sem, keep_sem, s_send, s_recv = refs[62:]
    place = Place()
    rows, width = dm.shape
    cols = pk.shape[2]
    c, t = place.c, place.t
    loads = [
        pltpu.make_async_copy(src, dst, in_sem.at[i])
        for i, (src, dst) in enumerate(zip(saved[:9], [stats, gr, hid, gp, pk, at, ho, qkv, n1]))
    ]
    loads.append(pltpu.make_async_copy(out_rows.at[t], got_out.at[t], in_sem.at[9]))
    loads.append(pltpu.make_async_copy(vector, vec, in_sem.at[10]))
    for copy in loads:
        copy.start()
    wq, wo, wu, wd = weights

    def slot_copies(i):
        slot = slots.at[i % 2]
        if i < 8:
            src = (wd if i < 4 else wu).at[i % 4]
            return [pltpu.make_async_copy(src, slot, slot_sem.at[i % 2, 0])]
        if i == 8:
            return [pltpu.make_async_copy(wo, slot, slot_sem.at[0, 0])]
        return [
            pltpu.make_async_copy(
                wq.at[i - 9, k], slot.at[:, pl.ds(k * cols, cols)], slot_sem.at[i % 2, k]
            )
            for k in range(3)
        ]

    def slot_start(i):
        if i < 13:
            for copy in slot_copies(i):
                copy.start()

    def slot_ready(i):
        for copy in slot_copies(i):
            copy.wait()

    slot_start(0)
    slot_start(1)
    place.greet()
    rows_one = exchange_rows(place, out_rows, got_out, row_send.at[0], row_recv.at[0])
    rows_two = exchange_rows(place, pk, got_in, row_send.at[1], row_recv.at[1])
    rows_one[0]()

    aways = [
        spare.at[:, :, :, :, :, pl.ds(0, 3 * cols)],
        spare.at[:, :, :, :, pl.ds(0, bufs[1].shape[4]), :],
        hid,
        spare,
    ]
    chain = [
        Sum(
            place, aways[w], bufs[w], got2[w], got3[w], got4[w], got5[w], results[w], sends.at[w], recvs.at[w], keep_sem.at[w]
        )
        for w in range(4)
    ]
    q, o, u, d = chain
    for i in (0, 1):
        loads[i].wait()

    def d_update(rs):
        dm[rs, :] = (stats[rs, 1:2] * joined(gr, rs)).astype(BF16)

    chunks(rows, 64, d_update)
    loads[2].wait()

    def send_half(one, a, left, right, total):
        def put(cs, value):
            size = value.shape[1]
            one.away[a, 0, :, :, :, cs] = value.astype(BF16).reshape(2, 2, -1, size)

        outer(left, right, total, put, block=256 if total % 512 else 512)
        one.core(a).start()

    def keep_half(one, a, left, right, total):
        one.core(a).wait_recv()

        def put(cs, value):
            size = value.shape[1]
            mine = one.buf[a, 0, :, :, :, cs].astype(F32).reshape(-1, size)
            one.buf[a, 0, :, :, :, cs] = (mine + value).astype(BF16).reshape(2, 2, -1, size)

        outer(left, right, total, put, block=256 if total % 512 else 512)

    def hid_half(a, parity):
        return half_blocks(lambda ls: hid[a, 0, :, :, :, ls].reshape(rows, WIDE), 8, parity)

    for a in range(4):
        send_half(d, a, hid_half(a, 1 - c), lambda cs: dm[:, cs], width)
    loads[3].wait()
    for a in range(4):
        slot_ready(a)

        def d_hidden(i, carry, a=a):
            cs = pl.ds(pl.multiple_of(i * 256, 256), 256)
            pre[...] = dot_nt(dm[...], slots[a % 2, cs, :])

            def bend(rs):
                gp[a, rs, cs] = (pre[rs, :] * gp[a, rs, cs].astype(F32)).astype(BF16)

            chunks(rows, 64, bend)
            return carry

        lax.fori_loop(0, gp.shape[2] // 256, d_hidden, 0)
        slot_start(a + 2)
    for a in range(4):
        keep_half(d, a, hid_half(a, c), lambda cs: dm[:, cs], width)
    d.one()
    loads[4].wait()
    loads[5].wait()
    loads[10].wait()

    def norm_two(rs):
        at[rs, :] += joined(pk, rs)
        n2[rs, :] = (at[rs, :] * stats[rs, 2:3] * vec[1:2, :]).astype(BF16)

    chunks(rows, 64, norm_two)
    left = half_blocks(lambda ls: n2[:, ls], 8, 1 - c)
    for a in range(4):
        send_half(u, a, left, lambda cs, a=a: gp[a, :, cs], gp.shape[2])
    for a in range(4):
        slot_ready(4 + a)

        def d_normed(i, carry, a=a):
            cs = pl.ds(pl.multiple_of(i * 256, 256), 256)
            part = dot_nt(gp[a], slots[a % 2, cs, :])
            if a == 0:
                dn[:, cs] = part
            else:
                dn[:, cs] += part
            return carry

        lax.fori_loop(0, width // 256, d_normed, 0)
        slot_start(a + 6)
    left = half_blocks(lambda ls: n2[:, ls], 8, c)
    for a in range(4):
        keep_half(u, a, left, lambda cs, a=a: gp[a, :, cs], gp.shape[2])
    u.one()

    sums[0] = jnp.zeros_like(sums[0])

    def norm_two_back(rs):
        mid, inv, grad = at[rs, :], stats[rs, 2:3], dn[rs, :]
        sums[0, 1:2, :] += jnp.sum(grad * mid * inv, axis=0, keepdims=True)
        grad = grad * vec[1:2, :]
        lean = jnp.sum(grad * mid, axis=1, keepdims=True)
        d_mid = inv * grad - mid * (inv * inv * inv * lean / width)
        at[rs, :] = d_mid
        dm[rs, :] = (stats[rs, 1:2] * joined(gr, rs) + d_mid).astype(BF16)

    chunks(rows, 64, norm_two_back)

    loads[6].wait()
    slot_ready(8)
    unit = bufs[1].shape[4]
    for a in range(4):
        turned = jnp.transpose(ho[a])

        def grad_out(i, carry, a=a, turned=turned):
            cs = pl.ds(pl.multiple_of(i * 256, 256), 256)
            pre[pl.ds(0, cols), :] = dot(turned, dm[:, cs])
            for b in range(4):
                away = pl.ds(pl.multiple_of((2 * b + 1 - c) * unit, unit), unit)
                mine = pl.ds(pl.multiple_of((2 * b + c) * unit, unit), unit)
                o.away[a, 0, b // 2, b % 2, :, cs] = pre[away, :].astype(BF16)
                own_out[a, 0, b // 2, b % 2, :, cs] = pre[mine, :].astype(BF16)
            return carry

        lax.fori_loop(0, width // 256, grad_out, 0)
        o.core(a).start()
        ho[a] = dot_nt(dm[...], slots[0, pl.ds(a * cols, cols), :]).astype(BF16)
    slot_start(10)
    d.two()
    for a in range(4):
        o.core(a).wait_recv()
        for b in range(4):
            o.add((a, 0, b // 2, b % 2), own_out[a, 0, b // 2, b % 2])
    o.one()
    loads[7].wait()
    for a in range(4):
        attend_back(a, cap, qkv, ho)
    loads[8].wait()

    def proj(a):
        return lambda cs: qkv[a, lax.div(cs.start, jnp.int32(cols))]

    left = half_blocks(lambda ls: n1[:, ls], 8, 1 - c)
    for a in range(4):
        send_half(q, a, left, proj(a), 3 * cols)
    for a in range(4):
        slot_ready(9 + a)

        def d_normed(i, carry, a=a):
            cs = pl.ds(pl.multiple_of(i * 256, 256), 256)
            part = dot_nt(qkv[a, 0], slots[(9 + a) % 2, cs, pl.ds(0, cols)])
            for k in (1, 2):
                part += dot_nt(qkv[a, k], slots[(9 + a) % 2, cs, pl.ds(k * cols, cols)])
            if a == 0:
                dn[:, cs] = part
            else:
                dn[:, cs] += part
            return carry

        lax.fori_loop(0, width // 256, d_normed, 0)
        slot_start(a + 11)
    left = half_blocks(lambda ls: n1[:, ls], 8, c)
    for a in range(4):
        keep_half(q, a, left, proj(a), 3 * cols)
    q.one()

    def norm_one_back(rs):
        x, grows, grad = joined(pk, rs), joined(gr, rs), dn[rs, :]
        inv, d_logit = stats[rs, 0:1], stats[rs, 3:4]
        sums[0, 0:1, :] += jnp.sum(grad * x * inv, axis=0, keepdims=True)
        sums[0, 2:3, :] += jnp.sum(d_logit * x, axis=0, keepdims=True)
        grad = grad * vec[0:1, :]
        lean = jnp.sum(grad * x, axis=1, keepdims=True)
        result = grows + at[rs, :] + inv * grad - x * (inv * inv * inv * lean / width) + d_logit * vec[2:3, :]
        for a in range(4):
            pk[a, rs, :] = result[:, a * cols : (a + 1) * cols].astype(BF16)

    chunks(rows, 64, norm_one_back)
    rows_two[0]()
    own_in = pltpu.make_async_copy(pk.at[t], got_in.at[t], in_sem.at[11])
    own_in.start()

    def step(n):
        bit = (CORE, X, Y)[n]
        return remote(sums.at[n], heard.at[n], s_send.at[n], s_recv.at[n], place.device(bit))

    def piece(r):
        lanes = pl.ds(pl.multiple_of(place.shard(r) * cols, cols), cols)
        return remote(sums.at[3, :, lanes], pieces.at[r - 1], s_send.at[2 + r], s_recv.at[2 + r], place.device(0, r))

    def after(tick):
        if tick < 3:
            if tick == 0:
                step(0).start()
            else:
                step(tick - 1).wait_recv()
                sums[tick] = sums[tick - 1] + heard[tick - 1]
                step(tick).start()
        if tick == 3:
            step(2).wait_recv()
            sums[3] = sums[2] + heard[2]
            for r in (1, 2, 3):
                piece(r).start()
        if tick == 4:
            for r in (1, 2, 3):
                piece(r).wait_recv()
            lanes = pl.ds(pl.multiple_of(t * cols, cols), cols)
            vec[:, pl.ds(0, cols)] = sums[3, :, lanes] + pieces[0] + pieces[1] + pieces[2]
            out_small.start()

    out_small = pltpu.make_async_copy(vec.at[:, pl.ds(0, cols)], small, in_sem.at[12])
    pipelined([d.stages()[1:], u.stages(), o.stages(), q.stages()], after)
    for n in range(3):
        step(n).wait_send()
    for r in (1, 2, 3):
        piece(r).wait_send()
    rows_one[1]()
    rows_two[1]()
    loads[9].wait()
    own_in.wait()
    out_small.wait()


def backward(cap, out_rows, vector, saved, weights):
    _, rows, cols = out_rows.shape
    width = 4 * cols
    inner = weights[3].shape[1]
    slices = [(128, 3 * cols), (cols // GROUP, width), (width // GROUP, inner), (inner // GROUP, width)]
    dma = pltpu.SemaphoreType.DMA
    vmem = pltpu.VMEM
    scratch = [
        vmem((4, rows, cols), BF16),
        vmem((4, rows, cols), BF16),
        vmem((rows, width), BF16),
        vmem((4, 3, rows, cols), BF16),
        vmem((4, rows, cols), BF16),
        vmem((rows, width), F32),
        vmem((4, 1, 2, 2, rows // 4, inner), BF16),
        vmem((4, rows, inner), BF16),
        vmem((rows, WIDE), F32),
        vmem((8, width), F32),
        vmem((2, width, width), BF16),
        vmem((rows, width), BF16),
        vmem((rows, width), F32),
        vmem((rows, width), BF16),
        vmem((rows, 256), F32),
        vmem((4, 1, 2, 2, 128, width), BF16),
        vmem((4, 1, 2, 2) + slices[1], BF16),
    ]
    scratch += [vmem((4, 1, 2, 2) + s, BF16) for s in slices]
    scratch += [vmem((2, 4, 1, 2, s[0] // 2, s[1]), BF16) for s in slices]
    scratch += [vmem((2, 4, 1, s[0] // 2, s[1]), BF16) for s in slices]
    scratch += [vmem((2, 1) + s, BF16) for s in slices]
    scratch += [vmem((1,) + s, BF16) for s in slices]
    scratch += [
        vmem((4, 8, width), F32),
        vmem((3, 8, width), F32),
        vmem((3, 8, cols), F32),
        dma((4, 19)),
        dma((4, 19)),
        dma((2, 3)),
        dma((2, 3)),
        dma((13,)),
        dma((2, 3)),
        dma((4,)),
        dma((6,)),
        dma((6,)),
    ]
    return pl.pallas_call(
        functools.partial(backward_kernel, cap),
        in_specs=[ANY] * (2 + len(saved) + 4),
        out_specs=[ANY] * 7,
        out_shape=[jax.ShapeDtypeStruct(out_rows.shape, BF16)] * 2
        + [jax.ShapeDtypeStruct((8, cols), F32)]
        + [jax.ShapeDtypeStruct((1, 8) + s, BF16) for s in slices],
        scratch_shapes=scratch,
        compiler_params=pltpu.CompilerParams(
            collective_id=2, has_side_effects=True, vmem_limit_bytes=62 * 1024 * 1024
        ),
        name="backward",
    )(out_rows, vector, *saved, *weights)


def body(all_dp, n_t, block_input, routes, out_grad, w_qkv, w_out, w_up, w_down, gain_attn, gain_mlp, w_router):
    seqs, length, cols = block_input.shape
    cap = routes.shape[1]
    width = cols * n_t
    own = seqs // n_t
    rows = own * cap
    heads = cols // HEAD_DIM
    outer_bits = [1 << i for i in range(3, all_dp.bit_length() - 1)]

    def send(value, mask_dp, mask_t):
        pairs = [
            (d * n_t + s, (d ^ mask_dp) * n_t + (s ^ mask_t)) for d in range(all_dp) for s in range(n_t)
        ]
        return lax.ppermute(value, ("dp", "tensor"), pairs)

    vector = jnp.concatenate([gain_attn[None], gain_mlp[None], w_router[None], jnp.zeros((5, cols), F32)])
    local = [
        w_qkv.transpose(1, 0, 2).reshape(3, GROUP, width // GROUP, cols),
        w_out.reshape(1, GROUP, cols // GROUP, width),
        w_up.reshape(1, GROUP, width // GROUP, w_up.shape[1]),
        w_down.reshape(1, GROUP, w_down.shape[0] // GROUP, width),
    ]
    picked_all = gather_rows(routes, block_input).reshape(n_t, rows, cols)
    grad_all = gather_rows(routes, out_grad).reshape(n_t, rows, cols)
    wq, wo, wu, wd, picked, grad_rows, normed_one, qkv, head_out, attn_out, hidden, bend, out_rows, stats, vectors = forward(
        cap, picked_all, grad_all, vector, local
    )
    vectors = vectors.transpose(1, 0, 2).reshape(8, width)
    got_out, got_in, sums, s_qkv, s_out, s_up, s_down = backward(
        cap,
        out_rows,
        vectors,
        [
            stats,
            grad_rows,
            hidden.reshape(n_t, 1, 2, 2, rows // 4, -1),
            bend,
            picked,
            attn_out,
            head_out,
            qkv,
            normed_one,
        ],
        [
            wq.reshape(n_t, 3, width, cols),
            wo.reshape(n_t * cols, width),
            wu.reshape(n_t, width, -1),
            wd.reshape(n_t, -1, width),
        ],
    )
    layer_out = scatter_rows(routes, block_input, got_out.reshape(seqs, cap, cols))
    input_grad = scatter_rows(routes, out_grad, got_in.reshape(seqs, cap, cols))
    for bit in outer_bits:
        sums = sums + send(sums, bit, 0)

    def settle(value, shape):
        value = value.reshape(shape).astype(F32)
        for bit in outer_bits:
            value = value + send(value, bit, 0)
        return value

    g_qkv = settle(s_qkv, (width, 3, cols))
    g_out = settle(s_out, w_out.shape)
    g_up = settle(s_up, w_up.shape)
    g_down = settle(s_down, w_down.shape)
    return (layer_out, input_grad, g_qkv, g_out, g_up, g_down, sums[0], sums[1], sums[2])


def solution(mesh):
    placed = (
        P("dp", None, "tensor"),
        P("dp", None),
        P("dp", None, "tensor"),
        P(None, None, "tensor"),
        P("tensor", None),
        P(None, "tensor"),
        P("tensor", None),
        P("tensor"),
        P("tensor"),
        P("tensor"),
    )
    return jax.shard_map(
        functools.partial(body, mesh.shape["dp"], mesh.shape["tensor"]),
        mesh=mesh,
        in_specs=placed,
        out_specs=(
            P("dp", None, "tensor"),
            P("dp", None, "tensor"),
            P(None, None, "tensor"),
            P("tensor", None),
            P(None, "tensor"),
            P("tensor", None),
            P("tensor"),
            P("tensor"),
            P("tensor"),
        ),
        check_vma=False,
    )
```

```python
import functools

import jax
import jax.numpy as jnp
from jax import lax
from jax.experimental import pallas as pl
from jax.experimental.pallas import tpu as pltpu
from jax.sharding import PartitionSpec as P

HEAD_DIM = 64
EPS = 1e-06
F32 = jnp.float32
BF16 = jnp.bfloat16


def exact_gelu(values):
    return jax.nn.gelu(values, approximate=False)


def write_kernel(routes_ref, *refs):
    blocks, rows, sums, outs = refs[0:2], refs[2:4], refs[4:8], refs[8:14]
    length, cols = blocks[0].shape[1:]
    cap = routes_ref.shape[2]
    places = lax.broadcasted_iota(jnp.int32, (length, cap), 0)
    chosen = (routes_ref[0] == places).astype(BF16)
    values = jnp.concatenate([rows[0][0], rows[1][0], jnp.ones((cap, WIDE), BF16)], axis=1)
    spread = jnp.dot(chosen, values, preferred_element_type=F32)
    hit = spread[:, 2 * cols :] > 0.5
    for i in range(2):
        for part in range(cols // WIDE):
            lanes = pl.ds(part * WIDE, WIDE)
            new = spread[:, i * cols + part * WIDE : i * cols + (part + 1) * WIDE]
            old = blocks[i][0, :, lanes].astype(F32)
            outs[i][0, :, lanes] = jnp.where(hit, new, old).astype(BF16)
    for k in range(3):
        outs[2][k] = sums[0][:, k * cols : (k + 1) * cols].astype(F32)
    for i in range(1, 4):
        outs[2 + i][...] = sums[i][...].astype(F32)


def write_results(routes, blocks, rows, sums):
    seqs, length, cols = blocks[0].shape
    cap = routes.shape[1]
    cut = [(s.shape[0] // seqs, s.shape[1]) for s in sums]
    block = pl.BlockSpec((1, length, cols), lambda s: (s, 0, 0))
    flat = [pl.BlockSpec(c, lambda s: (s, 0)) for c in cut]
    return pl.pallas_call(
        write_kernel,
        grid=(seqs,),
        in_specs=[pl.BlockSpec((1, 1, cap), lambda s: (s, 0, 0))]
        + [block] * 2
        + [pl.BlockSpec((1, cap, cols), lambda s: (s, 0, 0))] * 2
        + flat,
        out_specs=[block] * 2 + [pl.BlockSpec((3, cut[0][0], cols), lambda s: (0, s, 0))] + flat[1:],
        out_shape=[jax.ShapeDtypeStruct(b.shape, BF16) for b in blocks]
        + [jax.ShapeDtypeStruct((3, sums[0].shape[0], cols), F32)]
        + [jax.ShapeDtypeStruct(s.shape, F32) for s in sums[1:]],
        compiler_params=pltpu.CompilerParams(vmem_limit_bytes=60 * 1024 * 1024),
        name="write_results",
    )(routes[:, None, :], *blocks, *rows, *sums)


WIDE = 128
MESH = pl.DeviceIdType.MESH
GROUP = 8


def flip(value, bit):
    return value + bit - 2 * bit * lax.rem(lax.div(value, jnp.int32(bit)), jnp.int32(2))


class Place:
    def __init__(self):
        self.dp = lax.axis_index("dp").astype(jnp.int32)
        self.t = lax.axis_index("tensor").astype(jnp.int32)
        self.j = lax.rem(self.dp, jnp.int32(GROUP))
        self.c = lax.rem(self.j, jnp.int32(2))
        self.x = lax.rem(lax.div(self.j, jnp.int32(2)), jnp.int32(2))
        self.y = lax.div(self.j, jnp.int32(4))

    def slot(self, mask):
        value = self.j
        for bit in (1, 2, 4):
            if mask & bit:
                value = flip(value, bit)
        return value

    def shard(self, r):
        value = self.t
        for bit in (1, 2):
            if r & bit:
                value = flip(value, bit)
        return value

    def device(self, mask=0, r=0):
        value = self.dp
        for bit in (1, 2, 4):
            if mask & bit:
                value = flip(value, bit)
        return (value, self.shard(r))

    def greet(self):
        barrier = pltpu.get_barrier_semaphore()
        partners = [(mask, 0) for mask in (1, 2, 4)] + [(0, r) for r in (1, 2, 3)]
        for mask, r in partners:
            pl.semaphore_signal(barrier, inc=1, device_id=self.device(mask, r), device_id_type=MESH)
        pl.semaphore_wait(barrier, len(partners))


def remote(src, dst, send_sem, recv_sem, device):
    return pltpu.make_async_remote_copy(
        src_ref=src, dst_ref=dst, send_sem=send_sem, recv_sem=recv_sem, device_id=device, device_id_type=MESH
    )


CORE, X, Y = 1, 2, 4


def spread_slices(place, full, r, sends, recvs, own=None):
    def block(mask, part=None):
        ref = full.at[place.shard(r)] if r is not None else full
        ref = ref.at[:, place.slot(mask)]
        if part is None:
            return ref
        half = ref.shape[1] // 2
        return ref.at[:, pl.ds(part * half, half)]

    def copy(k, mask, to, part=None, src=None):
        return remote(src if src is not None else block(mask, part), block(mask, part), sends.at[k], recvs.at[k], place.device(to))

    def landed(k, mask, part=None):
        remote(block(mask, part), block(mask, part), sends.at[k], recvs.at[k], place.device(CORE)).wait_recv()

    plan = [
        (0, 0, X, None),
        (1, 0, Y, None),
        (2, 0, CORE, None),
        (3, X, Y, 0),
        (4, Y, X, 1),
        (5, X, CORE, None),
        (6, Y, CORE, None),
        (7, X | Y, CORE, None),
    ]

    def begin():
        for k in (0, 1, 2):
            _, mask, to, part = plan[k]
            copy(k, mask, to, part, own).start()

    def forward():
        landed(0, X)
        copy(*plan[3]).start()
        copy(*plan[5]).start()
        landed(1, Y)
        copy(*plan[4]).start()
        copy(*plan[6]).start()

    def corner():
        landed(3, X | Y, 0)
        landed(4, X | Y, 1)
        copy(*plan[7]).start()

    def finish():
        for k, mask in ((2, CORE), (5, CORE | X), (6, CORE | Y), (7, CORE | X | Y)):
            landed(k, mask)
        for k, mask, to, part in plan:
            copy(k, mask, to, part, own if k < 3 else None).wait_send()

    return [begin, forward, corner, finish]


def pipelined(chains, after=None):
    depth = max(len(chain) for chain in chains)
    for tick in range(len(chains) + depth - 1):
        for i in range(max(0, tick - depth + 1), min(tick, len(chains) - 1) + 1):
            stage = tick - i
            if stage < len(chains[i]):
                chains[i][stage]()
        if after is not None:
            after(tick)


def exchange_rows(place, src, dst, sends, recvs, relative=False):
    def copy(r):
        return remote(src.at[r - 1 if relative else place.shard(r)], dst.at[place.t], sends.at[r - 1], recvs.at[r - 1], place.device(0, r))

    def landed(r):
        ref = dst.at[place.shard(r)]
        return remote(ref, ref, sends.at[r - 1], recvs.at[r - 1], place.device(0, r))

    def begin(order=(2, 3, 1)):
        for r in order:
            copy(r).start()

    def finish():
        for r in (1, 2, 3):
            landed(r).wait_recv()
        for r in (1, 2, 3):
            copy(r).wait_send()

    return begin, finish


ANY = pl.BlockSpec(memory_space=pl.ANY)


def dot(a, b):
    return jnp.dot(a, b, preferred_element_type=F32)


def dot_nt(a, b):
    return lax.dot_general(a, b, (((1,), (1,)), ((), ())), preferred_element_type=F32)


def dot_tn(a, b):
    return lax.dot_general(a, b, (((0,), (0,)), ((), ())), preferred_element_type=F32)


def chunks(total, size, step):
    def one(i, carry):
        step(pl.ds(pl.multiple_of(i * size, size), size))
        return carry

    lax.fori_loop(0, total // size, one, 0)


def joined(ref, rows):
    return jnp.concatenate([ref[a, rows, :].astype(F32) for a in range(4)], axis=1)


def gain(vec, i):
    return jnp.concatenate([vec[a, i : i + 1, :] for a in range(4)], axis=1)


def norm_one(pk, vec, n1, stats):
    gain_one, route_w = gain(vec, 0), gain(vec, 2)
    width = gain_one.shape[1]

    def step(rows):
        x = joined(pk, rows)
        inv = lax.rsqrt(jnp.sum(x * x, axis=1, keepdims=True) / width + EPS)
        n1[rows, :] = (x * inv * gain_one).astype(BF16)
        stats[rows, 0:1] = inv
        stats[rows, 1:2] = jax.nn.sigmoid(jnp.sum(x * route_w, axis=1, keepdims=True))

    chunks(n1.shape[0], 64, step)


def project(a, n1, fq, qkv):
    width = n1.shape[1]

    def step(k, carry):
        weight = fq[a, k].reshape(width, -1)
        qkv[a, k] = dot(n1[...], weight).astype(BF16)
        return carry

    lax.fori_loop(0, 3, step, 0)


def attend(a, cap, qkv, ho):
    rows, cols = qkv.shape[2], qkv.shape[3]
    pairs = cols // WIDE
    scale = HEAD_DIM ** (-0.5)

    def step(i, carry):
        seq, pair = lax.div(i, jnp.int32(pairs)), lax.rem(i, jnp.int32(pairs))
        rs = pl.ds(pl.multiple_of(seq * cap, cap), cap)
        cs = pl.ds(pl.multiple_of(pair * WIDE, WIDE), WIDE)
        q, k, v = qkv[a, 0, rs, cs], qkv[a, 1, rs, cs], qkv[a, 2, rs, cs]
        first = lax.broadcasted_iota(jnp.int32, (cap, WIDE), 1) < HEAD_DIM
        causal = lax.broadcasted_iota(jnp.int32, (cap, cap), 0) >= lax.broadcasted_iota(jnp.int32, (cap, cap), 1)
        outs = []
        for mine in (first, jnp.logical_not(first)):
            scores = dot_nt(jnp.where(mine, q, jnp.zeros_like(q)), k) * scale
            scores = jnp.where(causal, scores, -1e30)
            exps = jnp.exp(scores - jnp.max(scores, axis=1, keepdims=True))
            probs = (exps / jnp.sum(exps, axis=1, keepdims=True)).astype(BF16)
            outs.append(dot(probs, v))
        ho[a, rs, cs] = jnp.where(first, outs[0], outs[1]).astype(BF16)
        return carry

    lax.fori_loop(0, rows // cap * pairs, step, 0)


def attend_out(pk, vec, ho, fo, at, n2, stats):
    gain_two = gain(vec, 1)
    rows, width = n2.shape
    cols = ho.shape[2]

    def product(rs):
        total = dot(ho[0, rs, :], fo[0].reshape(cols, width))
        for a in range(1, 4):
            total += dot(ho[a, rs, :], fo[a].reshape(cols, width))
        at[rs, :] = total

    chunks(rows, 256, product)

    def step(rs):
        mid = joined(pk, rs) + at[rs, :]
        inv = lax.rsqrt(jnp.sum(mid * mid, axis=1, keepdims=True) / width + EPS)
        n2[rs, :] = (mid * inv * gain_two).astype(BF16)
        stats[rs, 2:3] = inv

    chunks(rows, 64, step)


def raise_up(a, n2, fu, hid, gp, pre):
    rows, width = n2.shape
    inner = hid.shape[2]
    block = pre.shape[1]

    def step(i, carry):
        cs = pl.ds(pl.multiple_of(i * block, block), block)
        weight = fu[a, 0, :, :, cs].reshape(width, block)
        pre[...] = dot(n2[...], weight)

        def bend(rs):
            x = pre[rs, :]
            cdf = 0.5 * (1.0 + lax.erf(x * (2.0**-0.5)))
            hid[a, rs, cs] = (x * cdf).astype(BF16)
            gp[a, rs, cs] = (cdf + x * jnp.exp(-0.5 * x * x) * 0.3989422804014327).astype(BF16)

        chunks(rows, 64, bend)
        return carry

    lax.fori_loop(0, inner // block, step, 0)


def bring_down(a, hid, fd, acc, start):
    inner, width = hid.shape[2], acc.shape[1]
    block = 256

    def step(i, carry):
        cs = pl.ds(pl.multiple_of(i * block, block), block)
        part = dot(hid[a], fd[a, 0, :, :, cs].reshape(inner, block))
        if start:
            acc[:, cs] = part
        else:
            acc[:, cs] += part
        return carry

    lax.fori_loop(0, width // block, step, 0)


def finish_rows(pk, gr, at, acc, rows_out, stats):
    cols = pk.shape[2]

    def step(rs):
        update = at[rs, :] + acc[rs, :]
        router = stats[rs, 1:2]
        result = joined(pk, rs) + router * update
        for a in range(4):
            rows_out[a, rs, :] = result[:, a * cols : (a + 1) * cols].astype(BF16)
        lean = jnp.sum(joined(gr, rs) * update, axis=1, keepdims=True)
        stats[rs, 3:4] = lean * router * (1.0 - router)

    chunks(acc.shape[0], 64, step)


def forward_kernel(cap, *refs):
    whole, routes, vector = refs[0:2], refs[2], refs[3]
    local = refs[4:8]
    outs = refs[8:23]
    fulls = refs[23:27]
    pk, gr, vec, n1, qkv, ho, at, n2, hid, gp, acc, rows_out, stats, pre, staged, found, spots = refs[27:44]
    z_send, z_recv, p_send, p_recv, row_send, row_recv, own_sem, out_sem, stage_sem = refs[44:]
    place = Place()
    seqs = routes.shape[0]
    per = seqs // 4

    def stage(n):
        seq = place.shard((2, 1, 3, 0)[n // per]) * per + n % per
        return [
            pltpu.make_async_copy(whole[i].at[seq], staged.at[n % 2, i], stage_sem.at[n % 2, i]) for i in range(2)
        ] + [pltpu.make_async_copy(routes.at[pl.ds(seq, 1)], spots.at[n % 2], stage_sem.at[n % 2, 2])]

    for n in (0, 1):
        for copy in stage(n):
            copy.start()
    own = [pltpu.make_async_copy(vector, vec.at[place.t], own_sem.at[2])]
    for w in range(4):
        own.append(pltpu.make_async_copy(local[w], fulls[w].at[place.t], own_sem.at[3 + w]))
    for copy in own:
        copy.start()
    place.greet()

    def z_copy(w, r):
        if r == 3:
            block = fulls[w].at[place.shard(2), :, place.j]
            return remote(block, block, z_send.at[w, 2], z_recv.at[w, 2], place.device(0, 1))
        return remote(
            local[w].at[:, place.j],
            fulls[w].at[place.t, :, place.j],
            z_send.at[w, r - 1],
            z_recv.at[w, r - 1],
            place.device(0, r),
        )

    def z_landed(w, r):
        block = fulls[w].at[place.shard(r), :, place.j]
        remote(block, block, z_send.at[w, r - 1], z_recv.at[w, r - 1], place.device(0, 1)).wait_recv()

    def z_begin(w):
        z_copy(w, 2).start()
        z_copy(w, 1).start()

    def vec_copy(r):
        return remote(vector, vec.at[place.t], row_send.at[2, r - 1], row_recv.at[2, r - 1], place.device(0, r))

    def vec_landed(r):
        dst = vec.at[place.shard(r)]
        return remote(dst, dst, row_send.at[2, r - 1], row_recv.at[2, r - 1], place.device(0, r))

    rows_one = exchange_rows(place, found.at[0], pk, row_send.at[0], row_recv.at[0], True)
    rows_two = exchange_rows(place, found.at[1], gr, row_send.at[1], row_recv.at[1], True)

    def find(n):
        for copy in stage(n):
            copy.wait()
        length = staged.shape[2]
        spot = jnp.transpose(spots[n % 2].astype(F32)).astype(jnp.int32)
        chosen = (spot == lax.broadcasted_iota(jnp.int32, (cap, length), 1)).astype(BF16)
        rs = pl.ds(n % per * cap, cap)
        for i in range(2):
            value = dot(chosen, staged[n % 2, i]).astype(BF16)
            if n // per < 3:
                found[i, (2, 1, 3)[n // per] - 1, rs, :] = value
            else:
                (pk, gr)[i][place.t, rs, :] = value
        if n + 2 < seqs:
            for copy in stage(n + 2):
                copy.start()

    def find_rows():
        for n in range(seqs):
            find(n)
            if n % per == per - 1 and n // per < 3:
                rows_one[0](((2, 1, 3)[n // per],))

    q, o, u, d = 0, 1, 2, 3
    chains = []
    for w in range(4):
        for r in (2, 1, 3):
            stages = spread_slices(place, fulls[w], r, p_send.at[w, r - 1], p_recv.at[w, r - 1])

            def first(w=w, r=r, begin=stages[0]):
                z_landed(w, r)
                if r == 2:
                    z_copy(w, 3).start()
                    if w + 1 < 4:
                        z_begin(w + 1)
                    if w == 3:
                        rows_two[0]()
                begin()

            chains.append([first] + stages[1:])

    saved = [
        pltpu.make_async_copy(src, dst, out_sem.at[i])
        for i, (src, dst) in enumerate(zip(list(fulls) + [pk, gr, n1, qkv, ho, at, hid, gp, rows_out, stats, vec], outs))
    ]

    def read_rows():
        rows_one[1]()
        own[0].wait()
        for r in (1, 2, 3):
            vec_landed(r).wait_recv()
        norm_one(pk, vec, n1, stats)
        saved[4].start()
        saved[6].start()
        saved[14].start()

    def heads_of(r):
        a = place.shard(r)
        project(a, n1, fulls[q], qkv)
        attend(a, cap, qkv, ho)

    def up_of(r):
        raise_up(place.shard(r), n2, fulls[u], hid, gp, pre)

    def down_of(r, start=False):
        bring_down(place.shard(r), hid, fulls[d], acc, start)

    def after(tick):
        if tick == 2:
            read_rows()
            own[1].wait()
            heads_of(0)
        if tick in (3, 4, 5):
            heads_of((2, 1, 3)[tick - 3])
        if tick == 5:
            saved[0].start()
            saved[7].start()
            saved[8].start()
        if tick == 8:
            own[2].wait()
            attend_out(pk, vec, ho, fulls[o], at, n2, stats)
            saved[1].start()
            saved[9].start()
            own[3].wait()
            up_of(0)
        if tick in (9, 10, 11):
            up_of((2, 1, 3)[tick - 9])
        if tick == 11:
            for i in (2, 10, 11):
                saved[i].start()
            own[4].wait()
            down_of(0, True)
        if tick in (12, 13, 14):
            down_of((2, 1, 3)[tick - 12])

    z_begin(0)
    for r in (1, 2, 3):
        vec_copy(r).start()
    find_rows()
    pipelined(chains, after)
    saved[3].start()
    rows_two[1]()
    saved[5].start()
    finish_rows(pk, gr, at, acc, rows_out, stats)
    saved[12].start()
    saved[13].start()
    for w in range(4):
        for r in (1, 2, 3):
            z_copy(w, r).wait_send()
    for r in (1, 2, 3):
        vec_copy(r).wait_send()
    for copy in saved:
        copy.wait()


def forward(whole, routes, vector, local):
    seqs, length, cols = whole[0].shape
    cap = routes.shape[1]
    rows = seqs // 4 * cap
    width = 4 * cols
    inner = local[2].shape[3]
    fulls = [(4,) + w.shape for w in local]
    dma = pltpu.SemaphoreType.DMA
    kept = [
        ((4, rows, cols), BF16),
        ((4, rows, cols), BF16),
        ((rows, width), BF16),
        ((4, 3, rows, cols), BF16),
        ((4, rows, cols), BF16),
        ((rows, width), F32),
        ((4, rows, inner), BF16),
        ((4, rows, inner), BF16),
        ((4, rows, cols), BF16),
        ((rows, WIDE), F32),
        ((4, 8, cols), F32),
    ]
    vmem = pltpu.VMEM
    scratch = [vmem(f, BF16) for f in fulls] + [
        vmem((4, rows, cols), BF16),
        vmem((4, rows, cols), BF16),
        vmem((4, 8, cols), F32),
        vmem((rows, width), BF16),
        vmem((4, 3, rows, cols), BF16),
        vmem((4, rows, cols), BF16),
        vmem((rows, width), F32),
        vmem((rows, width), BF16),
        vmem((4, rows, inner), BF16),
        vmem((4, rows, inner), BF16),
        vmem((rows, width), F32),
        vmem((4, rows, cols), BF16),
        vmem((rows, WIDE), F32),
        vmem((rows, 256), F32),
        vmem((2, 2, length, cols), BF16),
        vmem((2, 3, rows, cols), BF16),
        vmem((2, 1, cap), jnp.int32),
        dma((4, 3)),
        dma((4, 3)),
        dma((4, 3, 8)),
        dma((4, 3, 8)),
        dma((3, 3)),
        dma((3, 3)),
        dma((7,)),
        dma((15,)),
        dma((2, 3)),
    ]
    return pl.pallas_call(
        functools.partial(forward_kernel, cap),
        in_specs=[ANY] * 8,
        out_specs=[ANY] * 15,
        out_shape=[jax.ShapeDtypeStruct(f, BF16) for f in fulls] + [jax.ShapeDtypeStruct(*k) for k in kept],
        scratch_shapes=scratch,
        compiler_params=pltpu.CompilerParams(
            collective_id=1, has_side_effects=True, vmem_limit_bytes=60 * 1024 * 1024
        ),
        name="forward",
    )(*whole, routes, vector, *local)


def half_blocks(ref_cols, count, parity):
    parts = []
    for b in range(count // 2):
        start = pl.multiple_of((2 * b + parity) * WIDE, WIDE)
        parts.append(ref_cols(pl.ds(start, WIDE)))
    return jnp.concatenate(parts, axis=1)


def outer(left, right, width, put, block=512):
    turned = jnp.transpose(left)

    def step(i, carry):
        cs = pl.ds(pl.multiple_of(i * block, block), block)
        put(cs, dot(turned, right(cs)))
        return carry

    lax.fori_loop(0, width // block, step, 0)


class Sum:
    def __init__(self, place, away, buf, got2, got3, got4, got5, result, sends, recvs, own_sem):
        self.place, self.away, self.buf, self.result = place, away, buf, result
        self.freed = False
        self.got2, self.got3, self.got4, self.got5 = got2, got3, got4, got5
        self.sends, self.recvs = sends, recvs
        rows = buf.shape[4]
        self.low, self.high = pl.ds(0, rows // 2), pl.ds(rows // 2, rows // 2)
        self.keep = pltpu.make_async_copy(
            buf.at[place.t, :, place.y, place.x], result.at[:, place.j], own_sem
        )
        self.spread = spread_slices(
            place,
            result,
            None,
            sends.at[pl.ds(23, 8)],
            recvs.at[pl.ds(23, 8)],
            own=buf.at[place.t, :, place.y, place.x],
        )

    def core(self, a):
        return remote(self.away.at[a], self.buf.at[a], self.sends.at[a], self.recvs.at[a], self.place.device(CORE))

    def away_free(self):
        if not self.freed:
            for a in range(4):
                self.core(a).wait_send()
        self.freed = True

    def copy(self, n):
        p, buf, a = self.place, self.buf, n % 4
        x, y, low, high = p.x, p.y, self.low, self.high
        if n >= 16:
            src, dst, r = (
                lambda: (buf.at[p.shard(1), :, y, x], self.got4.at[0], 1),
                lambda: (buf.at[p.shard(3), :, y, x], self.got4.at[1], 1),
                lambda: (buf.at[p.shard(2), :, y, x], self.got5, 2),
            )[n - 16]()
            device = p.device(0, r)
        else:
            src, dst, device = (
                lambda: (buf.at[a, :, :, 1 - x, low], self.got2.at[0, a], p.device(X)),
                lambda: (buf.at[a, :, 1 - y, :, high], self.got2.at[1, a], p.device(Y)),
                lambda: (buf.at[a, :, 1 - y, x, low], self.got3.at[0, a], p.device(Y)),
                lambda: (buf.at[a, :, y, 1 - x, high], self.got3.at[1, a], p.device(X)),
            )[n // 4]()
        return remote(src, dst, self.sends.at[4 + n], self.recvs.at[4 + n], device)

    def took(self, n):
        self.copy(n).wait_recv()
        self.copy(n).wait_send()

    def add(self, index, extra):
        self.buf[index] = (self.buf[index].astype(F32) + extra.astype(F32)).astype(BF16)

    def one(self, a):
        self.copy(a).start()
        self.copy(4 + a).start()

    def two(self):
        p = self.place
        for a in range(4):
            self.took(a)
            for b in range(2):
                self.add((a, 0, b, p.x, self.low), self.got2[0, a, 0, b])
            self.copy(8 + a).start()
            self.took(4 + a)
            for b in range(2):
                self.add((a, 0, p.y, b, self.high), self.got2[1, a, 0, b])
            self.copy(12 + a).start()

    def three(self):
        p = self.place
        for a in range(4):
            for n, part in ((0, self.low), (1, self.high)):
                self.took(8 + 4 * n + a)
                self.add((a, 0, p.y, p.x, part), self.got3[n, a, 0])
        self.copy(16).start()
        self.copy(17).start()

    def four(self):
        p = self.place
        for n, shard in ((0, p.t), (1, p.shard(2))):
            self.took(16 + n)
            self.add((shard, 0, p.y, p.x), self.got4[n, 0])
        self.copy(18).start()

    def five(self):
        p = self.place
        self.away_free()
        self.took(18)
        self.add((p.t, 0, p.y, p.x), self.got5[0])
        self.keep.start()
        self.spread[0]()

    def stages(self):
        return [self.two, self.three, self.four, self.five] + self.spread[1:] + [self.keep.wait]


def attend_back(a, cap, qkv, dh):
    rows, cols = qkv.shape[2], qkv.shape[3]
    pairs = cols // WIDE
    scale = HEAD_DIM ** (-0.5)

    def step(i, carry):
        seq, pair = lax.div(i, jnp.int32(pairs)), lax.rem(i, jnp.int32(pairs))
        rs = pl.ds(pl.multiple_of(seq * cap, cap), cap)
        cs = pl.ds(pl.multiple_of(pair * WIDE, WIDE), WIDE)
        q, k, v, g = qkv[a, 0, rs, cs], qkv[a, 1, rs, cs], qkv[a, 2, rs, cs], dh[a, rs, cs]
        first = lax.broadcasted_iota(jnp.int32, (cap, WIDE), 1) < HEAD_DIM
        causal = lax.broadcasted_iota(jnp.int32, (cap, cap), 0) >= lax.broadcasted_iota(jnp.int32, (cap, cap), 1)
        dq = dk = dv = None
        for mine in (first, jnp.logical_not(first)):
            zero = jnp.zeros_like(q)
            qh, kh, gh = jnp.where(mine, q, zero), jnp.where(mine, k, zero), jnp.where(mine, g, zero)
            scores = jnp.where(causal, dot_nt(qh, k) * scale, -1e30)
            exps = jnp.exp(scores - jnp.max(scores, axis=1, keepdims=True))
            probs = exps / jnp.sum(exps, axis=1, keepdims=True)
            d_probs = dot_nt(gh, v)
            lean = jnp.sum(probs * d_probs, axis=1, keepdims=True)
            d_scores = (probs * (d_probs - lean)).astype(BF16)
            parts = (dot(d_scores, kh), dot_tn(d_scores, qh), dot_tn(probs.astype(BF16), gh))
            dq, dk, dv = parts if dq is None else (dq + parts[0], dk + parts[1], dv + parts[2])
        qkv[a, 0, rs, cs] = (dq * scale).astype(BF16)
        qkv[a, 1, rs, cs] = (dk * scale).astype(BF16)
        qkv[a, 2, rs, cs] = dv.astype(BF16)
        return carry

    lax.fori_loop(0, rows // cap * pairs, step, 0)


def backward_kernel(cap, *refs):
    out_rows, vector = refs[0:2]
    saved = refs[2:11]
    weights = refs[11:15]
    got_out, got_in, small = refs[15:18]
    results = refs[18:22]
    pk, gr, n1, qkv, ho, at, hid, gp, stats = refs[22:31]
    vec, slots, dm, dn, n2, pre, spare, own_out = refs[31:39]
    bufs, got2, got3, got4, got5 = refs[39:43], refs[43:47], refs[47:51], refs[51:55], refs[55:59]
    sums, heard, pieces = refs[59:62]
    sends, recvs, row_send, row_recv, in_sem, slot_sem, keep_sem, s_send, s_recv = refs[62:]
    place = Place()
    rows, width = dm.shape
    cols = pk.shape[2]
    c, t = place.c, place.t
    loads = [
        pltpu.make_async_copy(src, dst, in_sem.at[i])
        for i, (src, dst) in enumerate(zip(saved[:9], [stats, gr, hid, gp, pk, at, ho, qkv, n1]))
    ]
    loads.append(pltpu.make_async_copy(out_rows.at[t], got_out.at[t], in_sem.at[9]))
    loads.append(pltpu.make_async_copy(vector, vec, in_sem.at[10]))
    for copy in loads:
        copy.start()
    wq, wo, wu, wd = weights

    def slot_copies(i):
        slot = slots.at[i % 2]
        if i < 8:
            src = (wd if i < 4 else wu).at[i % 4]
            return [pltpu.make_async_copy(src, slot, slot_sem.at[i % 2, 0])]
        if i == 8:
            return [pltpu.make_async_copy(wo, slot, slot_sem.at[0, 0])]
        return [
            pltpu.make_async_copy(
                wq.at[i - 9, k], slot.at[:, pl.ds(k * cols, cols)], slot_sem.at[i % 2, k]
            )
            for k in range(3)
        ]

    def slot_start(i):
        if i < 13:
            for copy in slot_copies(i):
                copy.start()

    def slot_ready(i):
        for copy in slot_copies(i):
            copy.wait()

    slot_start(0)
    slot_start(1)
    place.greet()
    rows_one = exchange_rows(place, out_rows, got_out, row_send.at[0], row_recv.at[0])
    rows_two = exchange_rows(place, pk, got_in, row_send.at[1], row_recv.at[1])
    rows_one[0]()

    aways = [
        spare.at[:, :, :, :, :, pl.ds(0, 3 * cols)],
        spare.at[:, :, :, :, pl.ds(0, bufs[1].shape[4]), :],
        hid,
        spare,
    ]
    chain = [
        Sum(
            place, aways[w], bufs[w], got2[w], got3[w], got4[w], got5[w], results[w], sends.at[w], recvs.at[w], keep_sem.at[w]
        )
        for w in range(4)
    ]
    q, o, u, d = chain
    for i in (0, 1):
        loads[i].wait()

    def d_update(rs):
        dm[rs, :] = (stats[rs, 1:2] * joined(gr, rs)).astype(BF16)

    chunks(rows, 64, d_update)
    loads[2].wait()

    def send_half(one, a, left, right, total):
        def put(cs, value):
            size = value.shape[1]
            one.away[a, 0, :, :, :, cs] = value.astype(BF16).reshape(2, 2, -1, size)

        outer(left, right, total, put, block=256 if total % 512 else 512)
        one.core(a).start()

    def keep_half(one, a, left, right, total):
        one.core(a).wait_recv()

        def put(cs, value):
            size = value.shape[1]
            mine = one.buf[a, 0, :, :, :, cs].astype(F32).reshape(-1, size)
            one.buf[a, 0, :, :, :, cs] = (mine + value).astype(BF16).reshape(2, 2, -1, size)

        outer(left, right, total, put, block=256 if total % 512 else 512)

    def hid_half(a, parity):
        return half_blocks(lambda ls: hid[a, 0, :, :, :, ls].reshape(rows, WIDE), 8, parity)

    for a in range(4):
        send_half(d, a, hid_half(a, 1 - c), lambda cs: dm[:, cs], width)
    for a in range(4):
        keep_half(d, a, hid_half(a, c), lambda cs: dm[:, cs], width)
        d.one(a)
    loads[3].wait()
    for a in range(4):
        slot_ready(a)

        def d_hidden(i, carry, a=a):
            cs = pl.ds(pl.multiple_of(i * 256, 256), 256)
            pre[...] = dot_nt(dm[...], slots[a % 2, cs, :])

            def bend(rs):
                gp[a, rs, cs] = (pre[rs, :] * gp[a, rs, cs].astype(F32)).astype(BF16)

            chunks(rows, 64, bend)
            return carry

        lax.fori_loop(0, gp.shape[2] // 256, d_hidden, 0)
        slot_start(a + 2)
    loads[4].wait()
    loads[5].wait()
    loads[10].wait()

    def norm_two(rs):
        at[rs, :] += joined(pk, rs)
        n2[rs, :] = (at[rs, :] * stats[rs, 2:3] * vec[1:2, :]).astype(BF16)

    chunks(rows, 64, norm_two)
    left = half_blocks(lambda ls: n2[:, ls], 8, 1 - c)
    for a in range(4):
        send_half(u, a, left, lambda cs, a=a: gp[a, :, cs], gp.shape[2])
    left = half_blocks(lambda ls: n2[:, ls], 8, c)
    for a in range(4):
        keep_half(u, a, left, lambda cs, a=a: gp[a, :, cs], gp.shape[2])
        u.one(a)
    for a in range(4):
        slot_ready(4 + a)

        def d_normed(i, carry, a=a):
            cs = pl.ds(pl.multiple_of(i * 256, 256), 256)
            part = dot_nt(gp[a], slots[a % 2, cs, :])
            if a == 0:
                dn[:, cs] = part
            else:
                dn[:, cs] += part
            return carry

        lax.fori_loop(0, width // 256, d_normed, 0)
        slot_start(a + 6)
        if a == 2:
            d.two()

    sums[0] = jnp.zeros_like(sums[0])

    def norm_two_back(rs):
        mid, inv, grad = at[rs, :], stats[rs, 2:3], dn[rs, :]
        sums[0, 1:2, :] += jnp.sum(grad * mid * inv, axis=0, keepdims=True)
        grad = grad * vec[1:2, :]
        lean = jnp.sum(grad * mid, axis=1, keepdims=True)
        d_mid = inv * grad - mid * (inv * inv * inv * lean / width)
        at[rs, :] = d_mid
        dm[rs, :] = (stats[rs, 1:2] * joined(gr, rs) + d_mid).astype(BF16)

    chunks(rows, 64, norm_two_back)

    d.away_free()
    loads[6].wait()
    slot_ready(8)
    unit = bufs[1].shape[4]
    for a in range(4):
        turned = jnp.transpose(ho[a])

        def grad_out(i, carry, a=a, turned=turned):
            cs = pl.ds(pl.multiple_of(i * 256, 256), 256)
            pre[pl.ds(0, cols), :] = dot(turned, dm[:, cs])
            for b in range(4):
                away = pl.ds(pl.multiple_of((2 * b + 1 - c) * unit, unit), unit)
                mine = pl.ds(pl.multiple_of((2 * b + c) * unit, unit), unit)
                o.away[a, 0, b // 2, b % 2, :, cs] = pre[away, :].astype(BF16)
                own_out[a, 0, b // 2, b % 2, :, cs] = pre[mine, :].astype(BF16)
            return carry

        lax.fori_loop(0, width // 256, grad_out, 0)
        o.core(a).start()
        ho[a] = dot_nt(dm[...], slots[0, pl.ds(a * cols, cols), :]).astype(BF16)
    slot_start(10)
    for a in range(4):
        o.core(a).wait_recv()
        for b in range(4):
            o.add((a, 0, b // 2, b % 2), own_out[a, 0, b // 2, b % 2])
        o.one(a)
    loads[7].wait()
    for a in range(4):
        attend_back(a, cap, qkv, ho)
        if a == 1:
            d.three()
        if a == 2:
            u.two()
    d.four()
    o.away_free()
    loads[8].wait()

    def proj(a):
        return lambda cs: qkv[a, lax.div(cs.start, jnp.int32(cols))]

    for a in range(4):
        slot_ready(9 + a)

        def d_normed(i, carry, a=a):
            cs = pl.ds(pl.multiple_of(i * 256, 256), 256)
            part = dot_nt(qkv[a, 0], slots[(9 + a) % 2, cs, pl.ds(0, cols)])
            for k in (1, 2):
                part += dot_nt(qkv[a, k], slots[(9 + a) % 2, cs, pl.ds(k * cols, cols)])
            if a == 0:
                dn[:, cs] = part
            else:
                dn[:, cs] += part
            return carry

        lax.fori_loop(0, width // 256, d_normed, 0)
        slot_start(a + 11)

    def norm_one_back(rs):
        x, grows, grad = joined(pk, rs), joined(gr, rs), dn[rs, :]
        inv, d_logit = stats[rs, 0:1], stats[rs, 3:4]
        sums[0, 0:1, :] += jnp.sum(grad * x * inv, axis=0, keepdims=True)
        sums[0, 2:3, :] += jnp.sum(d_logit * x, axis=0, keepdims=True)
        grad = grad * vec[0:1, :]
        lean = jnp.sum(grad * x, axis=1, keepdims=True)
        result = grows + at[rs, :] + inv * grad - x * (inv * inv * inv * lean / width) + d_logit * vec[2:3, :]
        for a in range(4):
            pk[a, rs, :] = result[:, a * cols : (a + 1) * cols].astype(BF16)

    chunks(rows, 64, norm_one_back)
    rows_two[0]()
    own_in = pltpu.make_async_copy(pk.at[t], got_in.at[t], in_sem.at[11])
    own_in.start()
    left = half_blocks(lambda ls: n1[:, ls], 8, 1 - c)
    for a in range(4):
        send_half(q, a, left, proj(a), 3 * cols)
    left = half_blocks(lambda ls: n1[:, ls], 8, c)
    for a in range(4):
        keep_half(q, a, left, proj(a), 3 * cols)
        q.one(a)

    def step(n):
        bit = (CORE, X, Y)[n]
        return remote(sums.at[n], heard.at[n], s_send.at[n], s_recv.at[n], place.device(bit))

    def piece(r):
        lanes = pl.ds(pl.multiple_of(place.shard(r) * cols, cols), cols)
        return remote(sums.at[3, :, lanes], pieces.at[r - 1], s_send.at[2 + r], s_recv.at[2 + r], place.device(0, r))

    def after(tick):
        if tick < 3:
            if tick == 0:
                step(0).start()
            else:
                step(tick - 1).wait_recv()
                sums[tick] = sums[tick - 1] + heard[tick - 1]
                step(tick).start()
        if tick == 3:
            step(2).wait_recv()
            sums[3] = sums[2] + heard[2]
            for r in (1, 2, 3):
                piece(r).start()
        if tick == 4:
            for r in (1, 2, 3):
                piece(r).wait_recv()
            lanes = pl.ds(pl.multiple_of(t * cols, cols), cols)
            vec[:, pl.ds(0, cols)] = sums[3, :, lanes] + pieces[0] + pieces[1] + pieces[2]
            out_small.start()

    out_small = pltpu.make_async_copy(vec.at[:, pl.ds(0, cols)], small, in_sem.at[12])
    order = "o0 u1 d3 o1 u2 q0 d4 u3 o2 q1 d5 u4 o3 q2 d6 u5 o4 q3 u6 o5 q4 o6 q5 q6 d7 u7 o7 q7"
    todo = {"d": d.stages(), "u": u.stages(), "o": o.stages(), "q": q.stages()}
    for tick, item in enumerate(order.split()):
        todo[item[0]][int(item[1])]()
        if tick % 2 == 0:
            after(tick // 2)
    for n in range(3):
        step(n).wait_send()
    for r in (1, 2, 3):
        piece(r).wait_send()
    rows_one[1]()
    rows_two[1]()
    loads[9].wait()
    own_in.wait()
    out_small.wait()


def backward(cap, out_rows, vector, saved, weights):
    _, rows, cols = out_rows.shape
    width = 4 * cols
    inner = weights[3].shape[1]
    slices = [(128, 3 * cols), (cols // GROUP, width), (width // GROUP, inner), (inner // GROUP, width)]
    dma = pltpu.SemaphoreType.DMA
    vmem = pltpu.VMEM
    scratch = [
        vmem((4, rows, cols), BF16),
        vmem((4, rows, cols), BF16),
        vmem((rows, width), BF16),
        vmem((4, 3, rows, cols), BF16),
        vmem((4, rows, cols), BF16),
        vmem((rows, width), F32),
        vmem((4, 1, 2, 2, rows // 4, inner), BF16),
        vmem((4, rows, inner), BF16),
        vmem((rows, WIDE), F32),
        vmem((8, width), F32),
        vmem((2, width, width), BF16),
        vmem((rows, width), BF16),
        vmem((rows, width), F32),
        vmem((rows, width), BF16),
        vmem((rows, 256), F32),
        vmem((4, 1, 2, 2, 128, width), BF16),
        vmem((4, 1, 2, 2) + slices[1], BF16),
    ]
    scratch += [vmem((4, 1, 2, 2) + s, BF16) for s in slices]
    scratch += [vmem((2, 4, 1, 2, s[0] // 2, s[1]), BF16) for s in slices]
    scratch += [vmem((2, 4, 1, s[0] // 2, s[1]), BF16) for s in slices]
    scratch += [vmem((2, 1) + s, BF16) for s in slices]
    scratch += [vmem((1,) + s, BF16) for s in slices]
    scratch += [
        vmem((4, 8, width), F32),
        vmem((3, 8, width), F32),
        vmem((3, 8, cols), F32),
        dma((4, 31)),
        dma((4, 31)),
        dma((2, 3)),
        dma((2, 3)),
        dma((13,)),
        dma((2, 3)),
        dma((4,)),
        dma((6,)),
        dma((6,)),
    ]
    return pl.pallas_call(
        functools.partial(backward_kernel, cap),
        in_specs=[ANY] * (2 + len(saved) + 4),
        out_specs=[ANY] * 7,
        out_shape=[jax.ShapeDtypeStruct(out_rows.shape, BF16)] * 2
        + [jax.ShapeDtypeStruct((8, cols), F32)]
        + [jax.ShapeDtypeStruct((1, 8) + s, BF16) for s in slices],
        scratch_shapes=scratch,
        compiler_params=pltpu.CompilerParams(
            collective_id=2, has_side_effects=True, vmem_limit_bytes=62 * 1024 * 1024
        ),
        name="backward",
    )(out_rows, vector, *saved, *weights)


def body(all_dp, n_t, block_input, routes, out_grad, w_qkv, w_out, w_up, w_down, gain_attn, gain_mlp, w_router):
    seqs, length, cols = block_input.shape
    cap = routes.shape[1]
    width = cols * n_t
    own = seqs // n_t
    rows = own * cap
    heads = cols // HEAD_DIM
    outer_bits = [1 << i for i in range(3, all_dp.bit_length() - 1)]

    def send(value, mask_dp, mask_t):
        pairs = [
            (d * n_t + s, (d ^ mask_dp) * n_t + (s ^ mask_t)) for d in range(all_dp) for s in range(n_t)
        ]
        return lax.ppermute(value, ("dp", "tensor"), pairs)

    vector = jnp.concatenate([gain_attn[None], gain_mlp[None], w_router[None], jnp.zeros((5, cols), F32)])
    local = [
        w_qkv.transpose(1, 0, 2).reshape(3, GROUP, width // GROUP, cols),
        w_out.reshape(1, GROUP, cols // GROUP, width),
        w_up.reshape(1, GROUP, width // GROUP, w_up.shape[1]),
        w_down.reshape(1, GROUP, w_down.shape[0] // GROUP, width),
    ]
    wq, wo, wu, wd, picked, grad_rows, normed_one, qkv, head_out, attn_out, hidden, bend, out_rows, stats, vectors = forward(
        [block_input, out_grad], routes, vector, local
    )
    vectors = vectors.transpose(1, 0, 2).reshape(8, width)
    got_out, got_in, sums, s_qkv, s_out, s_up, s_down = backward(
        cap,
        out_rows,
        vectors,
        [
            stats,
            grad_rows,
            hidden.reshape(n_t, 1, 2, 2, rows // 4, -1),
            bend,
            picked,
            attn_out,
            head_out,
            qkv,
            normed_one,
        ],
        [
            wq.reshape(n_t, 3, width, cols),
            wo.reshape(n_t * cols, width),
            wu.reshape(n_t, width, -1),
            wd.reshape(n_t, -1, width),
        ],
    )
    layer_out, input_grad, g_qkv, g_out, g_up, g_down = write_results(
        routes,
        [block_input, out_grad],
        [got_out.reshape(seqs, cap, cols), got_in.reshape(seqs, cap, cols)],
        [
            s_qkv.reshape(width, 3 * cols),
            s_out.reshape(w_out.shape),
            s_up.reshape(w_up.shape),
            s_down.reshape(w_down.shape),
        ],
    )
    for bit in outer_bits:
        sums = sums + send(sums, bit, 0)

    def settle(value):
        for bit in outer_bits:
            value = value + send(value, bit, 0)
        return value

    g_qkv, g_out, g_up, g_down = settle(g_qkv).transpose(1, 0, 2), settle(g_out), settle(g_up), settle(g_down)
    return (layer_out, input_grad, g_qkv, g_out, g_up, g_down, sums[0], sums[1], sums[2])


def solution(mesh):
    placed = (
        P("dp", None, "tensor"),
        P("dp", None),
        P("dp", None, "tensor"),
        P(None, None, "tensor"),
        P("tensor", None),
        P(None, "tensor"),
        P("tensor", None),
        P("tensor"),
        P("tensor"),
        P("tensor"),
    )
    return jax.shard_map(
        functools.partial(body, mesh.shape["dp"], mesh.shape["tensor"]),
        mesh=mesh,
        in_specs=placed,
        out_specs=(
            P("dp", None, "tensor"),
            P("dp", None, "tensor"),
            P(None, None, "tensor"),
            P("tensor", None),
            P(None, "tensor"),
            P("tensor", None),
            P("tensor"),
            P("tensor"),
            P("tensor"),
        ),
        check_vma=False,
    )
```

```python
import functools

import jax
import jax.numpy as jnp
from jax import lax
from jax.experimental import pallas as pl
from jax.experimental.pallas import tpu as pltpu
from jax.sharding import PartitionSpec as P

HEAD_DIM = 64
EPS = 1e-06
F32 = jnp.float32
BF16 = jnp.bfloat16


def exact_gelu(values):
    return jax.nn.gelu(values, approximate=False)


def write_kernel(routes_ref, *refs):
    blocks, rows, sums, outs = refs[0:2], refs[2:4], refs[4:8], refs[8:14]
    length, cols = blocks[0].shape[1:]
    cap = routes_ref.shape[2]
    places = lax.broadcasted_iota(jnp.int32, (length, cap), 0)
    chosen = (routes_ref[0] == places).astype(BF16)
    values = jnp.concatenate([rows[0][0], rows[1][0], jnp.ones((cap, WIDE), BF16)], axis=1)
    spread = jnp.dot(chosen, values, preferred_element_type=F32)
    spread = spread.astype(BF16)
    hit = spread[:, 2 * cols :] > 0.5
    for i in range(2):
        for part in range(cols // WIDE):
            lanes = pl.ds(part * WIDE, WIDE)
            new = spread[:, i * cols + part * WIDE : i * cols + (part + 1) * WIDE]
            outs[i][0, :, lanes] = jnp.where(hit, new, blocks[i][0, :, lanes])
    for k in range(3):
        outs[2][k] = sums[0][:, k * cols : (k + 1) * cols].astype(F32)
    for i in range(1, 4):
        outs[2 + i][...] = sums[i][...].astype(F32)


def write_results(routes, blocks, rows, sums):
    seqs, length, cols = blocks[0].shape
    cap = routes.shape[1]
    cut = [(s.shape[0] // seqs, s.shape[1]) for s in sums]
    block = pl.BlockSpec((1, length, cols), lambda s: (s, 0, 0))
    flat = [pl.BlockSpec(c, lambda s: (s, 0)) for c in cut]
    return pl.pallas_call(
        write_kernel,
        grid=(seqs,),
        in_specs=[pl.BlockSpec((1, 1, cap), lambda s: (s, 0, 0))]
        + [block] * 2
        + [pl.BlockSpec((1, cap, cols), lambda s: (s, 0, 0))] * 2
        + flat,
        out_specs=[block] * 2 + [pl.BlockSpec((3, cut[0][0], cols), lambda s: (0, s, 0))] + flat[1:],
        out_shape=[jax.ShapeDtypeStruct(b.shape, BF16) for b in blocks]
        + [jax.ShapeDtypeStruct((3, sums[0].shape[0], cols), F32)]
        + [jax.ShapeDtypeStruct(s.shape, F32) for s in sums[1:]],
        compiler_params=pltpu.CompilerParams(vmem_limit_bytes=60 * 1024 * 1024),
        name="write_results",
    )(routes[:, None, :], *blocks, *rows, *sums)


WIDE = 128
MESH = pl.DeviceIdType.MESH
GROUP = 8


def flip(value, bit):
    return value + bit - 2 * bit * lax.rem(lax.div(value, jnp.int32(bit)), jnp.int32(2))


class Place:
    def __init__(self):
        self.dp = lax.axis_index("dp").astype(jnp.int32)
        self.t = lax.axis_index("tensor").astype(jnp.int32)
        self.j = lax.rem(self.dp, jnp.int32(GROUP))
        self.c = lax.rem(self.j, jnp.int32(2))
        self.x = lax.rem(lax.div(self.j, jnp.int32(2)), jnp.int32(2))
        self.y = lax.div(self.j, jnp.int32(4))

    def slot(self, mask):
        value = self.j
        for bit in (1, 2, 4):
            if mask & bit:
                value = flip(value, bit)
        return value

    def shard(self, r):
        value = self.t
        for bit in (1, 2):
            if r & bit:
                value = flip(value, bit)
        return value

    def device(self, mask=0, r=0):
        value = self.dp
        for bit in (1, 2, 4):
            if mask & bit:
                value = flip(value, bit)
        return (value, self.shard(r))

    def greet(self):
        barrier = pltpu.get_barrier_semaphore()
        partners = [(mask, 0) for mask in (1, 2, 4)] + [(0, r) for r in (1, 2, 3)]
        for mask, r in partners:
            pl.semaphore_signal(barrier, inc=1, device_id=self.device(mask, r), device_id_type=MESH)
        pl.semaphore_wait(barrier, len(partners))


def remote(src, dst, send_sem, recv_sem, device):
    return pltpu.make_async_remote_copy(
        src_ref=src, dst_ref=dst, send_sem=send_sem, recv_sem=recv_sem, device_id=device, device_id_type=MESH
    )


CORE, X, Y = 1, 2, 4


def spread_slices(place, full, r, sends, recvs, own=None):
    def block(mask, part=None):
        ref = full.at[place.shard(r)] if r is not None else full
        ref = ref.at[:, place.slot(mask)]
        if part is None:
            return ref
        half = ref.shape[1] // 2
        return ref.at[:, pl.ds(part * half, half)]

    def copy(k, mask, to, part=None, src=None):
        return remote(src if src is not None else block(mask, part), block(mask, part), sends.at[k], recvs.at[k], place.device(to))

    def landed(k, mask, part=None):
        remote(block(mask, part), block(mask, part), sends.at[k], recvs.at[k], place.device(CORE)).wait_recv()

    plan = [
        (0, 0, X, None),
        (1, 0, Y, None),
        (2, 0, CORE, None),
        (3, X, Y, 0),
        (4, Y, X, 1),
        (5, X, CORE, None),
        (6, Y, CORE, None),
        (7, X | Y, CORE, None),
    ]

    def begin():
        for k in (0, 1, 2):
            _, mask, to, part = plan[k]
            copy(k, mask, to, part, own).start()

    def forward():
        landed(0, X)
        copy(*plan[3]).start()
        copy(*plan[5]).start()
        landed(1, Y)
        copy(*plan[4]).start()
        copy(*plan[6]).start()

    def corner():
        landed(3, X | Y, 0)
        landed(4, X | Y, 1)
        copy(*plan[7]).start()

    def finish():
        for k, mask in ((2, CORE), (5, CORE | X), (6, CORE | Y), (7, CORE | X | Y)):
            landed(k, mask)
        for k, mask, to, part in plan:
            copy(k, mask, to, part, own if k < 3 else None).wait_send()

    return [begin, forward, corner, finish]


def pipelined(chains, after=None):
    depth = max(len(chain) for chain in chains)
    for tick in range(len(chains) + depth - 1):
        for i in range(max(0, tick - depth + 1), min(tick, len(chains) - 1) + 1):
            stage = tick - i
            if stage < len(chains[i]):
                chains[i][stage]()
        if after is not None:
            after(tick)


def exchange_rows(place, src, dst, sends, recvs, relative=False):
    def copy(r):
        return remote(src.at[r - 1 if relative else place.shard(r)], dst.at[place.t], sends.at[r - 1], recvs.at[r - 1], place.device(0, r))

    def landed(r):
        ref = dst.at[place.shard(r)]
        return remote(ref, ref, sends.at[r - 1], recvs.at[r - 1], place.device(0, r))

    def begin(order=(2, 3, 1)):
        for r in order:
            copy(r).start()

    def finish():
        for r in (1, 2, 3):
            landed(r).wait_recv()
        for r in (1, 2, 3):
            copy(r).wait_send()

    return begin, finish


ANY = pl.BlockSpec(memory_space=pl.ANY)


def dot(a, b):
    return jnp.dot(a, b, preferred_element_type=F32)


def dot_nt(a, b):
    return lax.dot_general(a, b, (((1,), (1,)), ((), ())), preferred_element_type=F32)


def dot_tn(a, b):
    return lax.dot_general(a, b, (((0,), (0,)), ((), ())), preferred_element_type=F32)


def chunks(total, size, step):
    def one(i, carry):
        step(pl.ds(pl.multiple_of(i * size, size), size))
        return carry

    lax.fori_loop(0, total // size, one, 0)


def joined(ref, rows):
    return jnp.concatenate([ref[a, rows, :].astype(F32) for a in range(4)], axis=1)


def gain(vec, i):
    return jnp.concatenate([vec[a, i : i + 1, :] for a in range(4)], axis=1)


def norm_one(pk, vec, n1, stats):
    gain_one, route_w = gain(vec, 0), gain(vec, 2)
    width = gain_one.shape[1]

    def step(rows):
        x = joined(pk, rows)
        inv = lax.rsqrt(jnp.sum(x * x, axis=1, keepdims=True) / width + EPS)
        n1[rows, :] = (x * inv * gain_one).astype(BF16)
        stats[rows, 0:1] = inv
        stats[rows, 1:2] = jax.nn.sigmoid(jnp.sum(x * route_w, axis=1, keepdims=True))

    chunks(n1.shape[0], 64, step)


def project(a, n1, fq, qkv):
    width = n1.shape[1]

    def step(k, carry):
        weight = fq[a, k].reshape(width, -1)
        qkv[a, k] = dot(n1[...], weight).astype(BF16)
        return carry

    lax.fori_loop(0, 3, step, 0)


def attend(a, cap, qkv, ho):
    rows, cols = qkv.shape[2], qkv.shape[3]
    pairs = cols // WIDE
    scale = HEAD_DIM ** (-0.5)

    def step(i, carry):
        seq, pair = lax.div(i, jnp.int32(pairs)), lax.rem(i, jnp.int32(pairs))
        rs = pl.ds(pl.multiple_of(seq * cap, cap), cap)
        cs = pl.ds(pl.multiple_of(pair * WIDE, WIDE), WIDE)
        q, k, v = qkv[a, 0, rs, cs], qkv[a, 1, rs, cs], qkv[a, 2, rs, cs]
        first = lax.broadcasted_iota(jnp.int32, (cap, WIDE), 1) < HEAD_DIM
        causal = lax.broadcasted_iota(jnp.int32, (cap, cap), 0) >= lax.broadcasted_iota(jnp.int32, (cap, cap), 1)
        outs = []
        for mine in (first, jnp.logical_not(first)):
            scores = dot_nt(jnp.where(mine, q, jnp.zeros_like(q)), k) * scale
            scores = jnp.where(causal, scores, -1e30)
            exps = jnp.exp(scores - jnp.max(scores, axis=1, keepdims=True))
            probs = (exps / jnp.sum(exps, axis=1, keepdims=True)).astype(BF16)
            outs.append(dot(probs, v))
        ho[a, rs, cs] = jnp.where(first, outs[0], outs[1]).astype(BF16)
        return carry

    lax.fori_loop(0, rows // cap * pairs, step, 0)


def attend_out(pk, vec, ho, fo, at, n2, stats):
    gain_two = gain(vec, 1)
    rows, width = n2.shape
    cols = ho.shape[2]

    def product(rs):
        total = dot(ho[0, rs, :], fo[0].reshape(cols, width))
        for a in range(1, 4):
            total += dot(ho[a, rs, :], fo[a].reshape(cols, width))
        at[rs, :] = total

    chunks(rows, 256, product)

    def step(rs):
        mid = joined(pk, rs) + at[rs, :]
        inv = lax.rsqrt(jnp.sum(mid * mid, axis=1, keepdims=True) / width + EPS)
        n2[rs, :] = (mid * inv * gain_two).astype(BF16)
        stats[rs, 2:3] = inv

    chunks(rows, 64, step)


def raise_up(a, n2, fu, hid, gp, pre):
    rows, width = n2.shape
    inner = hid.shape[2]
    block = pre.shape[1]

    def step(i, carry):
        cs = pl.ds(pl.multiple_of(i * block, block), block)
        weight = fu[a, 0, :, :, cs].reshape(width, block)
        pre[...] = dot(n2[...], weight)

        def bend(rs):
            x = pre[rs, :]
            cdf = 0.5 * (1.0 + lax.erf(x * (2.0**-0.5)))
            hid[a, rs, cs] = (x * cdf).astype(BF16)
            gp[a, rs, cs] = (cdf + x * jnp.exp(-0.5 * x * x) * 0.3989422804014327).astype(BF16)

        chunks(rows, 64, bend)
        return carry

    lax.fori_loop(0, inner // block, step, 0)


def bring_down(a, hid, fd, acc, start):
    inner, width = hid.shape[2], acc.shape[1]
    block = 256

    def step(i, carry):
        cs = pl.ds(pl.multiple_of(i * block, block), block)
        part = dot(hid[a], fd[a, 0, :, :, cs].reshape(inner, block))
        if start:
            acc[:, cs] = part
        else:
            acc[:, cs] += part
        return carry

    lax.fori_loop(0, width // block, step, 0)


def finish_rows(pk, gr, at, acc, rows_out, stats):
    cols = pk.shape[2]

    def step(rs):
        update = at[rs, :] + acc[rs, :]
        router = stats[rs, 1:2]
        result = joined(pk, rs) + router * update
        for a in range(4):
            rows_out[a, rs, :] = result[:, a * cols : (a + 1) * cols].astype(BF16)
        lean = jnp.sum(joined(gr, rs) * update, axis=1, keepdims=True)
        stats[rs, 3:4] = lean * router * (1.0 - router)

    chunks(acc.shape[0], 64, step)


def forward_kernel(cap, *refs):
    whole, routes, vector = refs[0:2], refs[2], refs[3]
    local = refs[4:8]
    outs = refs[8:23]
    fulls = refs[23:27]
    pk, gr, vec, n1, qkv, ho, at, n2, hid, gp, acc, rows_out, stats, pre, staged, found, spots = refs[27:44]
    z_send, z_recv, p_send, p_recv, row_send, row_recv, own_sem, out_sem, stage_sem = refs[44:]
    place = Place()
    seqs = routes.shape[0]
    per = seqs // 4

    def stage(n):
        seq = place.shard((2, 1, 3, 0)[n // per]) * per + n % per
        return [
            pltpu.make_async_copy(whole[i].at[seq], staged.at[n % 2, i], stage_sem.at[n % 2, i]) for i in range(2)
        ] + [pltpu.make_async_copy(routes.at[pl.ds(seq, 1)], spots.at[n % 2], stage_sem.at[n % 2, 2])]

    for n in (0, 1):
        for copy in stage(n):
            copy.start()
    own = [pltpu.make_async_copy(vector, vec.at[place.t], own_sem.at[2])]
    for w in range(4):
        own.append(pltpu.make_async_copy(local[w], fulls[w].at[place.t], own_sem.at[3 + w]))
    for copy in own:
        copy.start()
    place.greet()

    def z_copy(w, r):
        if r == 3:
            block = fulls[w].at[place.shard(2), :, place.j]
            return remote(block, block, z_send.at[w, 2], z_recv.at[w, 2], place.device(0, 1))
        return remote(
            local[w].at[:, place.j],
            fulls[w].at[place.t, :, place.j],
            z_send.at[w, r - 1],
            z_recv.at[w, r - 1],
            place.device(0, r),
        )

    def z_landed(w, r):
        block = fulls[w].at[place.shard(r), :, place.j]
        remote(block, block, z_send.at[w, r - 1], z_recv.at[w, r - 1], place.device(0, 1)).wait_recv()

    def z_begin(w):
        z_copy(w, 2).start()
        z_copy(w, 1).start()

    def vec_copy(r):
        return remote(vector, vec.at[place.t], row_send.at[2, r - 1], row_recv.at[2, r - 1], place.device(0, r))

    def vec_landed(r):
        dst = vec.at[place.shard(r)]
        return remote(dst, dst, row_send.at[2, r - 1], row_recv.at[2, r - 1], place.device(0, r))

    rows_one = exchange_rows(place, found.at[0], pk, row_send.at[0], row_recv.at[0], True)
    rows_two = exchange_rows(place, found.at[1], gr, row_send.at[1], row_recv.at[1], True)

    def find(n):
        for copy in stage(n):
            copy.wait()
        length = staged.shape[2]
        spot = jnp.transpose(spots[n % 2].astype(F32)).astype(jnp.int32)
        chosen = (spot == lax.broadcasted_iota(jnp.int32, (cap, length), 1)).astype(BF16)
        rs = pl.ds(n % per * cap, cap)
        for i in range(2):
            value = dot(chosen, staged[n % 2, i]).astype(BF16)
            if n // per < 3:
                found[i, (2, 1, 3)[n // per] - 1, rs, :] = value
            else:
                (pk, gr)[i][place.t, rs, :] = value
        if n + 2 < seqs:
            for copy in stage(n + 2):
                copy.start()

    q, o, u, d = 0, 1, 2, 3
    groups = [(u,), (q, o), (d,)]
    chains = []
    for g, group in enumerate(groups):
        for r in (2, 1, 3):
            spread = [spread_slices(place, fulls[w], r, p_send.at[w, r - 1], p_recv.at[w, r - 1]) for w in group]

            def first(g=g, group=group, r=r, spread=spread):
                for w, stages in zip(group, spread):
                    z_landed(w, r)
                    if r == 2:
                        z_copy(w, 3).start()
                    stages[0]()
                if (g, r) == (0, 2):
                    z_begin(q)
                    z_begin(o)
                if (g, r) == (1, 1):
                    z_begin(d)
                if (g, r) == (2, 3):
                    rows_two[0]()

            def later(n, spread=spread):
                return lambda: [stages[n]() for stages in spread]

            chains.append([first, later(1), later(2), later(3)])

    saved = [
        pltpu.make_async_copy(src, dst, out_sem.at[i])
        for i, (src, dst) in enumerate(zip(list(fulls) + [pk, gr, n1, qkv, ho, at, hid, gp, rows_out, stats, vec], outs))
    ]

    def read_rows():
        rows_one[1]()
        own[0].wait()
        for r in (1, 2, 3):
            vec_landed(r).wait_recv()
        norm_one(pk, vec, n1, stats)
        saved[4].start()
        saved[6].start()
        saved[14].start()

    def heads_of(r):
        a = place.shard(r)
        project(a, n1, fulls[q], qkv)
        attend(a, cap, qkv, ho)

    def up_of(r):
        raise_up(place.shard(r), n2, fulls[u], hid, gp, pre)

    def down_of(r, start=False):
        bring_down(place.shard(r), hid, fulls[d], acc, start)

    def after(tick):
        if tick < 4:
            for n in range(per):
                find(tick * per + n)
        if tick == 3:
            rows_one[0]()
        if tick == 5:
            own[3].wait()
            saved[2].start()
        if tick == 6:
            read_rows()
            own[1].wait()
            heads_of(0)
            heads_of(2)
        if tick == 7:
            heads_of(1)
        if tick == 8:
            heads_of(3)
            own[2].wait()
            attend_out(pk, vec, ho, fulls[o], at, n2, stats)
            up_of(0)
            for i in (0, 1, 7, 8, 9):
                saved[i].start()
        if tick == 9:
            up_of(2)
            up_of(1)
        if tick == 10:
            up_of(3)
            saved[10].start()
            saved[11].start()
            own[4].wait()
            down_of(0, True)
            down_of(2)
        if tick == 11:
            down_of(1)
            down_of(3)

    z_begin(u)
    for r in (1, 2, 3):
        vec_copy(r).start()
    pipelined(chains, after)
    saved[3].start()
    rows_two[1]()
    saved[5].start()
    finish_rows(pk, gr, at, acc, rows_out, stats)
    saved[12].start()
    saved[13].start()
    for w in range(4):
        for r in (1, 2, 3):
            z_copy(w, r).wait_send()
    for r in (1, 2, 3):
        vec_copy(r).wait_send()
    for copy in saved:
        copy.wait()


def forward(whole, routes, vector, local):
    seqs, length, cols = whole[0].shape
    cap = routes.shape[1]
    rows = seqs // 4 * cap
    width = 4 * cols
    inner = local[2].shape[3]
    fulls = [(4,) + w.shape for w in local]
    dma = pltpu.SemaphoreType.DMA
    kept = [
        ((4, rows, cols), BF16),
        ((4, rows, cols), BF16),
        ((rows, width), BF16),
        ((4, 3, rows, cols), BF16),
        ((4, rows, cols), BF16),
        ((rows, width), F32),
        ((4, rows, inner), BF16),
        ((4, rows, inner), BF16),
        ((4, rows, cols), BF16),
        ((rows, WIDE), F32),
        ((4, 8, cols), F32),
    ]
    vmem = pltpu.VMEM
    scratch = [vmem(f, BF16) for f in fulls] + [
        vmem((4, rows, cols), BF16),
        vmem((4, rows, cols), BF16),
        vmem((4, 8, cols), F32),
        vmem((rows, width), BF16),
        vmem((4, 3, rows, cols), BF16),
        vmem((4, rows, cols), BF16),
        vmem((rows, width), F32),
        vmem((rows, width), BF16),
        vmem((4, rows, inner), BF16),
        vmem((4, rows, inner), BF16),
        vmem((rows, width), F32),
        vmem((4, rows, cols), BF16),
        vmem((rows, WIDE), F32),
        vmem((rows, 256), F32),
        vmem((2, 2, length, cols), BF16),
        vmem((2, 3, rows, cols), BF16),
        vmem((2, 1, cap), jnp.int32),
        dma((4, 3)),
        dma((4, 3)),
        dma((4, 3, 8)),
        dma((4, 3, 8)),
        dma((3, 3)),
        dma((3, 3)),
        dma((7,)),
        dma((15,)),
        dma((2, 3)),
    ]
    return pl.pallas_call(
        functools.partial(forward_kernel, cap),
        in_specs=[ANY] * 8,
        out_specs=[ANY] * 15,
        out_shape=[jax.ShapeDtypeStruct(f, BF16) for f in fulls] + [jax.ShapeDtypeStruct(*k) for k in kept],
        scratch_shapes=scratch,
        compiler_params=pltpu.CompilerParams(
            collective_id=1, has_side_effects=True, vmem_limit_bytes=60 * 1024 * 1024
        ),
        name="forward",
    )(*whole, routes, vector, *local)


def half_blocks(ref_cols, count, parity):
    parts = []
    for b in range(count // 2):
        start = pl.multiple_of((2 * b + parity) * WIDE, WIDE)
        parts.append(ref_cols(pl.ds(start, WIDE)))
    return jnp.concatenate(parts, axis=1)


def outer(left, right, width, put, block=512):
    turned = jnp.transpose(left)

    def step(i, carry):
        cs = pl.ds(pl.multiple_of(i * block, block), block)
        put(cs, dot(turned, right(cs)))
        return carry

    lax.fori_loop(0, width // block, step, 0)


class Sum:
    def __init__(self, place, away, buf, got2, got3, got4, got5, result, sends, recvs, own_sem):
        self.place, self.away, self.buf, self.result = place, away, buf, result
        self.freed = False
        self.got2, self.got3, self.got4, self.got5 = got2, got3, got4, got5
        self.sends, self.recvs = sends, recvs
        rows = buf.shape[4]
        self.low, self.high = pl.ds(0, rows // 2), pl.ds(rows // 2, rows // 2)
        self.keep = pltpu.make_async_copy(
            buf.at[place.t, :, place.y, place.x], result.at[:, place.j], own_sem
        )
        self.spread = spread_slices(
            place,
            result,
            None,
            sends.at[pl.ds(23, 8)],
            recvs.at[pl.ds(23, 8)],
            own=buf.at[place.t, :, place.y, place.x],
        )

    def core(self, a):
        return remote(self.away.at[a], self.buf.at[a], self.sends.at[a], self.recvs.at[a], self.place.device(CORE))

    def away_free(self):
        if not self.freed:
            for a in range(4):
                self.core(a).wait_send()
        self.freed = True

    def copy(self, n):
        p, buf, a = self.place, self.buf, n % 4
        x, y, low, high = p.x, p.y, self.low, self.high
        if n >= 16:
            src, dst, r = (
                lambda: (buf.at[p.shard(1), :, y, x], self.got4.at[0], 1),
                lambda: (buf.at[p.shard(3), :, y, x], self.got4.at[1], 1),
                lambda: (buf.at[p.shard(2), :, y, x], self.got5, 2),
            )[n - 16]()
            device = p.device(0, r)
        else:
            src, dst, device = (
                lambda: (buf.at[a, :, :, 1 - x, low], self.got2.at[0, a], p.device(X)),
                lambda: (buf.at[a, :, 1 - y, :, high], self.got2.at[1, a], p.device(Y)),
                lambda: (buf.at[a, :, 1 - y, x, low], self.got3.at[0, a], p.device(Y)),
                lambda: (buf.at[a, :, y, 1 - x, high], self.got3.at[1, a], p.device(X)),
            )[n // 4]()
        return remote(src, dst, self.sends.at[4 + n], self.recvs.at[4 + n], device)

    def took(self, n):
        self.copy(n).wait_recv()
        self.copy(n).wait_send()

    def add(self, index, extra):
        self.buf[index] = (self.buf[index].astype(F32) + extra.astype(F32)).astype(BF16)

    def one(self, a):
        self.copy(a).start()
        self.copy(4 + a).start()

    def two(self):
        p = self.place
        for a in range(4):
            self.took(a)
            for b in range(2):
                self.add((a, 0, b, p.x, self.low), self.got2[0, a, 0, b])
            self.copy(8 + a).start()
            self.took(4 + a)
            for b in range(2):
                self.add((a, 0, p.y, b, self.high), self.got2[1, a, 0, b])
            self.copy(12 + a).start()

    def three(self):
        p = self.place
        for a in range(4):
            for n, part in ((0, self.low), (1, self.high)):
                self.took(8 + 4 * n + a)
                self.add((a, 0, p.y, p.x, part), self.got3[n, a, 0])
        self.copy(16).start()
        self.copy(17).start()

    def four(self):
        p = self.place
        for n, shard in ((0, p.t), (1, p.shard(2))):
            self.took(16 + n)
            self.add((shard, 0, p.y, p.x), self.got4[n, 0])
        self.copy(18).start()

    def five(self):
        p = self.place
        self.away_free()
        self.took(18)
        self.add((p.t, 0, p.y, p.x), self.got5[0])
        self.keep.start()
        self.spread[0]()

    def stages(self):
        return [self.two, self.three, self.four, self.five] + self.spread[1:] + [self.keep.wait]


def attend_back(a, cap, qkv, dh):
    rows, cols = qkv.shape[2], qkv.shape[3]
    pairs = cols // WIDE
    scale = HEAD_DIM ** (-0.5)

    def step(i, carry):
        seq, pair = lax.div(i, jnp.int32(pairs)), lax.rem(i, jnp.int32(pairs))
        rs = pl.ds(pl.multiple_of(seq * cap, cap), cap)
        cs = pl.ds(pl.multiple_of(pair * WIDE, WIDE), WIDE)
        q, k, v, g = qkv[a, 0, rs, cs], qkv[a, 1, rs, cs], qkv[a, 2, rs, cs], dh[a, rs, cs]
        first = lax.broadcasted_iota(jnp.int32, (cap, WIDE), 1) < HEAD_DIM
        causal = lax.broadcasted_iota(jnp.int32, (cap, cap), 0) >= lax.broadcasted_iota(jnp.int32, (cap, cap), 1)
        dq = dk = dv = None
        for mine in (first, jnp.logical_not(first)):
            zero = jnp.zeros_like(q)
            qh, kh, gh = jnp.where(mine, q, zero), jnp.where(mine, k, zero), jnp.where(mine, g, zero)
            scores = jnp.where(causal, dot_nt(qh, k) * scale, -1e30)
            exps = jnp.exp(scores - jnp.max(scores, axis=1, keepdims=True))
            probs = exps / jnp.sum(exps, axis=1, keepdims=True)
            d_probs = dot_nt(gh, v)
            lean = jnp.sum(probs * d_probs, axis=1, keepdims=True)
            d_scores = (probs * (d_probs - lean)).astype(BF16)
            parts = (dot(d_scores, kh), dot_tn(d_scores, qh), dot_tn(probs.astype(BF16), gh))
            dq, dk, dv = parts if dq is None else (dq + parts[0], dk + parts[1], dv + parts[2])
        qkv[a, 0, rs, cs] = (dq * scale).astype(BF16)
        qkv[a, 1, rs, cs] = (dk * scale).astype(BF16)
        qkv[a, 2, rs, cs] = dv.astype(BF16)
        return carry

    lax.fori_loop(0, rows // cap * pairs, step, 0)


LAST_STAGES = [
    (1, 0), (2, 1), (3, 3), (1, 1), (2, 2), (0, 0), (3, 4),
    (2, 3), (1, 2), (0, 1), (3, 5), (2, 4), (1, 3), (0, 2),
    (3, 6), (2, 5), (1, 4), (0, 3), (2, 6), (1, 5), (0, 4),
    (1, 6), (0, 5), (0, 6), (3, 7), (2, 7), (1, 7), (0, 7),
]


def backward_kernel(cap, *refs):
    out_rows, vector = refs[0:2]
    saved = refs[2:11]
    weights = refs[11:15]
    got_out, got_in, small = refs[15:18]
    results = refs[18:22]
    pk, gr, n1, qkv, ho, at, hid, gp, stats = refs[22:31]
    vec, slots, dm, dn, n2, pre, spare, own_out = refs[31:39]
    bufs, got2, got3, got4, got5 = refs[39:43], refs[43:47], refs[47:51], refs[51:55], refs[55:59]
    sums, heard, pieces = refs[59:62]
    sends, recvs, row_send, row_recv, in_sem, slot_sem, keep_sem, s_send, s_recv = refs[62:]
    place = Place()
    rows, width = dm.shape
    cols = pk.shape[2]
    c, t = place.c, place.t
    loads = [
        pltpu.make_async_copy(src, dst, in_sem.at[i])
        for i, (src, dst) in enumerate(zip(saved[:9], [stats, gr, hid, gp, pk, at, ho, qkv, n1]))
    ]
    loads.append(pltpu.make_async_copy(out_rows.at[t], got_out.at[t], in_sem.at[9]))
    loads.append(pltpu.make_async_copy(vector, vec, in_sem.at[10]))
    for copy in loads:
        copy.start()
    wq, wo, wu, wd = weights

    def slot_copies(i):
        slot = slots.at[i % 2]
        if i < 8:
            src = (wd if i < 4 else wu).at[i % 4]
            return [pltpu.make_async_copy(src, slot, slot_sem.at[i % 2, 0])]
        if i == 8:
            return [pltpu.make_async_copy(wo, slot, slot_sem.at[0, 0])]
        return [
            pltpu.make_async_copy(
                wq.at[i - 9, k], slot.at[:, pl.ds(k * cols, cols)], slot_sem.at[i % 2, k]
            )
            for k in range(3)
        ]

    def slot_start(i):
        if i < 13:
            for copy in slot_copies(i):
                copy.start()

    def slot_ready(i):
        for copy in slot_copies(i):
            copy.wait()

    slot_start(0)
    slot_start(1)
    place.greet()
    rows_one = exchange_rows(place, out_rows, got_out, row_send.at[0], row_recv.at[0])
    rows_two = exchange_rows(place, pk, got_in, row_send.at[1], row_recv.at[1])
    rows_one[0]()

    aways = [
        spare.at[:, :, :, :, :, pl.ds(0, 3 * cols)],
        spare.at[:, :, :, :, pl.ds(0, bufs[1].shape[4]), :],
        hid,
        spare,
    ]
    chain = [
        Sum(
            place, aways[w], bufs[w], got2[w], got3[w], got4[w], got5[w], results[w], sends.at[w], recvs.at[w], keep_sem.at[w]
        )
        for w in range(4)
    ]
    q, o, u, d = chain
    for i in (0, 1):
        loads[i].wait()

    def d_update(rs):
        dm[rs, :] = (stats[rs, 1:2] * joined(gr, rs)).astype(BF16)

    chunks(rows, 64, d_update)
    loads[2].wait()

    def send_half(one, a, left, right, total):
        def put(cs, value):
            size = value.shape[1]
            one.away[a, 0, :, :, :, cs] = value.astype(BF16).reshape(2, 2, -1, size)

        outer(left, right, total, put, block=256 if total % 512 else 512)
        one.core(a).start()

    def keep_half(one, a, left, right, total):
        one.core(a).wait_recv()

        def put(cs, value):
            size = value.shape[1]
            mine = one.buf[a, 0, :, :, :, cs].astype(F32).reshape(-1, size)
            one.buf[a, 0, :, :, :, cs] = (mine + value).astype(BF16).reshape(2, 2, -1, size)

        outer(left, right, total, put, block=256 if total % 512 else 512)

    def hid_half(a, parity):
        return half_blocks(lambda ls: hid[a, 0, :, :, :, ls].reshape(rows, WIDE), 8, parity)

    for a in range(4):
        send_half(d, a, hid_half(a, 1 - c), lambda cs: dm[:, cs], width)
    for a in range(4):
        keep_half(d, a, hid_half(a, c), lambda cs: dm[:, cs], width)
        d.one(a)
    loads[3].wait()
    for a in range(4):
        slot_ready(a)

        def d_hidden(i, carry, a=a):
            cs = pl.ds(pl.multiple_of(i * 256, 256), 256)
            pre[...] = dot_nt(dm[...], slots[a % 2, cs, :])

            def bend(rs):
                gp[a, rs, cs] = (pre[rs, :] * gp[a, rs, cs].astype(F32)).astype(BF16)

            chunks(rows, 64, bend)
            return carry

        lax.fori_loop(0, gp.shape[2] // 256, d_hidden, 0)
        slot_start(a + 2)
    loads[4].wait()
    loads[5].wait()
    loads[10].wait()

    def norm_two(rs):
        at[rs, :] += joined(pk, rs)
        n2[rs, :] = (at[rs, :] * stats[rs, 2:3] * vec[1:2, :]).astype(BF16)

    chunks(rows, 64, norm_two)
    left = half_blocks(lambda ls: n2[:, ls], 8, 1 - c)
    for a in range(4):
        send_half(u, a, left, lambda cs, a=a: gp[a, :, cs], gp.shape[2])
    left = half_blocks(lambda ls: n2[:, ls], 8, c)
    for a in range(4):
        keep_half(u, a, left, lambda cs, a=a: gp[a, :, cs], gp.shape[2])
        u.one(a)
    for a in range(4):
        slot_ready(4 + a)

        def d_normed(i, carry, a=a):
            cs = pl.ds(pl.multiple_of(i * 256, 256), 256)
            part = dot_nt(gp[a], slots[a % 2, cs, :])
            if a == 0:
                dn[:, cs] = part
            else:
                dn[:, cs] += part
            return carry

        lax.fori_loop(0, width // 256, d_normed, 0)
        slot_start(a + 6)
        if a == 2:
            d.two()

    sums[0] = jnp.zeros_like(sums[0])

    def norm_two_back(rs):
        mid, inv, grad = at[rs, :], stats[rs, 2:3], dn[rs, :]
        sums[0, 1:2, :] += jnp.sum(grad * mid * inv, axis=0, keepdims=True)
        grad = grad * vec[1:2, :]
        lean = jnp.sum(grad * mid, axis=1, keepdims=True)
        d_mid = inv * grad - mid * (inv * inv * inv * lean / width)
        at[rs, :] = d_mid
        dm[rs, :] = (stats[rs, 1:2] * joined(gr, rs) + d_mid).astype(BF16)

    chunks(rows, 64, norm_two_back)

    d.away_free()
    loads[6].wait()
    slot_ready(8)
    unit = bufs[1].shape[4]
    for a in range(4):
        turned = jnp.transpose(ho[a])

        def grad_out(i, carry, a=a, turned=turned):
            cs = pl.ds(pl.multiple_of(i * 256, 256), 256)
            pre[pl.ds(0, cols), :] = dot(turned, dm[:, cs])
            for b in range(4):
                away = pl.ds(pl.multiple_of((2 * b + 1 - c) * unit, unit), unit)
                mine = pl.ds(pl.multiple_of((2 * b + c) * unit, unit), unit)
                o.away[a, 0, b // 2, b % 2, :, cs] = pre[away, :].astype(BF16)
                own_out[a, 0, b // 2, b % 2, :, cs] = pre[mine, :].astype(BF16)
            return carry

        lax.fori_loop(0, width // 256, grad_out, 0)
        o.core(a).start()
        ho[a] = dot_nt(dm[...], slots[0, pl.ds(a * cols, cols), :]).astype(BF16)
    slot_start(10)
    for a in range(4):
        o.core(a).wait_recv()
        for b in range(4):
            o.add((a, 0, b // 2, b % 2), own_out[a, 0, b // 2, b % 2])
        o.one(a)
    loads[7].wait()
    for a in range(4):
        attend_back(a, cap, qkv, ho)
        if a == 1:
            d.three()
        if a == 2:
            u.two()
    d.four()
    o.away_free()
    loads[8].wait()

    def proj(a):
        return lambda cs: qkv[a, lax.div(cs.start, jnp.int32(cols))]

    for a in range(4):
        slot_ready(9 + a)

        def d_normed(i, carry, a=a):
            cs = pl.ds(pl.multiple_of(i * 256, 256), 256)
            part = dot_nt(qkv[a, 0], slots[(9 + a) % 2, cs, pl.ds(0, cols)])
            for k in (1, 2):
                part += dot_nt(qkv[a, k], slots[(9 + a) % 2, cs, pl.ds(k * cols, cols)])
            if a == 0:
                dn[:, cs] = part
            else:
                dn[:, cs] += part
            return carry

        lax.fori_loop(0, width // 256, d_normed, 0)
        slot_start(a + 11)

    def norm_one_back(rs):
        x, grows, grad = joined(pk, rs), joined(gr, rs), dn[rs, :]
        inv, d_logit = stats[rs, 0:1], stats[rs, 3:4]
        sums[0, 0:1, :] += jnp.sum(grad * x * inv, axis=0, keepdims=True)
        sums[0, 2:3, :] += jnp.sum(d_logit * x, axis=0, keepdims=True)
        grad = grad * vec[0:1, :]
        lean = jnp.sum(grad * x, axis=1, keepdims=True)
        result = grows + at[rs, :] + inv * grad - x * (inv * inv * inv * lean / width) + d_logit * vec[2:3, :]
        for a in range(4):
            pk[a, rs, :] = result[:, a * cols : (a + 1) * cols].astype(BF16)

    chunks(rows, 64, norm_one_back)
    rows_two[0]()
    own_in = pltpu.make_async_copy(pk.at[t], got_in.at[t], in_sem.at[11])
    own_in.start()
    left = half_blocks(lambda ls: n1[:, ls], 8, 1 - c)
    for a in range(4):
        send_half(q, a, left, proj(a), 3 * cols)
    left = half_blocks(lambda ls: n1[:, ls], 8, c)
    for a in range(4):
        keep_half(q, a, left, proj(a), 3 * cols)
        q.one(a)

    def step(n):
        bit = (CORE, X, Y)[n]
        return remote(sums.at[n], heard.at[n], s_send.at[n], s_recv.at[n], place.device(bit))

    def piece(r):
        lanes = pl.ds(pl.multiple_of(place.shard(r) * cols, cols), cols)
        return remote(sums.at[3, :, lanes], pieces.at[r - 1], s_send.at[2 + r], s_recv.at[2 + r], place.device(0, r))

    def after(tick):
        if tick < 3:
            if tick == 0:
                step(0).start()
            else:
                step(tick - 1).wait_recv()
                sums[tick] = sums[tick - 1] + heard[tick - 1]
                step(tick).start()
        if tick == 3:
            step(2).wait_recv()
            sums[3] = sums[2] + heard[2]
            for r in (1, 2, 3):
                piece(r).start()
        if tick == 4:
            for r in (1, 2, 3):
                piece(r).wait_recv()
            lanes = pl.ds(pl.multiple_of(t * cols, cols), cols)
            vec[:, pl.ds(0, cols)] = sums[3, :, lanes] + pieces[0] + pieces[1] + pieces[2]
            out_small.start()

    out_small = pltpu.make_async_copy(vec.at[:, pl.ds(0, cols)], small, in_sem.at[12])
    todo = [one.stages() for one in (q, o, u, d)]
    for tick, (one, stage) in enumerate(LAST_STAGES):
        todo[one][stage]()
        if tick % 2 == 0:
            after(tick // 2)
    for n in range(3):
        step(n).wait_send()
    for r in (1, 2, 3):
        piece(r).wait_send()
    rows_one[1]()
    rows_two[1]()
    loads[9].wait()
    own_in.wait()
    out_small.wait()


def backward(cap, out_rows, vector, saved, weights):
    _, rows, cols = out_rows.shape
    width = 4 * cols
    inner = weights[3].shape[1]
    slices = [(128, 3 * cols), (cols // GROUP, width), (width // GROUP, inner), (inner // GROUP, width)]
    dma = pltpu.SemaphoreType.DMA
    vmem = pltpu.VMEM
    scratch = [
        vmem((4, rows, cols), BF16),
        vmem((4, rows, cols), BF16),
        vmem((rows, width), BF16),
        vmem((4, 3, rows, cols), BF16),
        vmem((4, rows, cols), BF16),
        vmem((rows, width), F32),
        vmem((4, 1, 2, 2, rows // 4, inner), BF16),
        vmem((4, rows, inner), BF16),
        vmem((rows, WIDE), F32),
        vmem((8, width), F32),
        vmem((2, width, width), BF16),
        vmem((rows, width), BF16),
        vmem((rows, width), F32),
        vmem((rows, width), BF16),
        vmem((rows, 256), F32),
        vmem((4, 1, 2, 2, 128, width), BF16),
        vmem((4, 1, 2, 2) + slices[1], BF16),
    ]
    scratch += [vmem((4, 1, 2, 2) + s, BF16) for s in slices]
    scratch += [vmem((2, 4, 1, 2, s[0] // 2, s[1]), BF16) for s in slices]
    scratch += [vmem((2, 4, 1, s[0] // 2, s[1]), BF16) for s in slices]
    scratch += [vmem((2, 1) + s, BF16) for s in slices]
    scratch += [vmem((1,) + s, BF16) for s in slices]
    scratch += [
        vmem((4, 8, width), F32),
        vmem((3, 8, width), F32),
        vmem((3, 8, cols), F32),
        dma((4, 31)),
        dma((4, 31)),
        dma((2, 3)),
        dma((2, 3)),
        dma((13,)),
        dma((2, 3)),
        dma((4,)),
        dma((6,)),
        dma((6,)),
    ]
    return pl.pallas_call(
        functools.partial(backward_kernel, cap),
        in_specs=[ANY] * (2 + len(saved) + 4),
        out_specs=[ANY] * 7,
        out_shape=[jax.ShapeDtypeStruct(out_rows.shape, BF16)] * 2
        + [jax.ShapeDtypeStruct((8, cols), F32)]
        + [jax.ShapeDtypeStruct((1, 8) + s, BF16) for s in slices],
        scratch_shapes=scratch,
        compiler_params=pltpu.CompilerParams(
            collective_id=2, has_side_effects=True, vmem_limit_bytes=62 * 1024 * 1024
        ),
        name="backward",
    )(out_rows, vector, *saved, *weights)


def body(all_dp, n_t, block_input, routes, out_grad, w_qkv, w_out, w_up, w_down, gain_attn, gain_mlp, w_router):
    seqs, length, cols = block_input.shape
    cap = routes.shape[1]
    width = cols * n_t
    own = seqs // n_t
    rows = own * cap
    heads = cols // HEAD_DIM
    outer_bits = [1 << i for i in range(3, all_dp.bit_length() - 1)]

    def send(value, mask_dp, mask_t):
        pairs = [
            (d * n_t + s, (d ^ mask_dp) * n_t + (s ^ mask_t)) for d in range(all_dp) for s in range(n_t)
        ]
        return lax.ppermute(value, ("dp", "tensor"), pairs)

    vector = jnp.concatenate([gain_attn[None], gain_mlp[None], w_router[None], jnp.zeros((5, cols), F32)])
    local = [
        w_qkv.transpose(1, 0, 2).reshape(3, GROUP, width // GROUP, cols),
        w_out.reshape(1, GROUP, cols // GROUP, width),
        w_up.reshape(1, GROUP, width // GROUP, w_up.shape[1]),
        w_down.reshape(1, GROUP, w_down.shape[0] // GROUP, width),
    ]
    wq, wo, wu, wd, picked, grad_rows, normed_one, qkv, head_out, attn_out, hidden, bend, out_rows, stats, vectors = forward(
        [block_input, out_grad], routes, vector, local
    )
    vectors = vectors.transpose(1, 0, 2).reshape(8, width)
    got_out, got_in, sums, s_qkv, s_out, s_up, s_down = backward(
        cap,
        out_rows,
        vectors,
        [
            stats,
            grad_rows,
            hidden.reshape(n_t, 1, 2, 2, rows // 4, -1),
            bend,
            picked,
            attn_out,
            head_out,
            qkv,
            normed_one,
        ],
        [
            wq.reshape(n_t, 3, width, cols),
            wo.reshape(n_t * cols, width),
            wu.reshape(n_t, width, -1),
            wd.reshape(n_t, -1, width),
        ],
    )
    layer_out, input_grad, g_qkv, g_out, g_up, g_down = write_results(
        routes,
        [block_input, out_grad],
        [got_out.reshape(seqs, cap, cols), got_in.reshape(seqs, cap, cols)],
        [
            s_qkv.reshape(width, 3 * cols),
            s_out.reshape(w_out.shape),
            s_up.reshape(w_up.shape),
            s_down.reshape(w_down.shape),
        ],
    )
    for bit in outer_bits:
        sums = sums + send(sums, bit, 0)

    def settle(value):
        for bit in outer_bits:
            value = value + send(value, bit, 0)
        return value

    g_qkv, g_out, g_up, g_down = settle(g_qkv).transpose(1, 0, 2), settle(g_out), settle(g_up), settle(g_down)
    return (layer_out, input_grad, g_qkv, g_out, g_up, g_down, sums[0], sums[1], sums[2])


def solution(mesh):
    placed = (
        P("dp", None, "tensor"),
        P("dp", None),
        P("dp", None, "tensor"),
        P(None, None, "tensor"),
        P("tensor", None),
        P(None, "tensor"),
        P("tensor", None),
        P("tensor"),
        P("tensor"),
        P("tensor"),
    )
    return jax.shard_map(
        functools.partial(body, mesh.shape["dp"], mesh.shape["tensor"]),
        mesh=mesh,
        in_specs=placed,
        out_specs=(
            P("dp", None, "tensor"),
            P("dp", None, "tensor"),
            P(None, None, "tensor"),
            P("tensor", None),
            P(None, "tensor"),
            P("tensor", None),
            P("tensor"),
            P("tensor"),
            P("tensor"),
        ),
        check_vma=False,
    )
```

```python
import functools

import jax
import jax.numpy as jnp
from jax import lax
from jax.experimental import pallas as pl
from jax.experimental.pallas import tpu as pltpu
from jax.sharding import PartitionSpec as P

HEAD_DIM = 64
EPS = 1e-06
F32 = jnp.float32
BF16 = jnp.bfloat16


def exact_gelu(values):
    return jax.nn.gelu(values, approximate=False)


def write_kernel(routes_ref, *refs):
    blocks, rows, sums, outs = refs[0:2], refs[2:4], refs[4:8], refs[8:14]
    length, cols = blocks[0].shape[1:]
    cap = routes_ref.shape[2]
    places = lax.broadcasted_iota(jnp.int32, (length, cap), 0)
    chosen = (routes_ref[0] == places).astype(BF16)
    values = jnp.concatenate([rows[0][0], rows[1][0], jnp.ones((cap, WIDE), BF16)], axis=1)
    spread = jnp.dot(chosen, values, preferred_element_type=F32)
    spread = spread.astype(BF16)
    hit = spread[:, 2 * cols :] > 0.5
    for i in range(2):
        for part in range(cols // WIDE):
            lanes = pl.ds(part * WIDE, WIDE)
            new = spread[:, i * cols + part * WIDE : i * cols + (part + 1) * WIDE]
            outs[i][0, :, lanes] = jnp.where(hit, new, blocks[i][0, :, lanes])
    for k in range(3):
        outs[2][k] = sums[0][:, k * cols : (k + 1) * cols].astype(F32)
    for i in range(1, 4):
        outs[2 + i][...] = sums[i][...].astype(F32)


def write_results(routes, blocks, rows, sums):
    seqs, length, cols = blocks[0].shape
    cap = routes.shape[1]
    cut = [(s.shape[0] // seqs, s.shape[1]) for s in sums]
    block = pl.BlockSpec((1, length, cols), lambda s: (s, 0, 0))
    flat = [pl.BlockSpec(c, lambda s: (s, 0)) for c in cut]
    return pl.pallas_call(
        write_kernel,
        grid=(seqs,),
        in_specs=[pl.BlockSpec((1, 1, cap), lambda s: (s, 0, 0))]
        + [block] * 2
        + [pl.BlockSpec((1, cap, cols), lambda s: (s, 0, 0))] * 2
        + flat,
        out_specs=[block] * 2 + [pl.BlockSpec((3, cut[0][0], cols), lambda s: (0, s, 0))] + flat[1:],
        out_shape=[jax.ShapeDtypeStruct(b.shape, BF16) for b in blocks]
        + [jax.ShapeDtypeStruct((3, sums[0].shape[0], cols), F32)]
        + [jax.ShapeDtypeStruct(s.shape, F32) for s in sums[1:]],
        compiler_params=pltpu.CompilerParams(vmem_limit_bytes=60 * 1024 * 1024),
        name="write_results",
    )(routes[:, None, :], *blocks, *rows, *sums)


WIDE = 128
MESH = pl.DeviceIdType.MESH
GROUP = 8


def flip(value, bit):
    return value + bit - 2 * bit * lax.rem(lax.div(value, jnp.int32(bit)), jnp.int32(2))


class Place:
    def __init__(self):
        self.dp = lax.axis_index("dp").astype(jnp.int32)
        self.t = lax.axis_index("tensor").astype(jnp.int32)
        self.j = lax.rem(self.dp, jnp.int32(GROUP))
        self.c = lax.rem(self.j, jnp.int32(2))
        self.x = lax.rem(lax.div(self.j, jnp.int32(2)), jnp.int32(2))
        self.y = lax.div(self.j, jnp.int32(4))

    def slot(self, mask):
        value = self.j
        for bit in (1, 2, 4):
            if mask & bit:
                value = flip(value, bit)
        return value

    def shard(self, r):
        value = self.t
        for bit in (1, 2):
            if r & bit:
                value = flip(value, bit)
        return value

    def device(self, mask=0, r=0):
        value = self.dp
        for bit in (1, 2, 4):
            if mask & bit:
                value = flip(value, bit)
        return (value, self.shard(r))

    def greet(self):
        barrier = pltpu.get_barrier_semaphore()
        partners = [(mask, 0) for mask in (1, 2, 4)] + [(0, r) for r in (1, 2, 3)]
        for mask, r in partners:
            pl.semaphore_signal(barrier, inc=1, device_id=self.device(mask, r), device_id_type=MESH)
        pl.semaphore_wait(barrier, len(partners))


def remote(src, dst, send_sem, recv_sem, device):
    return pltpu.make_async_remote_copy(
        src_ref=src, dst_ref=dst, send_sem=send_sem, recv_sem=recv_sem, device_id=device, device_id_type=MESH
    )


CORE, X, Y = 1, 2, 4


def spread_slices(place, full, r, sends, recvs, own=None):
    def block(mask, part=None):
        ref = full.at[place.shard(r)] if r is not None else full
        ref = ref.at[:, place.slot(mask)]
        if part is None:
            return ref
        half = ref.shape[1] // 2
        return ref.at[:, pl.ds(part * half, half)]

    def copy(k, mask, to, part=None, src=None):
        return remote(src if src is not None else block(mask, part), block(mask, part), sends.at[k], recvs.at[k], place.device(to))

    def landed(k, mask, part=None):
        remote(block(mask, part), block(mask, part), sends.at[k], recvs.at[k], place.device(CORE)).wait_recv()

    plan = [
        (0, 0, X, None),
        (1, 0, Y, None),
        (2, 0, CORE, None),
        (3, X, Y, 0),
        (4, Y, X, 1),
        (5, X, CORE, None),
        (6, Y, CORE, None),
        (7, X | Y, CORE, None),
    ]

    def begin():
        for k in (0, 1, 2):
            _, mask, to, part = plan[k]
            copy(k, mask, to, part, own).start()

    def forward():
        landed(0, X)
        copy(*plan[3]).start()
        copy(*plan[5]).start()
        landed(1, Y)
        copy(*plan[4]).start()
        copy(*plan[6]).start()

    def corner():
        landed(3, X | Y, 0)
        landed(4, X | Y, 1)
        copy(*plan[7]).start()

    def finish():
        for k, mask in ((2, CORE), (5, CORE | X), (6, CORE | Y), (7, CORE | X | Y)):
            landed(k, mask)
        for k, mask, to, part in plan:
            copy(k, mask, to, part, own if k < 3 else None).wait_send()

    return [begin, forward, corner, finish]


def pipelined(chains, after=None):
    depth = max(len(chain) for chain in chains)
    for tick in range(len(chains) + depth - 1):
        for i in range(max(0, tick - depth + 1), min(tick, len(chains) - 1) + 1):
            stage = tick - i
            if stage < len(chains[i]):
                chains[i][stage]()
        if after is not None:
            after(tick)


def exchange_rows(place, src, dst, sends, recvs, relative=False):
    def copy(r):
        return remote(src.at[r - 1 if relative else place.shard(r)], dst.at[place.t], sends.at[r - 1], recvs.at[r - 1], place.device(0, r))

    def landed(r):
        ref = dst.at[place.shard(r)]
        return remote(ref, ref, sends.at[r - 1], recvs.at[r - 1], place.device(0, r))

    def begin(order=(2, 3, 1)):
        for r in order:
            copy(r).start()

    def finish():
        for r in (1, 2, 3):
            landed(r).wait_recv()
        for r in (1, 2, 3):
            copy(r).wait_send()

    return begin, finish


ANY = pl.BlockSpec(memory_space=pl.ANY)


def dot(a, b):
    return jnp.dot(a, b, preferred_element_type=F32)


def dot_nt(a, b):
    return lax.dot_general(a, b, (((1,), (1,)), ((), ())), preferred_element_type=F32)


def dot_tn(a, b):
    return lax.dot_general(a, b, (((0,), (0,)), ((), ())), preferred_element_type=F32)


def chunks(total, size, step):
    def one(i, carry):
        step(pl.ds(pl.multiple_of(i * size, size), size))
        return carry

    lax.fori_loop(0, total // size, one, 0)


def joined(ref, rows):
    return jnp.concatenate([ref[a, rows, :].astype(F32) for a in range(4)], axis=1)


def gain(vec, i):
    return jnp.concatenate([vec[a, i : i + 1, :] for a in range(4)], axis=1)


def norm_one(pk, vec, n1, stats):
    gain_one, route_w = gain(vec, 0), gain(vec, 2)
    width = gain_one.shape[1]

    def step(rows):
        x = joined(pk, rows)
        inv = lax.rsqrt(jnp.sum(x * x, axis=1, keepdims=True) / width + EPS)
        n1[rows, :] = (x * inv * gain_one).astype(BF16)
        stats[rows, 0:1] = inv
        stats[rows, 1:2] = jax.nn.sigmoid(jnp.sum(x * route_w, axis=1, keepdims=True))

    chunks(n1.shape[0], 64, step)


def project(a, n1, fq, qkv):
    width = n1.shape[1]

    def step(k, carry):
        weight = fq[a, k].reshape(width, -1)
        qkv[a, k] = dot(n1[...], weight).astype(BF16)
        return carry

    lax.fori_loop(0, 3, step, 0)


def attend(a, cap, qkv, ho):
    rows, cols = qkv.shape[2], qkv.shape[3]
    pairs = cols // WIDE
    scale = HEAD_DIM ** (-0.5)

    def step(i, carry):
        seq, pair = lax.div(i, jnp.int32(pairs)), lax.rem(i, jnp.int32(pairs))
        rs = pl.ds(pl.multiple_of(seq * cap, cap), cap)
        cs = pl.ds(pl.multiple_of(pair * WIDE, WIDE), WIDE)
        q, k, v = qkv[a, 0, rs, cs], qkv[a, 1, rs, cs], qkv[a, 2, rs, cs]
        first = lax.broadcasted_iota(jnp.int32, (cap, WIDE), 1) < HEAD_DIM
        causal = lax.broadcasted_iota(jnp.int32, (cap, cap), 0) >= lax.broadcasted_iota(jnp.int32, (cap, cap), 1)
        outs = []
        for mine in (first, jnp.logical_not(first)):
            scores = dot_nt(jnp.where(mine, q, jnp.zeros_like(q)), k) * scale
            scores = jnp.where(causal, scores, -1e30)
            exps = jnp.exp(scores - jnp.max(scores, axis=1, keepdims=True))
            probs = (exps / jnp.sum(exps, axis=1, keepdims=True)).astype(BF16)
            outs.append(dot(probs, v))
        ho[a, rs, cs] = jnp.where(first, outs[0], outs[1]).astype(BF16)
        return carry

    lax.fori_loop(0, rows // cap * pairs, step, 0)


def attend_out(pk, vec, ho, fo, at, n2, stats):
    gain_two = gain(vec, 1)
    rows, width = n2.shape
    cols = ho.shape[2]

    def product(rs):
        total = dot(ho[0, rs, :], fo[0].reshape(cols, width))
        for a in range(1, 4):
            total += dot(ho[a, rs, :], fo[a].reshape(cols, width))
        at[rs, :] = total

    chunks(rows, 256, product)

    def step(rs):
        mid = joined(pk, rs) + at[rs, :]
        inv = lax.rsqrt(jnp.sum(mid * mid, axis=1, keepdims=True) / width + EPS)
        n2[rs, :] = (mid * inv * gain_two).astype(BF16)
        stats[rs, 2:3] = inv

    chunks(rows, 64, step)


def raise_up(a, n2, fu, hid, gp, pre):
    rows, width = n2.shape
    inner = hid.shape[2]
    block = pre.shape[1]

    def step(i, carry):
        cs = pl.ds(pl.multiple_of(i * block, block), block)
        weight = fu[a, 0, :, :, cs].reshape(width, block)
        pre[...] = dot(n2[...], weight)

        def bend(rs):
            x = pre[rs, :]
            cdf = 0.5 * (1.0 + lax.erf(x * (2.0**-0.5)))
            hid[a, rs, cs] = (x * cdf).astype(BF16)
            gp[a, rs, cs] = (cdf + x * jnp.exp(-0.5 * x * x) * 0.3989422804014327).astype(BF16)

        chunks(rows, 64, bend)
        return carry

    lax.fori_loop(0, inner // block, step, 0)


def bring_down(a, hid, fd, acc, start):
    inner, width = hid.shape[2], acc.shape[1]
    block = 256

    def step(i, carry):
        cs = pl.ds(pl.multiple_of(i * block, block), block)
        part = dot(hid[a], fd[a, 0, :, :, cs].reshape(inner, block))
        if start:
            acc[:, cs] = part
        else:
            acc[:, cs] += part
        return carry

    lax.fori_loop(0, width // block, step, 0)


def finish_rows(pk, gr, at, acc, rows_out, stats):
    cols = pk.shape[2]

    def step(rs):
        update = at[rs, :] + acc[rs, :]
        router = stats[rs, 1:2]
        result = joined(pk, rs) + router * update
        for a in range(4):
            rows_out[a, rs, :] = result[:, a * cols : (a + 1) * cols].astype(BF16)
        lean = jnp.sum(joined(gr, rs) * update, axis=1, keepdims=True)
        stats[rs, 3:4] = lean * router * (1.0 - router)

    chunks(acc.shape[0], 64, step)


def forward_kernel(cap, *refs):
    whole, routes, vector = refs[0:2], refs[2], refs[3]
    local = refs[4:8]
    outs = refs[8:23]
    fulls = refs[23:27]
    pk, gr, vec, n1, qkv, ho, at, n2, hid, gp, acc, rows_out, stats, pre, staged, found, spots = refs[27:44]
    z_send, z_recv, p_send, p_recv, row_send, row_recv, own_sem, out_sem, stage_sem = refs[44:]
    place = Place()
    seqs = routes.shape[0]
    per = seqs // 4

    def stage(n):
        seq = place.shard((2, 1, 3, 0)[n // per]) * per + n % per
        return [
            pltpu.make_async_copy(whole[i].at[seq], staged.at[n % 2, i], stage_sem.at[n % 2, i]) for i in range(2)
        ] + [pltpu.make_async_copy(routes.at[pl.ds(seq, 1)], spots.at[n % 2], stage_sem.at[n % 2, 2])]

    for n in (0, 1):
        for copy in stage(n):
            copy.start()
    own = [pltpu.make_async_copy(vector, vec.at[place.t], own_sem.at[2])]
    for w in range(4):
        own.append(pltpu.make_async_copy(local[w], fulls[w].at[place.t], own_sem.at[3 + w]))
    for copy in own:
        copy.start()
    place.greet()

    def z_copy(w, r):
        if r == 3:
            block = fulls[w].at[place.shard(2), :, place.j]
            return remote(block, block, z_send.at[w, 2], z_recv.at[w, 2], place.device(0, 1))
        return remote(
            local[w].at[:, place.j],
            fulls[w].at[place.t, :, place.j],
            z_send.at[w, r - 1],
            z_recv.at[w, r - 1],
            place.device(0, r),
        )

    def z_landed(w, r):
        block = fulls[w].at[place.shard(r), :, place.j]
        remote(block, block, z_send.at[w, r - 1], z_recv.at[w, r - 1], place.device(0, 1)).wait_recv()

    def z_begin(w):
        z_copy(w, 2).start()
        z_copy(w, 1).start()

    def vec_copy(r):
        return remote(vector, vec.at[place.t], row_send.at[2, r - 1], row_recv.at[2, r - 1], place.device(0, r))

    def vec_landed(r):
        dst = vec.at[place.shard(r)]
        return remote(dst, dst, row_send.at[2, r - 1], row_recv.at[2, r - 1], place.device(0, r))

    rows_one = exchange_rows(place, found.at[0], pk, row_send.at[0], row_recv.at[0], True)
    rows_two = exchange_rows(place, found.at[1], gr, row_send.at[1], row_recv.at[1], True)

    def find(n):
        for copy in stage(n):
            copy.wait()
        length = staged.shape[2]
        spot = jnp.transpose(spots[n % 2].astype(F32)).astype(jnp.int32)
        chosen = (spot == lax.broadcasted_iota(jnp.int32, (cap, length), 1)).astype(BF16)
        rs = pl.ds(n % per * cap, cap)
        for i in range(2):
            value = dot(chosen, staged[n % 2, i]).astype(BF16)
            if n // per < 3:
                found[i, (2, 1, 3)[n // per] - 1, rs, :] = value
            else:
                (pk, gr)[i][place.t, rs, :] = value
        if n + 2 < seqs:
            for copy in stage(n + 2):
                copy.start()

    q, o, u, d = 0, 1, 2, 3
    groups = [(u,), (q, o), (d,)]
    chains = []
    for g, group in enumerate(groups):
        for r in (2, 1, 3):
            spread = [spread_slices(place, fulls[w], r, p_send.at[w, r - 1], p_recv.at[w, r - 1]) for w in group]

            def first(g=g, group=group, r=r, spread=spread):
                for w, stages in zip(group, spread):
                    z_landed(w, r)
                    if r == 2:
                        z_copy(w, 3).start()
                    stages[0]()
                if (g, r) == (0, 2):
                    z_begin(q)
                    z_begin(o)
                if (g, r) == (1, 1):
                    z_begin(d)
                if (g, r) == (2, 3):
                    rows_two[0]()

            def later(n, spread=spread):
                return lambda: [stages[n]() for stages in spread]

            chains.append([first, later(1), later(2), later(3)])

    saved = [
        pltpu.make_async_copy(src, dst, out_sem.at[i])
        for i, (src, dst) in enumerate(zip(list(fulls) + [pk, gr, n1, qkv, ho, at, hid, gp, rows_out, stats, vec], outs))
    ]

    def read_rows():
        rows_one[1]()
        own[0].wait()
        for r in (1, 2, 3):
            vec_landed(r).wait_recv()
        norm_one(pk, vec, n1, stats)
        saved[4].start()
        saved[6].start()
        saved[14].start()

    def heads_of(r):
        a = place.shard(r)
        project(a, n1, fulls[q], qkv)
        attend(a, cap, qkv, ho)

    def up_of(r):
        raise_up(place.shard(r), n2, fulls[u], hid, gp, pre)

    def down_of(r, start=False):
        bring_down(place.shard(r), hid, fulls[d], acc, start)

    def after(tick):
        if tick < 4:
            for n in range(per):
                find(tick * per + n)
        if tick < 3:
            rows_one[0](((2, 1, 3)[tick],))
        if tick == 5:
            own[3].wait()
            saved[2].start()
            read_rows()
            own[1].wait()
            heads_of(0)
        if tick == 6:
            heads_of(2)
        if tick == 7:
            heads_of(1)
        if tick == 8:
            heads_of(3)
            own[2].wait()
            attend_out(pk, vec, ho, fulls[o], at, n2, stats)
            up_of(0)
            for i in (0, 1, 7, 8, 9):
                saved[i].start()
        if tick == 9:
            up_of(2)
            up_of(1)
        if tick == 10:
            up_of(3)
            saved[10].start()
            saved[11].start()
            own[4].wait()
            down_of(0, True)
            down_of(2)
        if tick == 11:
            down_of(1)
            down_of(3)

    z_begin(u)
    for r in (1, 2, 3):
        vec_copy(r).start()
    pipelined(chains, after)
    saved[3].start()
    rows_two[1]()
    saved[5].start()
    finish_rows(pk, gr, at, acc, rows_out, stats)
    saved[12].start()
    saved[13].start()
    for w in range(4):
        for r in (1, 2, 3):
            z_copy(w, r).wait_send()
    for r in (1, 2, 3):
        vec_copy(r).wait_send()
    for copy in saved:
        copy.wait()


def forward(whole, routes, vector, local):
    seqs, length, cols = whole[0].shape
    cap = routes.shape[1]
    rows = seqs // 4 * cap
    width = 4 * cols
    inner = local[2].shape[3]
    fulls = [(4,) + w.shape for w in local]
    dma = pltpu.SemaphoreType.DMA
    kept = [
        ((4, rows, cols), BF16),
        ((4, rows, cols), BF16),
        ((rows, width), BF16),
        ((4, 3, rows, cols), BF16),
        ((4, rows, cols), BF16),
        ((rows, width), F32),
        ((4, rows, inner), BF16),
        ((4, rows, inner), BF16),
        ((4, rows, cols), BF16),
        ((rows, WIDE), F32),
        ((4, 8, cols), F32),
    ]
    vmem = pltpu.VMEM
    scratch = [vmem(f, BF16) for f in fulls] + [
        vmem((4, rows, cols), BF16),
        vmem((4, rows, cols), BF16),
        vmem((4, 8, cols), F32),
        vmem((rows, width), BF16),
        vmem((4, 3, rows, cols), BF16),
        vmem((4, rows, cols), BF16),
        vmem((rows, width), F32),
        vmem((rows, width), BF16),
        vmem((4, rows, inner), BF16),
        vmem((4, rows, inner), BF16),
        vmem((rows, width), F32),
        vmem((4, rows, cols), BF16),
        vmem((rows, WIDE), F32),
        vmem((rows, 256), F32),
        vmem((2, 2, length, cols), BF16),
        vmem((2, 3, rows, cols), BF16),
        vmem((2, 1, cap), jnp.int32),
        dma((4, 3)),
        dma((4, 3)),
        dma((4, 3, 8)),
        dma((4, 3, 8)),
        dma((3, 3)),
        dma((3, 3)),
        dma((7,)),
        dma((15,)),
        dma((2, 3)),
    ]
    return pl.pallas_call(
        functools.partial(forward_kernel, cap),
        in_specs=[ANY] * 8,
        out_specs=[ANY] * 15,
        out_shape=[jax.ShapeDtypeStruct(f, BF16) for f in fulls] + [jax.ShapeDtypeStruct(*k) for k in kept],
        scratch_shapes=scratch,
        compiler_params=pltpu.CompilerParams(
            collective_id=1, has_side_effects=True, vmem_limit_bytes=60 * 1024 * 1024
        ),
        name="forward",
    )(*whole, routes, vector, *local)


def half_blocks(ref_cols, count, parity):
    parts = []
    for b in range(count // 2):
        start = pl.multiple_of((2 * b + parity) * WIDE, WIDE)
        parts.append(ref_cols(pl.ds(start, WIDE)))
    return jnp.concatenate(parts, axis=1)


def outer(left, right, width, put, block=512):
    turned = jnp.transpose(left)

    def step(i, carry):
        cs = pl.ds(pl.multiple_of(i * block, block), block)
        put(cs, dot(turned, right(cs)))
        return carry

    lax.fori_loop(0, width // block, step, 0)


class Sum:
    def __init__(self, place, away, buf, got2, got3, got4, got5, result, sends, recvs, own_sem):
        self.place, self.away, self.buf, self.result = place, away, buf, result
        self.freed = False
        self.got2, self.got3, self.got4, self.got5 = got2, got3, got4, got5
        self.sends, self.recvs = sends, recvs
        rows = buf.shape[4]
        self.low, self.high = pl.ds(0, rows // 2), pl.ds(rows // 2, rows // 2)
        self.keep = pltpu.make_async_copy(
            buf.at[place.t, :, place.y, place.x], result.at[:, place.j], own_sem
        )
        self.spread = spread_slices(
            place,
            result,
            None,
            sends.at[pl.ds(23, 8)],
            recvs.at[pl.ds(23, 8)],
            own=buf.at[place.t, :, place.y, place.x],
        )

    def core(self, a):
        return remote(self.away.at[a], self.buf.at[a], self.sends.at[a], self.recvs.at[a], self.place.device(CORE))

    def away_free(self):
        if not self.freed:
            for a in range(4):
                self.core(a).wait_send()
        self.freed = True

    def copy(self, n):
        p, buf, a = self.place, self.buf, n % 4
        x, y, low, high = p.x, p.y, self.low, self.high
        if n >= 16:
            src, dst, r = (
                lambda: (buf.at[p.shard(1), :, y, x], self.got4.at[0], 1),
                lambda: (buf.at[p.shard(3), :, y, x], self.got4.at[1], 1),
                lambda: (buf.at[p.shard(2), :, y, x], self.got5, 2),
            )[n - 16]()
            device = p.device(0, r)
        else:
            src, dst, device = (
                lambda: (buf.at[a, :, :, 1 - x, low], self.got2.at[0, a], p.device(X)),
                lambda: (buf.at[a, :, 1 - y, :, high], self.got2.at[1, a], p.device(Y)),
                lambda: (buf.at[a, :, 1 - y, x, low], self.got3.at[0, a], p.device(Y)),
                lambda: (buf.at[a, :, y, 1 - x, high], self.got3.at[1, a], p.device(X)),
            )[n // 4]()
        return remote(src, dst, self.sends.at[4 + n], self.recvs.at[4 + n], device)

    def took(self, n):
        self.copy(n).wait_recv()
        self.copy(n).wait_send()

    def add(self, index, extra):
        self.buf[index] = (self.buf[index].astype(F32) + extra.astype(F32)).astype(BF16)

    def one(self, a):
        self.copy(a).start()
        self.copy(4 + a).start()

    def two(self):
        p = self.place
        for a in range(4):
            self.took(a)
            for b in range(2):
                self.add((a, 0, b, p.x, self.low), self.got2[0, a, 0, b])
            self.copy(8 + a).start()
            self.took(4 + a)
            for b in range(2):
                self.add((a, 0, p.y, b, self.high), self.got2[1, a, 0, b])
            self.copy(12 + a).start()

    def three(self):
        p = self.place
        for a in range(4):
            for n, part in ((0, self.low), (1, self.high)):
                self.took(8 + 4 * n + a)
                self.add((a, 0, p.y, p.x, part), self.got3[n, a, 0])
        self.copy(16).start()
        self.copy(17).start()

    def four(self):
        p = self.place
        for n, shard in ((0, p.t), (1, p.shard(2))):
            self.took(16 + n)
            self.add((shard, 0, p.y, p.x), self.got4[n, 0])
        self.copy(18).start()

    def five(self):
        p = self.place
        self.away_free()
        self.took(18)
        self.add((p.t, 0, p.y, p.x), self.got5[0])
        self.keep.start()
        self.spread[0]()

    def stages(self):
        return [self.two, self.three, self.four, self.five] + self.spread[1:] + [self.keep.wait]


def attend_back(a, cap, qkv, dh):
    rows, cols = qkv.shape[2], qkv.shape[3]
    pairs = cols // WIDE
    scale = HEAD_DIM ** (-0.5)

    def step(i, carry):
        seq, pair = lax.div(i, jnp.int32(pairs)), lax.rem(i, jnp.int32(pairs))
        rs = pl.ds(pl.multiple_of(seq * cap, cap), cap)
        cs = pl.ds(pl.multiple_of(pair * WIDE, WIDE), WIDE)
        q, k, v, g = qkv[a, 0, rs, cs], qkv[a, 1, rs, cs], qkv[a, 2, rs, cs], dh[a, rs, cs]
        first = lax.broadcasted_iota(jnp.int32, (cap, WIDE), 1) < HEAD_DIM
        causal = lax.broadcasted_iota(jnp.int32, (cap, cap), 0) >= lax.broadcasted_iota(jnp.int32, (cap, cap), 1)
        dq = dk = dv = None
        for mine in (first, jnp.logical_not(first)):
            zero = jnp.zeros_like(q)
            qh, kh, gh = jnp.where(mine, q, zero), jnp.where(mine, k, zero), jnp.where(mine, g, zero)
            scores = jnp.where(causal, dot_nt(qh, k) * scale, -1e30)
            exps = jnp.exp(scores - jnp.max(scores, axis=1, keepdims=True))
            probs = exps / jnp.sum(exps, axis=1, keepdims=True)
            d_probs = dot_nt(gh, v)
            lean = jnp.sum(probs * d_probs, axis=1, keepdims=True)
            d_scores = (probs * (d_probs - lean)).astype(BF16)
            parts = (dot(d_scores, kh), dot_tn(d_scores, qh), dot_tn(probs.astype(BF16), gh))
            dq, dk, dv = parts if dq is None else (dq + parts[0], dk + parts[1], dv + parts[2])
        qkv[a, 0, rs, cs] = (dq * scale).astype(BF16)
        qkv[a, 1, rs, cs] = (dk * scale).astype(BF16)
        qkv[a, 2, rs, cs] = dv.astype(BF16)
        return carry

    lax.fori_loop(0, rows // cap * pairs, step, 0)


LAST_STAGES = [
    (1, 0), (2, 1), (3, 3), (1, 1), (2, 2), (0, 0), (3, 4),
    (2, 3), (1, 2), (0, 1), (3, 5), (2, 4), (1, 3), (0, 2),
    (3, 6), (2, 5), (1, 4), (0, 3), (2, 6), (1, 5), (0, 4),
    (1, 6), (0, 5), (0, 6), (3, 7), (2, 7), (1, 7), (0, 7),
]


def backward_kernel(cap, *refs):
    out_rows, vector = refs[0:2]
    saved = refs[2:11]
    weights = refs[11:15]
    got_out, got_in, small = refs[15:18]
    results = refs[18:22]
    pk, gr, n1, qkv, ho, at, hid, gp, stats = refs[22:31]
    vec, slots, dm, dn, n2, pre, spare, own_out = refs[31:39]
    bufs, got2, got3, got4, got5 = refs[39:43], refs[43:47], refs[47:51], refs[51:55], refs[55:59]
    sums, heard, pieces = refs[59:62]
    sends, recvs, row_send, row_recv, in_sem, slot_sem, keep_sem, s_send, s_recv = refs[62:]
    place = Place()
    rows, width = dm.shape
    cols = pk.shape[2]
    c, t = place.c, place.t
    loads = [
        pltpu.make_async_copy(src, dst, in_sem.at[i])
        for i, (src, dst) in enumerate(zip(saved[:9], [stats, gr, hid, gp, pk, at, ho, qkv, n1]))
    ]
    loads.append(pltpu.make_async_copy(out_rows.at[t], got_out.at[t], in_sem.at[9]))
    loads.append(pltpu.make_async_copy(vector, vec, in_sem.at[10]))
    for copy in loads:
        copy.start()
    wq, wo, wu, wd = weights

    def slot_copies(i):
        slot = slots.at[i % 2]
        if i < 8:
            src = (wd if i < 4 else wu).at[i % 4]
            return [pltpu.make_async_copy(src, slot, slot_sem.at[i % 2, 0])]
        if i == 8:
            return [pltpu.make_async_copy(wo, slot, slot_sem.at[0, 0])]
        return [
            pltpu.make_async_copy(
                wq.at[i - 9, k], slot.at[:, pl.ds(k * cols, cols)], slot_sem.at[i % 2, k]
            )
            for k in range(3)
        ]

    def slot_start(i):
        if i < 13:
            for copy in slot_copies(i):
                copy.start()

    def slot_ready(i):
        for copy in slot_copies(i):
            copy.wait()

    slot_start(0)
    slot_start(1)
    place.greet()
    rows_one = exchange_rows(place, out_rows, got_out, row_send.at[0], row_recv.at[0])
    rows_two = exchange_rows(place, pk, got_in, row_send.at[1], row_recv.at[1])
    rows_one[0]()

    aways = [
        spare.at[:, :, :, :, :, pl.ds(0, 3 * cols)],
        spare.at[:, :, :, :, pl.ds(0, bufs[1].shape[4]), :],
        hid,
        spare,
    ]
    chain = [
        Sum(
            place, aways[w], bufs[w], got2[w], got3[w], got4[w], got5[w], results[w], sends.at[w], recvs.at[w], keep_sem.at[w]
        )
        for w in range(4)
    ]
    q, o, u, d = chain
    for i in (0, 1):
        loads[i].wait()

    def d_update(rs):
        dm[rs, :] = (stats[rs, 1:2] * joined(gr, rs)).astype(BF16)

    chunks(rows, 64, d_update)
    loads[2].wait()

    def send_half(one, a, left, right, total):
        def put(cs, value):
            size = value.shape[1]
            one.away[a, 0, :, :, :, cs] = value.astype(BF16).reshape(2, 2, -1, size)

        outer(left, right, total, put, block=256 if total % 512 else 512)
        one.core(a).start()

    def keep_half(one, a, left, right, total):
        one.core(a).wait_recv()

        def put(cs, value):
            size = value.shape[1]
            mine = one.buf[a, 0, :, :, :, cs].astype(F32).reshape(-1, size)
            one.buf[a, 0, :, :, :, cs] = (mine + value).astype(BF16).reshape(2, 2, -1, size)

        outer(left, right, total, put, block=256 if total % 512 else 512)

    def hid_half(a, parity):
        return half_blocks(lambda ls: hid[a, 0, :, :, :, ls].reshape(rows, WIDE), 8, parity)

    for a in range(4):
        send_half(d, a, hid_half(a, 1 - c), lambda cs: dm[:, cs], width)
    for a in range(4):
        keep_half(d, a, hid_half(a, c), lambda cs: dm[:, cs], width)
        d.one(a)
    loads[3].wait()
    for a in range(4):
        slot_ready(a)

        def d_hidden(i, carry, a=a):
            cs = pl.ds(pl.multiple_of(i * 256, 256), 256)
            pre[...] = dot_nt(dm[...], slots[a % 2, cs, :])

            def bend(rs):
                gp[a, rs, cs] = (pre[rs, :] * gp[a, rs, cs].astype(F32)).astype(BF16)

            chunks(rows, 64, bend)
            return carry

        lax.fori_loop(0, gp.shape[2] // 256, d_hidden, 0)
        slot_start(a + 2)
    loads[4].wait()
    loads[5].wait()
    loads[10].wait()

    def norm_two(rs):
        at[rs, :] += joined(pk, rs)
        n2[rs, :] = (at[rs, :] * stats[rs, 2:3] * vec[1:2, :]).astype(BF16)

    chunks(rows, 64, norm_two)
    left = half_blocks(lambda ls: n2[:, ls], 8, 1 - c)
    for a in range(4):
        send_half(u, a, left, lambda cs, a=a: gp[a, :, cs], gp.shape[2])
    left = half_blocks(lambda ls: n2[:, ls], 8, c)
    for a in range(4):
        keep_half(u, a, left, lambda cs, a=a: gp[a, :, cs], gp.shape[2])
        u.one(a)
    for a in range(4):
        slot_ready(4 + a)

        def d_normed(i, carry, a=a):
            cs = pl.ds(pl.multiple_of(i * 256, 256), 256)
            part = dot_nt(gp[a], slots[a % 2, cs, :])
            if a == 0:
                dn[:, cs] = part
            else:
                dn[:, cs] += part
            return carry

        lax.fori_loop(0, width // 256, d_normed, 0)
        slot_start(a + 6)
        if a == 2:
            d.two()

    sums[0] = jnp.zeros_like(sums[0])

    def norm_two_back(rs):
        mid, inv, grad = at[rs, :], stats[rs, 2:3], dn[rs, :]
        sums[0, 1:2, :] += jnp.sum(grad * mid * inv, axis=0, keepdims=True)
        grad = grad * vec[1:2, :]
        lean = jnp.sum(grad * mid, axis=1, keepdims=True)
        d_mid = inv * grad - mid * (inv * inv * inv * lean / width)
        at[rs, :] = d_mid
        dm[rs, :] = (stats[rs, 1:2] * joined(gr, rs) + d_mid).astype(BF16)

    chunks(rows, 64, norm_two_back)

    d.away_free()
    loads[6].wait()
    slot_ready(8)
    unit = bufs[1].shape[4]
    for a in range(4):
        turned = jnp.transpose(ho[a])

        def grad_out(i, carry, a=a, turned=turned):
            cs = pl.ds(pl.multiple_of(i * 256, 256), 256)
            pre[pl.ds(0, cols), :] = dot(turned, dm[:, cs])
            for b in range(4):
                away = pl.ds(pl.multiple_of((2 * b + 1 - c) * unit, unit), unit)
                mine = pl.ds(pl.multiple_of((2 * b + c) * unit, unit), unit)
                o.away[a, 0, b // 2, b % 2, :, cs] = pre[away, :].astype(BF16)
                own_out[a, 0, b // 2, b % 2, :, cs] = pre[mine, :].astype(BF16)
            return carry

        lax.fori_loop(0, width // 256, grad_out, 0)
        o.core(a).start()
        ho[a] = dot_nt(dm[...], slots[0, pl.ds(a * cols, cols), :]).astype(BF16)
    slot_start(10)
    for a in range(4):
        o.core(a).wait_recv()
        for b in range(4):
            o.add((a, 0, b // 2, b % 2), own_out[a, 0, b // 2, b % 2])
        o.one(a)
    loads[7].wait()
    for a in range(4):
        attend_back(a, cap, qkv, ho)
        if a == 1:
            d.three()
        if a == 2:
            u.two()
    d.four()
    o.away_free()
    loads[8].wait()

    def proj(a):
        return lambda cs: qkv[a, lax.div(cs.start, jnp.int32(cols))]

    for a in range(4):
        slot_ready(9 + a)

        def d_normed(i, carry, a=a):
            cs = pl.ds(pl.multiple_of(i * 256, 256), 256)
            part = dot_nt(qkv[a, 0], slots[(9 + a) % 2, cs, pl.ds(0, cols)])
            for k in (1, 2):
                part += dot_nt(qkv[a, k], slots[(9 + a) % 2, cs, pl.ds(k * cols, cols)])
            if a == 0:
                dn[:, cs] = part
            else:
                dn[:, cs] += part
            return carry

        lax.fori_loop(0, width // 256, d_normed, 0)
        slot_start(a + 11)

    def norm_one_back(rs):
        x, grows, grad = joined(pk, rs), joined(gr, rs), dn[rs, :]
        inv, d_logit = stats[rs, 0:1], stats[rs, 3:4]
        sums[0, 0:1, :] += jnp.sum(grad * x * inv, axis=0, keepdims=True)
        sums[0, 2:3, :] += jnp.sum(d_logit * x, axis=0, keepdims=True)
        grad = grad * vec[0:1, :]
        lean = jnp.sum(grad * x, axis=1, keepdims=True)
        result = grows + at[rs, :] + inv * grad - x * (inv * inv * inv * lean / width) + d_logit * vec[2:3, :]
        for a in range(4):
            pk[a, rs, :] = result[:, a * cols : (a + 1) * cols].astype(BF16)

    chunks(rows, 64, norm_one_back)
    rows_two[0]()
    own_in = pltpu.make_async_copy(pk.at[t], got_in.at[t], in_sem.at[11])
    own_in.start()
    left = half_blocks(lambda ls: n1[:, ls], 8, 1 - c)
    for a in range(4):
        send_half(q, a, left, proj(a), 3 * cols)
    left = half_blocks(lambda ls: n1[:, ls], 8, c)
    for a in range(4):
        keep_half(q, a, left, proj(a), 3 * cols)
        q.one(a)

    def step(n):
        bit = (CORE, X, Y)[n]
        return remote(sums.at[n], heard.at[n], s_send.at[n], s_recv.at[n], place.device(bit))

    def piece(r):
        lanes = pl.ds(pl.multiple_of(place.shard(r) * cols, cols), cols)
        return remote(sums.at[3, :, lanes], pieces.at[r - 1], s_send.at[2 + r], s_recv.at[2 + r], place.device(0, r))

    def after(tick):
        if tick < 3:
            if tick == 0:
                step(0).start()
            else:
                step(tick - 1).wait_recv()
                sums[tick] = sums[tick - 1] + heard[tick - 1]
                step(tick).start()
        if tick == 3:
            step(2).wait_recv()
            sums[3] = sums[2] + heard[2]
            for r in (1, 2, 3):
                piece(r).start()
        if tick == 4:
            for r in (1, 2, 3):
                piece(r).wait_recv()
            lanes = pl.ds(pl.multiple_of(t * cols, cols), cols)
            vec[:, pl.ds(0, cols)] = sums[3, :, lanes] + pieces[0] + pieces[1] + pieces[2]
            out_small.start()

    out_small = pltpu.make_async_copy(vec.at[:, pl.ds(0, cols)], small, in_sem.at[12])
    todo = [one.stages() for one in (q, o, u, d)]
    for tick, (one, stage) in enumerate(LAST_STAGES):
        todo[one][stage]()
        if tick % 2 == 0:
            after(tick // 2)
    for n in range(3):
        step(n).wait_send()
    for r in (1, 2, 3):
        piece(r).wait_send()
    rows_one[1]()
    rows_two[1]()
    loads[9].wait()
    own_in.wait()
    out_small.wait()


def backward(cap, out_rows, vector, saved, weights):
    _, rows, cols = out_rows.shape
    width = 4 * cols
    inner = weights[3].shape[1]
    slices = [(128, 3 * cols), (cols // GROUP, width), (width // GROUP, inner), (inner // GROUP, width)]
    dma = pltpu.SemaphoreType.DMA
    vmem = pltpu.VMEM
    scratch = [
        vmem((4, rows, cols), BF16),
        vmem((4, rows, cols), BF16),
        vmem((rows, width), BF16),
        vmem((4, 3, rows, cols), BF16),
        vmem((4, rows, cols), BF16),
        vmem((rows, width), F32),
        vmem((4, 1, 2, 2, rows // 4, inner), BF16),
        vmem((4, rows, inner), BF16),
        vmem((rows, WIDE), F32),
        vmem((8, width), F32),
        vmem((2, width, width), BF16),
        vmem((rows, width), BF16),
        vmem((rows, width), F32),
        vmem((rows, width), BF16),
        vmem((rows, 256), F32),
        vmem((4, 1, 2, 2, 128, width), BF16),
        vmem((4, 1, 2, 2) + slices[1], BF16),
    ]
    scratch += [vmem((4, 1, 2, 2) + s, BF16) for s in slices]
    scratch += [vmem((2, 4, 1, 2, s[0] // 2, s[1]), BF16) for s in slices]
    scratch += [vmem((2, 4, 1, s[0] // 2, s[1]), BF16) for s in slices]
    scratch += [vmem((2, 1) + s, BF16) for s in slices]
    scratch += [vmem((1,) + s, BF16) for s in slices]
    scratch += [
        vmem((4, 8, width), F32),
        vmem((3, 8, width), F32),
        vmem((3, 8, cols), F32),
        dma((4, 31)),
        dma((4, 31)),
        dma((2, 3)),
        dma((2, 3)),
        dma((13,)),
        dma((2, 3)),
        dma((4,)),
        dma((6,)),
        dma((6,)),
    ]
    return pl.pallas_call(
        functools.partial(backward_kernel, cap),
        in_specs=[ANY] * (2 + len(saved) + 4),
        out_specs=[ANY] * 7,
        out_shape=[jax.ShapeDtypeStruct(out_rows.shape, BF16)] * 2
        + [jax.ShapeDtypeStruct((8, cols), F32)]
        + [jax.ShapeDtypeStruct((1, 8) + s, BF16) for s in slices],
        scratch_shapes=scratch,
        compiler_params=pltpu.CompilerParams(
            collective_id=2, has_side_effects=True, vmem_limit_bytes=62 * 1024 * 1024
        ),
        name="backward",
    )(out_rows, vector, *saved, *weights)


def body(all_dp, n_t, block_input, routes, out_grad, w_qkv, w_out, w_up, w_down, gain_attn, gain_mlp, w_router):
    seqs, length, cols = block_input.shape
    cap = routes.shape[1]
    width = cols * n_t
    own = seqs // n_t
    rows = own * cap
    heads = cols // HEAD_DIM
    outer_bits = [1 << i for i in range(3, all_dp.bit_length() - 1)]

    def send(value, mask_dp, mask_t):
        pairs = [
            (d * n_t + s, (d ^ mask_dp) * n_t + (s ^ mask_t)) for d in range(all_dp) for s in range(n_t)
        ]
        return lax.ppermute(value, ("dp", "tensor"), pairs)

    vector = jnp.concatenate([gain_attn[None], gain_mlp[None], w_router[None], jnp.zeros((5, cols), F32)])
    local = [
        w_qkv.transpose(1, 0, 2).reshape(3, GROUP, width // GROUP, cols),
        w_out.reshape(1, GROUP, cols // GROUP, width),
        w_up.reshape(1, GROUP, width // GROUP, w_up.shape[1]),
        w_down.reshape(1, GROUP, w_down.shape[0] // GROUP, width),
    ]
    wq, wo, wu, wd, picked, grad_rows, normed_one, qkv, head_out, attn_out, hidden, bend, out_rows, stats, vectors = forward(
        [block_input, out_grad], routes, vector, local
    )
    vectors = vectors.transpose(1, 0, 2).reshape(8, width)
    got_out, got_in, sums, s_qkv, s_out, s_up, s_down = backward(
        cap,
        out_rows,
        vectors,
        [
            stats,
            grad_rows,
            hidden.reshape(n_t, 1, 2, 2, rows // 4, -1),
            bend,
            picked,
            attn_out,
            head_out,
            qkv,
            normed_one,
        ],
        [
            wq.reshape(n_t, 3, width, cols),
            wo.reshape(n_t * cols, width),
            wu.reshape(n_t, width, -1),
            wd.reshape(n_t, -1, width),
        ],
    )
    layer_out, input_grad, g_qkv, g_out, g_up, g_down = write_results(
        routes,
        [block_input, out_grad],
        [got_out.reshape(seqs, cap, cols), got_in.reshape(seqs, cap, cols)],
        [
            s_qkv.reshape(width, 3 * cols),
            s_out.reshape(w_out.shape),
            s_up.reshape(w_up.shape),
            s_down.reshape(w_down.shape),
        ],
    )
    for bit in outer_bits:
        sums = sums + send(sums, bit, 0)

    def settle(value):
        for bit in outer_bits:
            value = value + send(value, bit, 0)
        return value

    g_qkv, g_out, g_up, g_down = settle(g_qkv).transpose(1, 0, 2), settle(g_out), settle(g_up), settle(g_down)
    return (layer_out, input_grad, g_qkv, g_out, g_up, g_down, sums[0], sums[1], sums[2])


def solution(mesh):
    placed = (
        P("dp", None, "tensor"),
        P("dp", None),
        P("dp", None, "tensor"),
        P(None, None, "tensor"),
        P("tensor", None),
        P(None, "tensor"),
        P("tensor", None),
        P("tensor"),
        P("tensor"),
        P("tensor"),
    )
    return jax.shard_map(
        functools.partial(body, mesh.shape["dp"], mesh.shape["tensor"]),
        mesh=mesh,
        in_specs=placed,
        out_specs=(
            P("dp", None, "tensor"),
            P("dp", None, "tensor"),
            P(None, None, "tensor"),
            P("tensor", None),
            P(None, "tensor"),
            P("tensor", None),
            P("tensor"),
            P("tensor"),
            P("tensor"),
        ),
        check_vma=False,
    )
```
